128 devices in a mesh: dev: 128 (over z, y, x, core).
Axes of the slice: x: 4, y: 4, z: 4, core: 2. Of those that a mesh axis runs over, the one named last changes fastest.
Arguments:
- params: float32 [59, 524288], P(None, 'dev'), as said below
- adam_m: float32 [59, 524288], P(None, 'dev'), may hold values from -3 to 3
- adam_v: float32 [59, 524288], P(None, 'dev'), may hold values from 1e-05 to 0.001
- target: float32 [3, 131072], P(None, 'dev'), may hold values from 0 to 1
- req_rows: int32 [128, 5120], P('dev'), may hold values from 0 to 4095, as said below
- tile_list: int32 [128, 5120], P('dev'), may hold values from 0 to 5119
- tile_len: int32 [512], P('dev'), may hold values from 1 to 1280, 409600 in all
- tile_order: int32 [512, 1280], P('dev'), may hold values from 0 to 1279, as said below
- tile_pos: int32 [512], P('dev'), may hold values from 0 to 511, as said below
- bg_ids: int32 [128], replicated, may hold values from 0 to 524287
Outputs:
- new_params: float32 [59, 524288], P(None, 'dev')
- new_m: float32 [59, 524288], P(None, 'dev')
- new_v: float32 [59, 524288], P(None, 'dev')
The draws below stay inside these ranges and needn't reach their ends.
Inputs may be any that keep to these rules, and one draw needn't show every extreme that they name: `params`: device o owns region o mod 64 (tiles 2 * 4 (o mod 64) onward, in row-major order) in depth layer o // 64: its Gaussians' centers project into that region, row 2 (depth) lies in 2 to 4 in layer 0 and in 4 to 6 in layer 1; row 6 (quaternion w) lies in 0.5 to 1.5. `req_rows`: within one window's 512 slots of a device the rows are distinct. `tile_order`: each row is a permutation that orders the tile's entries by increasing depth of their Gaussians. `tile_pos`: a permutation; device d renders 4 of the 8 tiles of region d mod 64.
All inputs are finite; a program needn't handle non-finite values. No bound on the sum of `tile_len` on one device may be relied on, other than what follows from the above.
Results may differ from the reference program's by a relative error of at most 0.0003.
Values sent between devices are 32-bit elements; how exact they have to be, the bound alone decides.
A program may use at most 128 MiB of HBM per device.

```python
import math
import jax
import jax.numpy as jnp
import numpy as np
from jax import lax

PARAMS = 59
TILES_X = 32
LIST = 1280
NBG = 128
NEAR = 10
CAP = 512
G_DEV = 4096
TILES_DEV = 4
G_TOTAL = 524288
TILES_TOTAL = 512
TILES_Y = 16
PIXELS = 131072
ROW_REGIONS = 4
N_DEV = 128


def depth_ranks(key):
    base = jax.random.fold_in(key, 9002)
    keys = jax.random.split(base, N_DEV)
    ranks = jax.vmap(lambda sub_key: jax.random.permutation(sub_key, G_DEV))(keys)
    return ranks.astype(jnp.int32)


def layout(key):
    base = jax.random.fold_in(key, 9001)
    keys = jax.random.split(base, 3)
    regions = N_DEV // 2
    row_regions = TILES_X // (2 * TILES_DEV)
    region_lines = regions // row_regions
    slots = NEAR * CAP
    bins = G_DEV // CAP
    jitter = jax.random.randint(keys[0], (N_DEV, slots), 0, bins)
    offset = jnp.repeat(jax.random.randint(keys[1], (N_DEV, NEAR), 0, G_DEV), CAP, axis=1)
    within = jnp.arange(slots, dtype=jnp.int32) % CAP
    requests = ((within[None, :] * bins + jitter + offset) % G_DEV).astype(jnp.int32)
    device = jnp.arange(N_DEV, dtype=jnp.int32)
    region = device % regions
    column = region % row_regions
    line = region // row_regions
    valid_five = jnp.stack([column >= 0, column + 1 < row_regions, column >= 1, line + 1 < region_lines, line >= 1], axis=1)
    valid_all = jnp.concatenate([valid_five, valid_five], axis=1)
    slot_valid = jnp.repeat(valid_all, CAP, axis=1)
    index = jnp.arange(slots, dtype=jnp.int32)
    scores = jax.random.randint(keys[2], (N_DEV, TILES_DEV, slots), 0, 65536) * slots + index
    scores = jnp.where(slot_valid[:, None, :], scores, -1 - index)
    chosen = jnp.argsort(-scores, axis=-1)[:, :, :LIST].astype(jnp.int32)
    tile_list = chosen.reshape(N_DEV, TILES_DEV * LIST)
    step_table = jnp.array([0, 1, -1, row_regions, -row_regions], dtype=jnp.int32)
    window = chosen // CAP
    shift_by = step_table[window % 5] + window // 5 * regions
    owner = (device[:, None, None] + shift_by) % N_DEV
    row = requests[device[:, None, None], chosen]
    ranks = depth_ranks(key)
    depth_key = owner // regions * (G_DEV * regions) + ranks[owner, row] * regions + owner % regions
    order = jnp.argsort(depth_key, axis=-1).astype(jnp.int32)
    return (requests, tile_list, order.reshape(TILES_TOTAL, LIST))


def draw_req_rows(key, part):
    return layout(key)[0]


def draw_tile_list(key, part):
    return layout(key)[1]


def draw_tile_order(key, part):
    return layout(key)[2]


def draw_tile_pos(key, part):
    base = jax.random.fold_in(key, 9003)
    regions = N_DEV // 2
    span = 2 * TILES_DEV
    scores = jax.random.randint(base, (regions, span), 0, 65536) * span + jnp.arange(span, dtype=jnp.int32)
    perm = jnp.argsort(scores, axis=1).astype(jnp.int32)
    slot = jnp.arange(TILES_TOTAL, dtype=jnp.int32)
    device = slot // TILES_DEV
    within = slot % TILES_DEV
    layer = device // regions
    region = device % regions
    return (region * span + perm[region, layer * TILES_DEV + within]).astype(jnp.int32)


def draw_params(key, part):
    keys = jax.random.split(key, 9)
    count = G_TOTAL
    regions = N_DEV // 2
    row_regions = TILES_X // (2 * TILES_DEV)
    width = 16.0 * TILES_X
    height = 16.0 * TILES_Y
    strip = 32.0 * TILES_DEV
    column_id = jnp.arange(count, dtype=jnp.int32)
    owner = column_id // G_DEV
    layer = owner // regions
    region = owner % regions
    rank = depth_ranks(key).reshape(-1)
    depth_key = (rank * regions + region).astype(jnp.float32)
    depth = 2.0 + 2.0 * layer.astype(jnp.float32) + 2.0 * (depth_key + 0.5) / float(G_DEV * regions)
    screen_u = (region % row_regions).astype(jnp.float32) * strip + jax.random.uniform(keys[1], (count,), jnp.float32, 0.0, strip)
    screen_v = (region // row_regions).astype(jnp.float32) * 16.0 + jax.random.uniform(keys[2], (count,), jnp.float32, 0.0, 16.0)
    pos_x = (screen_u - 0.5 * width) * depth / 512.0
    pos_y = (screen_v - 0.5 * height) * depth / 512.0
    log_scales = jnp.log(depth / 512.0)[None, :] + jax.random.uniform(keys[3], (3, count), jnp.float32, math.log(24.0), math.log(160.0))
    quat_w = jax.random.uniform(keys[4], (1, count), jnp.float32, 0.5, 1.5)
    quat_rest = 0.5 * jax.random.normal(keys[5], (3, count), jnp.float32)
    logit = jax.random.uniform(keys[6], (1, count), jnp.float32, -6.0, -3.5)
    base_color = jax.random.normal(keys[7], (3, count), jnp.float32)
    higher = 0.3 * jax.random.normal(keys[8], (45, count), jnp.float32)
    return jnp.concatenate([pos_x[None, :], pos_y[None, :], depth[None, :], log_scales, quat_w, quat_rest, logit, base_color, higher], axis=0)


def place_ends(values, stream_key, smallest, largest):
    spot = [jax.random.randint(jax.random.fold_in(stream_key, axis), (), 0, length) for axis, length in enumerate(values.shape)]
    longest = values.shape.index(max(values.shape))
    beside = spot[:longest] + [(spot[longest] + 1) % values.shape[longest]] + spot[longest + 1:]
    return values.at[tuple(spot)].set(smallest).at[tuple(beside)].set(largest)


def steps_of(key, extent, cuts, smallest, top_value):
    loudness, own = 1.0, jax.random.fold_in(key, 6)
    for axis_at, shards_of in cuts:
        steps = jnp.exp(jax.random.uniform(jax.random.fold_in(own, axis_at), (shards_of,), jnp.float32, smallest / len(cuts), top_value / len(cuts)))
        loudness = loudness * jnp.repeat(steps, extent[axis_at] // shards_of).reshape([-1 if axis == axis_at else 1 for axis in range(len(extent))])
    return loudness


def length_profile(amount, total, bound, slope):
    loads = [(1 << 20) // math.isqrt(grade ** slope) + 1 for grade in range(2, amount + 1)]
    spare, given = total - bound - (amount - 1), [1] * (amount - 1)
    while spare > 0:
        movable = [i for i in range(amount - 1) if given[i] < bound]
        pool, budget = sum([loads[i] for i in movable]), spare
        for i in movable:
            extra = min(bound - given[i], max(1, budget * loads[i] // pool), spare)
            given[i] = given[i] + extra
            spare = spare - extra
    return np.array([bound] + given)


def ragged(rng, amount, total, reach, lean):
    if amount == 2:
        one = jax.random.randint(rng, (), max(1, total - reach), min(reach, total - 1) + 1)
        return jnp.stack([one, total - one])
    lengths = jnp.asarray(length_profile(amount, total, reach, lean), jnp.int32)
    pairs = (amount - 1) // 2
    source_of, sink = lengths[1:1 + 2 * pairs:2], lengths[2:2 + 2 * pairs:2]
    room = jnp.minimum(source_of - 1, reach - sink)
    shifted = jax.random.randint(jax.random.fold_in(rng, 1), (pairs,), 0, 1 << 20) % (room + 1)
    lengths = lengths.at[1:1 + 2 * pairs:2].set(source_of - shifted).at[2:2 + 2 * pairs:2].set(sink + shifted)
    return lengths[jax.random.permutation(jax.random.fold_in(rng, 2), amount)]


def gaussian(own_key, extent, scale, bound, shards=(), kind=jnp.bfloat16):
    level = steps_of(own_key, extent, shards, -0.22, 0.18) if shards else 1.0
    values = jax.random.normal(own_key, extent, jnp.float32) * scale * level
    return jnp.minimum(jnp.maximum(values, -bound), bound).astype(kind)


def setup_inputs(seed: int = 0) -> dict:
    key_list = jax.random.split(jax.random.key(seed), 11)
    params = draw_params(jax.random.fold_in(key_list[10], 71), 0)
    adam_m = gaussian(key_list[1], (PARAMS, G_TOTAL), 0.2, 3.0, ((1, 128),), jnp.float32)
    adam_v = jnp.clip(jnp.exp(math.log(0.001) - 4.6051703 * jax.random.uniform(key_list[2], (PARAMS, G_TOTAL), jnp.float32) ** steps_of(key_list[2], (PARAMS, G_TOTAL), ((1, 128),), -0.2, 0.2)), 9.999999747378752e-06, 0.001)
    target = jnp.clip(1.0 * jax.random.uniform(key_list[3], (3, PIXELS), jnp.float32) ** steps_of(key_list[3], (3, PIXELS), ((1, 128),), -0.2, 0.2), 0.0, 1.0)
    req_rows = draw_req_rows(jax.random.fold_in(key_list[10], 71), 0)
    tile_list = draw_tile_list(jax.random.fold_in(key_list[10], 71), 0)
    tile_len = ragged(key_list[6], TILES_TOTAL, TILES_TOTAL * LIST * 5 // 8, LIST, 2).astype(jnp.int32)
    tile_order = draw_tile_order(jax.random.fold_in(key_list[10], 71), 0)
    tile_pos = draw_tile_pos(jax.random.fold_in(key_list[10], 71), 0)
    bg_ids = place_ends(jax.random.randint(key_list[9], (NBG,), 0, G_TOTAL), jax.random.fold_in(key_list[9], 1), 0, G_TOTAL - 1).astype(jnp.int32)
    return {"params": params, "adam_m": adam_m, "adam_v": adam_v, "target": target, "req_rows": req_rows, "tile_list": tile_list, "tile_len": tile_len, "tile_order": tile_order, "tile_pos": tile_pos, "bg_ids": bg_ids}


FOCAL = 512.0
HIGH = lax.Precision.HIGHEST
BIAS_ONE = 1.0 - 0.9 ** 10
BIAS_TWO = 1.0 - 0.999 ** 10

def harmonics(dir_x, dir_y, dir_z):
    sq_x = dir_x * dir_x
    sq_y = dir_y * dir_y
    sq_z = dir_z * dir_z
    return jnp.stack([0.28209479177387814 + 0.0 * dir_x, -0.4886025119029199 * dir_y, 0.4886025119029199 * dir_z, -0.4886025119029199 * dir_x, 1.0925484305920792 * dir_x * dir_y, -1.0925484305920792 * dir_y * dir_z, 0.31539156525252005 * (2.0 * sq_z - sq_x - sq_y), -1.0925484305920792 * dir_x * dir_z, 0.5462742152960396 * (sq_x - sq_y), -0.5900435899266435 * dir_y * (3.0 * sq_x - sq_y), 2.890611442640554 * dir_x * dir_y * dir_z, -0.4570457994644658 * dir_y * (4.0 * sq_z - sq_x - sq_y), 0.3731763325901154 * dir_z * (2.0 * sq_z - 3.0 * sq_x - 3.0 * sq_y), -0.4570457994644658 * dir_x * (4.0 * sq_z - sq_x - sq_y), 1.445305721320277 * dir_z * (sq_x - sq_y), -0.5900435899266435 * dir_x * (sq_x - 3.0 * sq_y)])

def project(rows, center_y):
    pos_x, pos_y, depth = (rows[0], rows[1], rows[2])
    stretches = (jnp.exp(rows[3]), jnp.exp(rows[4]), jnp.exp(rows[5]))
    quat_norm = jnp.sqrt(rows[6] * rows[6] + rows[7] * rows[7] + rows[8] * rows[8] + rows[9] * rows[9])
    quat_w = rows[6] / quat_norm
    quat_x = rows[7] / quat_norm
    quat_y = rows[8] / quat_norm
    quat_z = rows[9] / quat_norm
    rotation = ((1.0 - 2.0 * (quat_y * quat_y + quat_z * quat_z), 2.0 * (quat_x * quat_y - quat_w * quat_z), 2.0 * (quat_x * quat_z + quat_w * quat_y)), (2.0 * (quat_x * quat_y + quat_w * quat_z), 1.0 - 2.0 * (quat_x * quat_x + quat_z * quat_z), 2.0 * (quat_y * quat_z - quat_w * quat_x)), (2.0 * (quat_x * quat_z - quat_w * quat_y), 2.0 * (quat_y * quat_z + quat_w * quat_x), 1.0 - 2.0 * (quat_x * quat_x + quat_y * quat_y)))
    inv_depth = 1.0 / depth
    focal_z = FOCAL * inv_depth
    slope_x = pos_x * inv_depth
    slope_y = pos_y * inv_depth
    cov_a = 0.3
    cov_b = 0.0
    cov_c = 0.3
    for column in range(3):
        axis_x = rotation[0][column] * stretches[column]
        axis_y = rotation[1][column] * stretches[column]
        axis_z = rotation[2][column] * stretches[column]
        image_u = focal_z * (axis_x - slope_x * axis_z)
        image_v = focal_z * (axis_y - slope_y * axis_z)
        cov_a = cov_a + image_u * image_u
        cov_b = cov_b + image_u * image_v
        cov_c = cov_c + image_v * image_v
    determ = cov_a * cov_c - cov_b * cov_b
    center_u = FOCAL * slope_x + 8.0 * TILES_X
    center_v = FOCAL * slope_y + center_y
    opacity = jax.nn.sigmoid(rows[10])
    distance = jnp.sqrt(pos_x * pos_x + pos_y * pos_y + depth * depth)
    basis = harmonics(pos_x / distance, pos_y / distance, depth / distance)
    coeffs = rows[11:].reshape(16, 3, rows.shape[1])
    color = lax.optimization_barrier(jnp.sum(basis[:, None, :] * coeffs, axis=0)) + 0.5
    head = jnp.stack([center_u, center_v, cov_c / determ, -cov_b / determ, cov_a / determ, opacity])
    return jnp.concatenate([head, color], axis=0)

def tile_loss(splats, live, tile_at, goal):
    pixel = jnp.arange(256, dtype=jnp.int32)
    corner_x = (tile_at % TILES_X * 16).astype(jnp.float32)
    corner_y = (tile_at // TILES_X * 16).astype(jnp.float32)
    grid_x = corner_x + (pixel % 16).astype(jnp.float32) + 0.5
    grid_y = corner_y + (pixel // 16).astype(jnp.float32) + 0.5
    delta_x = grid_x[:, None] - splats[0][None, :]
    delta_y = grid_y[:, None] - splats[1][None, :]
    power = -0.5 * (splats[2][None, :] * delta_x * delta_x + splats[4][None, :] * delta_y * delta_y) - splats[3][None, :] * delta_x * delta_y
    alpha = splats[5][None, :] * jnp.exp(power) * live[None, :]
    log_keep = jnp.log1p(-alpha)
    transmit = jnp.exp(jnp.cumsum(log_keep, axis=1) - log_keep)
    weight = alpha * transmit
    render = jnp.einsum('pk,ck->cp', weight, splats[6:9], precision=HIGH)
    diff = render - goal
    return 8.0 * jnp.sum(diff * diff)

def adam_step(params, adam_m, adam_v, grads):
    new_m = 0.9 * adam_m + 0.1 * grads
    new_v = 0.999 * adam_v + 0.001 * grads * grads
    update = new_m / BIAS_ONE / (jnp.sqrt(new_v / BIAS_TWO) + 1e-08)
    return (params - 0.05 * update, new_m, new_v)

def reference(params, adam_m, adam_v, target, req_rows, tile_list, tile_len, tile_order, tile_pos, bg_ids):
    devices = req_rows.shape[0]
    g_local = params.shape[1] // devices
    tiles_total = tile_order.shape[0]
    list_len = tile_order.shape[1]
    tiles_dev = tiles_total // devices
    regions = devices // 2
    center_y = 8.0 * (tiles_total // TILES_X)
    step_table = jnp.array([0, 1, -1, ROW_REGIONS, -ROW_REGIONS], dtype=jnp.int32)
    lists = tile_list.reshape(tiles_total, list_len)
    ordered = jnp.take_along_axis(lists, tile_order, axis=1).astype(jnp.int32)
    owner_dev = jnp.arange(tiles_total, dtype=jnp.int32) // tiles_dev
    window = ordered // CAP
    offset = step_table[window % 5] + window // 5 * regions
    owner = ((owner_dev[:, None] + offset) % devices).astype(jnp.int32)
    local_row = req_rows[owner_dev[:, None], ordered]
    gauss_ids = (owner * g_local + local_row).astype(jnp.int32)
    live = (tile_order < tile_len[:, None]).astype(jnp.float32)
    targets = target.reshape(3, tiles_total, 256).transpose(1, 0, 2)
    back_live = jnp.ones((bg_ids.shape[0],), jnp.float32)

    def total_loss(rows):
        splats = project(rows, center_y)
        back_splats = splats[:, bg_ids]

        def one(item):
            ids, mask, tile_at, goal = item
            entries = jnp.concatenate([splats[:, ids], back_splats], axis=1)
            return tile_loss(entries, jnp.concatenate([mask, back_live]), tile_at, goal)
        return jnp.sum(lax.map(jax.checkpoint(one), (gauss_ids, live, tile_pos, targets)))
    grads = jax.grad(total_loss)(params)
    return adam_step(params, adam_m, adam_v, grads)
```

```python
import functools

import jax
import jax.numpy as jnp
from jax import lax
from jax.experimental import pallas as pl
from jax.experimental.pallas import tpu as pltpu
from jax.sharding import PartitionSpec as P

TILES_X = 32
NEAR = 10
FOCAL = 512.0
BIAS_ONE = 1.0 - 0.9**10
BIAS_TWO = 1.0 - 0.999**10
MESH = pl.DeviceIdType.MESH
F32 = jnp.float32
BF16 = jnp.bfloat16
LANES = 128
INNER = 16
SPLAT = 9


def harmonics(dir_x, dir_y, dir_z):
    sq_x = dir_x * dir_x
    sq_y = dir_y * dir_y
    sq_z = dir_z * dir_z
    return [
        0.28209479177387814 + 0.0 * dir_x,
        -0.4886025119029199 * dir_y,
        0.4886025119029199 * dir_z,
        -0.4886025119029199 * dir_x,
        1.0925484305920792 * dir_x * dir_y,
        -1.0925484305920792 * dir_y * dir_z,
        0.31539156525252005 * (2.0 * sq_z - sq_x - sq_y),
        -1.0925484305920792 * dir_x * dir_z,
        0.5462742152960396 * (sq_x - sq_y),
        -0.5900435899266435 * dir_y * (3.0 * sq_x - sq_y),
        2.890611442640554 * dir_x * dir_y * dir_z,
        -0.4570457994644658 * dir_y * (4.0 * sq_z - sq_x - sq_y),
        0.3731763325901154 * dir_z * (2.0 * sq_z - 3.0 * sq_x - 3.0 * sq_y),
        -0.4570457994644658 * dir_x * (4.0 * sq_z - sq_x - sq_y),
        1.445305721320277 * dir_z * (sq_x - sq_y),
        -0.5900435899266435 * dir_x * (sq_x - 3.0 * sq_y),
    ]


def geometry(rows, center_y):
    pos_x, pos_y, depth = (rows[0], rows[1], rows[2])
    stretches = (jnp.exp(rows[3]), jnp.exp(rows[4]), jnp.exp(rows[5]))
    quat_norm = jnp.sqrt(
        rows[6] * rows[6] + rows[7] * rows[7] + rows[8] * rows[8] + rows[9] * rows[9]
    )
    inv_norm = 1.0 / quat_norm
    quat_w = rows[6] * inv_norm
    quat_x = rows[7] * inv_norm
    quat_y = rows[8] * inv_norm
    quat_z = rows[9] * inv_norm
    rotation = (
        (
            1.0 - 2.0 * (quat_y * quat_y + quat_z * quat_z),
            2.0 * (quat_x * quat_y - quat_w * quat_z),
            2.0 * (quat_x * quat_z + quat_w * quat_y),
        ),
        (
            2.0 * (quat_x * quat_y + quat_w * quat_z),
            1.0 - 2.0 * (quat_x * quat_x + quat_z * quat_z),
            2.0 * (quat_y * quat_z - quat_w * quat_x),
        ),
        (
            2.0 * (quat_x * quat_z - quat_w * quat_y),
            2.0 * (quat_y * quat_z + quat_w * quat_x),
            1.0 - 2.0 * (quat_x * quat_x + quat_y * quat_y),
        ),
    )
    inv_depth = 1.0 / depth
    focal_z = FOCAL * inv_depth
    slope_x = pos_x * inv_depth
    slope_y = pos_y * inv_depth
    cov_a = 0.3
    cov_b = 0.0
    cov_c = 0.3
    for column in range(3):
        axis_x = rotation[0][column] * stretches[column]
        axis_y = rotation[1][column] * stretches[column]
        axis_z = rotation[2][column] * stretches[column]
        image_u = focal_z * (axis_x - slope_x * axis_z)
        image_v = focal_z * (axis_y - slope_y * axis_z)
        cov_a = cov_a + image_u * image_u
        cov_b = cov_b + image_u * image_v
        cov_c = cov_c + image_v * image_v
    inv_determ = 1.0 / (cov_a * cov_c - cov_b * cov_b)
    center_u = FOCAL * slope_x + 8.0 * TILES_X
    center_v = FOCAL * slope_y + center_y
    inv_distance = 1.0 / jnp.sqrt(pos_x * pos_x + pos_y * pos_y + depth * depth)
    basis = harmonics(pos_x * inv_distance, pos_y * inv_distance, depth * inv_distance)
    conic = [cov_c * inv_determ, -cov_b * inv_determ, cov_a * inv_determ]
    return [center_u, center_v] + conic + basis


def lane_gather(source, index):
    numbers = lax.GatherDimensionNumbers(
        offset_dims=(),
        collapsed_slice_dims=(1,),
        start_index_map=(1,),
        operand_batching_dims=(0,),
        start_indices_batching_dims=(0,),
    )
    return lax.gather(
        source,
        index[..., None],
        numbers,
        (1, 1),
        mode=lax.GatherScatterMode.PROMISE_IN_BOUNDS,
    )


def wide(row, rows=8):
    return jnp.broadcast_to(row, (rows, row.shape[-1]))


def pieces_of(value):
    first = value.astype(BF16)
    return first, (value - first.astype(F32)).astype(BF16)


def project_kernel(center_y, params, bg_ids, splats, back):
    step = pl.program_id(0)
    chunk = params.shape[1]
    rows = [params[i : i + 1, :] for i in range(11)]
    made = geometry(rows, center_y)
    opacity = jax.nn.sigmoid(rows[10])
    colors = []
    for c in range(3):
        total = made[5] * params[11 + c : 12 + c, :]
        for k in range(1, 16):
            total = total + made[5 + k] * params[11 + 3 * k + c : 12 + 3 * k + c, :]
        colors.append(total + 0.5)
    for i, row in enumerate(made[:5] + [opacity] + colors):
        splats[i : i + 1, :] = row
    splats[SPLAT:16, :] = jnp.zeros((16 - SPLAT, chunk), F32)
    me = lax.axis_index("dev")
    g_local = chunk * pl.num_programs(0)

    @pl.when(step == 0)
    def _():
        back[...] = jnp.zeros_like(back)

    local = wide(bg_ids[...] - (me * g_local + step * chunk))
    high = jnp.right_shift(local, 7)
    low = jnp.bitwise_and(local, LANES - 1)
    for half in range(2):
        total = back[half * 8 : half * 8 + 8, :]
        for c in range(chunk // LANES):
            found = lane_gather(splats[half * 8 : half * 8 + 8, c * LANES : (c + 1) * LANES], low)
            total = jnp.where(high == c, found, total)
        back[half * 8 : half * 8 + 8, :] = total


def project_local(params, bg_ids, center_y):
    count, g_local = params.shape
    chunk = 512
    return pl.pallas_call(
        functools.partial(project_kernel, center_y),
        grid=(g_local // chunk,),
        out_shape=(
            jax.ShapeDtypeStruct((16, g_local), F32),
            jax.ShapeDtypeStruct((16, LANES), F32),
        ),
        in_specs=[
            pl.BlockSpec((count, chunk), lambda i: (0, i)),
            pl.BlockSpec((1, LANES), lambda i: (0, 0)),
        ],
        out_specs=(
            pl.BlockSpec((16, chunk), lambda i: (0, i)),
            pl.BlockSpec((16, LANES), lambda i: (0, 0)),
        ),
        name="project_local",
    )(params, bg_ids)


def offsets_of(devices):
    lines = [0, 1, -1, 4, -4]
    return [(lines[w % 5] + w // 5 * (devices // 2)) % devices for w in range(NEAR)]


def exchange(devices, direction, block_of, given, taken, send_sem, recv_sem, local_sem):
    me = lax.axis_index("dev")
    copies = []
    for w, offset in enumerate(offsets_of(devices)):
        if offset == 0:
            copies.append(pltpu.make_async_copy(block_of(given, w), block_of(taken, w), local_sem))
            continue
        copies.append(
            pltpu.make_async_remote_copy(
                src_ref=block_of(given, w),
                dst_ref=block_of(taken, w),
                send_sem=send_sem.at[w],
                recv_sem=recv_sem.at[w],
                device_id=(lax.rem(me + (offset * direction) % devices, devices),),
                device_id_type=MESH,
            )
        )
    return copies


def inner_partner(me, k):
    return me // INNER * INNER + lax.rem(lax.rem(me, INNER) + k, INNER)


def outer_partner(devices, me, k):
    return lax.rem(me + INNER * k, devices)


def spread(count, partner, given, taken, send_sem, recv_sem, base):
    me = lax.axis_index("dev")
    return [
        pltpu.make_async_remote_copy(
            src_ref=given,
            dst_ref=taken.at[k],
            send_sem=send_sem.at[base + k],
            recv_sem=recv_sem.at[base + k],
            device_id=(partner(me, k),),
            device_id_type=MESH,
        )
        for k in range(1, count)
    ]


def greet(devices, inner, outer):
    me = lax.axis_index("dev")
    partners = [lax.rem(me + offset, devices) for offset in offsets_of(devices) if offset]
    if inner:
        partners += [inner_partner(me, k) for k in range(1, INNER)]
    if outer:
        partners += [outer_partner(devices, me, k) for k in range(1, devices // INNER)]
    barrier = pltpu.get_barrier_semaphore()
    for partner in partners:
        pl.semaphore_signal(barrier, inc=1, device_id=(partner,), device_id_type=MESH)
    pl.semaphore_wait(barrier, len(partners))


def request_kernel(devices, req, back, wanted, gathered, send_sem, recv_sem, local_sem):
    cap = req.shape[1] // NEAR
    greet(devices, True, False)
    block = lambda ref, w: ref.at[:, pl.ds(w * cap, cap)]
    copies = exchange(devices, 1, block, req, wanted, send_sem, recv_sem, local_sem.at[0])
    copies += spread(INNER, inner_partner, back, gathered, send_sem, recv_sem, NEAR)
    copies.append(pltpu.make_async_copy(back, gathered.at[0], local_sem.at[1]))
    for copy in copies:
        copy.start()
    for copy in copies:
        copy.wait()


def supply_kernel(devices, sent, back, arrived, gathered, send_sem, recv_sem, local_sem):
    greet(devices, False, True)
    block = lambda ref, w: ref.at[w]
    copies = exchange(devices, -1, block, sent, arrived, send_sem, recv_sem, local_sem.at[0])
    partner = functools.partial(outer_partner, devices)
    copies += spread(devices // INNER, partner, back, gathered, send_sem, recv_sem, NEAR)
    copies.append(pltpu.make_async_copy(back, gathered.at[0], local_sem.at[1]))
    for copy in copies:
        copy.start()
    for copy in copies:
        copy.wait()


def return_kernel(
    devices, grads, back, returned, gathered, held, total, send_sem, recv_sem, local_sem
):
    greet(devices, True, True)
    block = lambda ref, w: ref.at[w]
    inner = spread(INNER, inner_partner, back, held, send_sem, recv_sem, NEAR)
    copies = exchange(devices, 1, block, grads, returned, send_sem, recv_sem, local_sem.at[0])
    for copy in inner + copies:
        copy.start()
    for copy in inner:
        copy.wait()
    summed = back[...]
    for k in range(1, INNER):
        summed = summed + held[k]
    total[...] = summed
    partner = functools.partial(outer_partner, devices)
    outer = spread(devices // INNER, partner, total, gathered, send_sem, recv_sem, NEAR + INNER)
    outer.append(pltpu.make_async_copy(total, gathered.at[0], local_sem.at[1]))
    for copy in outer:
        copy.start()
    for copy in outer + copies:
        copy.wait()


def communicate(kernel, ident, devices, main, back, groups, scratch, semaphores, back_space):
    spec = pl.BlockSpec(memory_space=pl.ANY)
    return pl.pallas_call(
        functools.partial(kernel, devices),
        out_shape=(
            jax.ShapeDtypeStruct(main.shape, main.dtype),
            jax.ShapeDtypeStruct((groups,) + back.shape, F32),
        ),
        in_specs=[spec, pl.BlockSpec(memory_space=back_space)],
        out_specs=(spec, spec),
        scratch_shapes=scratch
        + [
            pltpu.SemaphoreType.DMA((semaphores,)),
            pltpu.SemaphoreType.DMA((semaphores,)),
            pltpu.SemaphoreType.DMA((2,)),
        ],
        compiler_params=pltpu.CompilerParams(collective_id=ident, has_side_effects=True),
        name=kernel.__name__,
    )(main, back)


def owner_gather_kernel(splats, wanted, gathered, sent, back, index):
    for r in range(wanted.shape[1] // LANES):
        index[r : r + 1, :] = wanted[:, r * LANES : (r + 1) * LANES]
    chunks = splats.shape[1] // LANES

    @pl.loop(0, index.shape[0] // 8)
    def _(i):
        rows = index[pl.ds(pl.multiple_of(i * 8, 8), 8), :]
        high = jnp.right_shift(rows, 7)
        low = jnp.bitwise_and(rows, LANES - 1)
        totals = [jnp.zeros((8, LANES), F32) for _ in range(SPLAT)]
        for c in range(chunks):
            here = high == c
            for f in range(SPLAT):
                source = wide(splats[f : f + 1, c * LANES : (c + 1) * LANES])
                totals[f] = jnp.where(here, lane_gather(source, low), totals[f])
        for half in range(2):
            for f in range(SPLAT):
                sent[i * 2 + half, f * 4 : f * 4 + 4, :] = totals[f][half * 4 : half * 4 + 4, :]
            sent[i * 2 + half, 36:40, :] = jnp.zeros((4, LANES), F32)

    summed = gathered[0]
    for k in range(1, gathered.shape[0]):
        summed = summed + gathered[k]
    back[...] = summed


def owner_gather(splats, wanted, gathered):
    slots = wanted.shape[1]
    return pl.pallas_call(
        owner_gather_kernel,
        out_shape=(
            jax.ShapeDtypeStruct((NEAR, 40, LANES), F32),
            jax.ShapeDtypeStruct((16, LANES), F32),
        ),
        scratch_shapes=[pltpu.VMEM((slots // LANES, LANES), jnp.int32)],
        name="owner_gather",
    )(splats, wanted, gathered)


def scatter_columns(index, values, left, right, column, bins):
    high = wide(jnp.right_shift(index, 8), 16)
    low = wide(jnp.bitwise_and(index, 255), 256)
    place = lax.broadcasted_iota(jnp.int32, (256, LANES), 0)
    right[:, pl.ds(column, LANES)] = jnp.where(place == low, 1.0, 0.0).astype(BF16)
    first = values.astype(BF16).astype(F32)
    second = values - first
    for h in range(bins):
        here = high == h
        left[h * 32 : h * 32 + 16, pl.ds(column, LANES)] = jnp.where(here, first, 0.0).astype(BF16)
        left[h * 32 + 16 : h * 32 + 32, pl.ds(column, LANES)] = jnp.where(here, second, 0.0).astype(BF16)


def scatter_product(left, right, product):
    depth = left.shape[1]
    step = 768 if depth % 768 == 0 else 1280
    product[...] = jnp.zeros_like(product)

    @pl.loop(0, depth // step)
    def _(i):
        columns = pl.ds(pl.multiple_of(i * step, LANES), step)
        product[...] += lax.dot_general(
            left[:, columns],
            right[:, columns],
            (((1,), (1,)), ((), ())),
            preferred_element_type=F32,
        )


def tiles_kernel(
    arrived,
    backs,
    tile_list,
    tile_order,
    tile_len,
    tile_pos,
    target,
    slot_grads,
    back_grads,
    order,
    live,
    entries,
    wished_in,
    wished,
    alphas,
    split,
    sums,
    terms,
    carried,
    color_sums,
    entry_grads,
    before,
    after,
    left,
    right,
    product,
):
    tiles, list_len = tile_order.shape
    groups = list_len // LANES
    lasts = groups + 1
    back_row = tiles * groups

    eight = lax.broadcasted_iota(jnp.int32, (8, LANES), 0)
    lengths = jnp.zeros((8, LANES), jnp.int32)
    for t in range(tiles):
        lengths = jnp.where(lax.rem(eight, tiles) == t, tile_len[t], lengths)
    for pair in range(groups // 2):
        ranks = jnp.concatenate(
            [
                tile_order[:, (2 * pair) * LANES : (2 * pair + 1) * LANES],
                tile_order[:, (2 * pair + 1) * LANES : (2 * pair + 2) * LANES],
            ],
            axis=0,
        )
        high = jnp.right_shift(ranks, 7)
        low = jnp.bitwise_and(ranks, LANES - 1)
        named = jnp.zeros((8, LANES), jnp.int32)
        for c in range(groups):
            part = [
                tile_list[:, t * list_len + c * LANES : t * list_len + (c + 1) * LANES]
                for t in range(tiles)
            ]
            source = jnp.concatenate(part + part, axis=0)
            named = jnp.where(high == c, lane_gather(source, low), named)
        order[pair * 8 : pair * 8 + 8, :] = named
        live[pair * 8 : pair * 8 + 8, :] = jnp.where(ranks < lengths, 1.0, 0.0)

    @pl.loop(0, back_row // 8)
    def _(i):
        spots = pl.ds(pl.multiple_of(i * 8, 8), 8)
        slots = order[spots, :]
        high = jnp.right_shift(slots, 7)
        low = jnp.bitwise_and(slots, LANES - 1)

        def window(w, totals):
            totals = list(totals)
            for k in range(4):
                here = high == w * 4 + k
                for f in range(SPLAT):
                    source = wide(arrived[w, f * 4 + k : f * 4 + k + 1, :])
                    totals[f] = jnp.where(here, lane_gather(source, low), totals[f])
            return tuple(totals)

        none = tuple(jnp.zeros((8, LANES), F32) for _ in range(SPLAT))
        totals = lax.fori_loop(0, NEAR, window, none)
        for f in range(SPLAT):
            entries[f, spots, :] = totals[f] * live[spots, :] if f == 5 else totals[f]

    summed = backs[0]
    for k in range(1, backs.shape[0]):
        summed = summed + backs[k]
    for f in range(SPLAT):
        entries[f, back_row : back_row + 1, :] = summed[f : f + 1, :]

    wished_in[...] = jnp.zeros_like(wished_in)
    for t in range(tiles):
        wished_in[3 * t : 3 * t + 3, :] = target[:, t * 256 : (t + 1) * 256]
    columns = jnp.transpose(wished_in[...])
    for t in range(tiles):
        for c in range(3):
            one = columns[:, 3 * t + c : 3 * t + c + 1]
            wished[t * 3 + c] = jnp.broadcast_to(one, (256, LANES))

    row_at = jnp.bitwise_and(lax.broadcasted_iota(jnp.int32, (256, 256), 0), LANES - 1)
    col_at = lax.broadcasted_iota(jnp.int32, (256, 256), 1)
    before[...] = jnp.where((row_at < col_at) | (col_at >= LANES), 1.0, 0.0).astype(BF16)
    after[...] = jnp.where((row_at > col_at) | (col_at >= LANES), 1.0, 0.0).astype(BF16)
    entry_grads[...] = jnp.zeros_like(entry_grads)

    def row_of(t, j):
        listed = j // 2 * 8 + lax.rem(j, 2) * 4 + t
        return jnp.where(j == groups, back_row, listed)

    def entry(f, row):
        return wide(entries[f, pl.ds(row, 1), :])

    across = (
        lax.broadcasted_iota(jnp.int32, (2, 8, LANES), 0) * 8
        + lax.broadcasted_iota(jnp.int32, (2, 8, LANES), 1)
    ).astype(F32) + 0.5

    @pl.loop(0, tiles)
    def _(t):
        place = tile_pos[t]
        corner_x = (lax.rem(place, TILES_X) * 16).astype(F32)
        corner_y = (place // TILES_X * 16).astype(F32)

        @pl.loop(0, lasts)
        def _(j):
            row = row_of(t, j)
            delta_x = (across + corner_x) - entry(0, row)[None]
            center_v = entry(1, row)
            flat = -0.5 * entry(2, row)[None] * delta_x * delta_x
            mixed = -entry(3, row)[None] * delta_x
            half_c = -0.5 * entry(4, row)
            opacity = entry(5, row)[None]
            for y in range(16):
                delta_y = (corner_y + (y + 0.5)) - center_v
                slope = half_c * delta_y
                power = (mixed + slope[None]) * delta_y[None] + flat
                alpha = opacity * jnp.exp(power)
                keep = jnp.log(1.0 - alpha)
                spot = slice(y * 16, y * 16 + 16)
                alphas[j, spot, :] = alpha.reshape(16, LANES)
                first, second = pieces_of(keep.reshape(16, LANES))
                split[j, spot, :LANES] = first
                split[j, spot, LANES:] = second

        @pl.loop(0, lasts)
        def _(j):
            sums[j] = jnp.dot(split[j], before[...], preferred_element_type=F32)

        color_sums[...] = jnp.zeros_like(color_sums)

        @pl.loop(0, 16)
        def _(y):
            spot = pl.ds(pl.multiple_of(y * 16, 16), 16)
            gone = jnp.zeros((16, LANES), F32)
            seen = [jnp.zeros((2, 8, LANES), F32) for _ in range(3)]
            weights = []
            for j in range(lasts):
                row = row_of(t, j)
                transmit = jnp.exp(gone + sums[j, spot, :LANES])
                gone = gone + sums[j, spot, LANES:]
                weight = (alphas[j, spot, :] * transmit).reshape(2, 8, LANES)
                weights.append(weight)
                for c in range(3):
                    seen[c] = seen[c] + weight * entry(6 + c, row)[None]
            slopes = []
            for c in range(3):
                color = jnp.sum(seen[c].reshape(16, LANES), axis=1, keepdims=True)
                slope = 16.0 * (color - wished[t * 3 + c, spot, :])
                slopes.append(slope.reshape(2, 8, LANES))
            for j in range(lasts):
                row = row_of(t, j)
                pull = slopes[0] * entry(6, row)[None]
                pull = pull + slopes[1] * entry(7, row)[None]
                pull = pull + slopes[2] * entry(8, row)[None]
                term = (pull * weights[j]).reshape(16, LANES)
                terms[j, spot, :] = term
                first, second = pieces_of(term)
                split[j, spot, :LANES] = first
                split[j, spot, LANES:] = second
                for c in range(3):
                    part = slopes[c] * weights[j]
                    color_sums[c, j] += part[0] + part[1]

        @pl.loop(0, lasts)
        def _(j):
            sums[j] = jnp.dot(split[j], after[...], preferred_element_type=F32)

        carried[...] = jnp.zeros_like(carried)

        @pl.loop(0, lasts)
        def _(back_j):
            j = groups - back_j
            row = row_of(t, j)
            delta_x = (across + corner_x) - entry(0, row)[None]
            center_v = entry(1, row)
            zero = jnp.zeros((2, 8, LANES), F32)
            sum_none, sum_y, sum_yy = zero, zero, zero
            for y in range(16):
                spot = slice(y * 16, y * 16 + 16)
                behind = carried[spot, :] + sums[j, spot, :LANES]
                carried[spot, :] += sums[j, spot, LANES:]
                alpha = alphas[j, spot, :]
                share = alpha / (1.0 - alpha)
                pull = (terms[j, spot, :] - behind * share).reshape(2, 8, LANES)
                delta_y = ((corner_y + (y + 0.5)) - center_v)[None]
                sum_none = sum_none + pull
                moved = pull * delta_y
                sum_y = sum_y + moved
                sum_yy = sum_yy + moved * delta_y

            def fold(value):
                return jnp.sum(value[0] + value[1], axis=0, keepdims=True)

            first_x = sum_none * delta_x
            in_none = fold(sum_none)
            in_x = fold(first_x)
            in_xx = fold(first_x * delta_x)
            in_xy = fold(sum_y * delta_x)
            in_y = fold(sum_y)
            in_yy = fold(sum_yy)
            con_a, con_b, con_c = (entries[f, pl.ds(row, 1), :] for f in (2, 3, 4))
            made = [
                con_a * in_x + con_b * in_y,
                con_c * in_y + con_b * in_x,
                -0.5 * in_xx,
                -in_xy,
                -0.5 * in_yy,
                in_none,
            ]
            made += [jnp.sum(color_sums[c, j], axis=0, keepdims=True) for c in range(3)]
            for f in range(SPLAT):
                entry_grads[row, f : f + 1, :] += made[f]

    back_grads[...] = entry_grads[back_row]

    @pl.loop(0, back_row)
    def _(r):
        column = pl.multiple_of(r * LANES, LANES)
        scatter_columns(order[pl.ds(r, 1), :], entry_grads[r], left, right, column, 2 * NEAR)

    scatter_product(left, right, product)
    for h in range(2 * NEAR):
        value = product[h * 32 : h * 32 + 16, :] + product[h * 32 + 16 : h * 32 + 32, :]
        for f in range(SPLAT):
            for half in range(2):
                at = f * 4 + (h % 2) * 2 + half
                slot_grads[h // 2, at : at + 1, :] = value[f : f + 1, half * LANES : (half + 1) * LANES]
    for w in range(NEAR):
        slot_grads[w, 36:40, :] = jnp.zeros((4, LANES), F32)


def render_tiles(arrived, backs, tile_list, tile_order, tile_len, tile_pos, target):
    tiles, list_len = tile_order.shape
    rows = tiles * list_len // LANES
    lasts = list_len // LANES + 1
    vmem = pl.BlockSpec(memory_space=pltpu.VMEM)
    smem = pl.BlockSpec(memory_space=pltpu.SMEM)
    return pl.pallas_call(
        tiles_kernel,
        out_shape=(
            jax.ShapeDtypeStruct((NEAR, 40, LANES), F32),
            jax.ShapeDtypeStruct((16, LANES), F32),
        ),
        in_specs=[vmem, vmem, vmem, vmem, smem, smem, vmem],
        out_specs=(vmem, vmem),
        scratch_shapes=[
            pltpu.VMEM((rows, LANES), jnp.int32),
            pltpu.VMEM((rows, LANES), F32),
            pltpu.VMEM((SPLAT, rows + 8, LANES), F32),
            pltpu.VMEM((LANES, 256), F32),
            pltpu.VMEM((tiles * 3, 256, LANES), F32),
            pltpu.VMEM((lasts, 256, LANES), F32),
            pltpu.VMEM((lasts, 256, 256), BF16),
            pltpu.VMEM((lasts, 256, 256), F32),
            pltpu.VMEM((lasts, 256, LANES), F32),
            pltpu.VMEM((256, LANES), F32),
            pltpu.VMEM((3, lasts, 8, LANES), F32),
            pltpu.VMEM((rows + 1, 16, LANES), F32),
            pltpu.VMEM((256, 256), BF16),
            pltpu.VMEM((256, 256), BF16),
            pltpu.VMEM((2 * NEAR * 32, rows * LANES), BF16),
            pltpu.VMEM((256, rows * LANES), BF16),
            pltpu.VMEM((2 * NEAR * 32, 256), F32),
        ],
        compiler_params=pltpu.CompilerParams(vmem_limit_bytes=48 * 2**20),
        name="render_tiles",
    )(arrived, backs, tile_list, tile_order, tile_len, tile_pos, target)


def owner_sum_kernel(returned, wanted, backs, bg_ids, grads, left, right, product):
    slots = wanted.shape[1]
    g_local = grads.shape[1]
    bins = g_local // 256
    padding = lambda count: [jnp.zeros((16 - count, LANES), F32)]

    @pl.loop(0, NEAR)
    def _(w):
        for k in range(4):
            column = pl.multiple_of((w * 4 + k) * LANES, LANES)
            rows = [returned[w, f * 4 + k : f * 4 + k + 1, :] for f in range(SPLAT)]
            values = jnp.concatenate(rows + padding(SPLAT), axis=0)
            scatter_columns(wanted[:, pl.ds(column, LANES)], values, left, right, column, bins)

    summed = backs[0]
    for k in range(1, backs.shape[0]):
        summed = summed + backs[k]
    mine = bg_ids[...] - lax.axis_index("dev") * g_local
    scatter_columns(mine, summed, left, right, slots, bins)
    left[:, slots + LANES :] = jnp.zeros((left.shape[0], LANES), BF16)
    right[:, slots + LANES :] = jnp.zeros((256, LANES), BF16)
    scatter_product(left, right, product)
    for h in range(bins):
        value = product[h * 32 : h * 32 + 16, :] + product[h * 32 + 16 : h * 32 + 32, :]
        grads[:, h * 256 : (h + 1) * 256] = value


def owner_sum(returned, wanted, backs, bg_ids, g_local):
    depth = wanted.shape[1] + 2 * LANES
    bins = g_local // 256
    return pl.pallas_call(
        owner_sum_kernel,
        out_shape=jax.ShapeDtypeStruct((16, g_local), F32),
        scratch_shapes=[
            pltpu.VMEM((bins * 32, depth), BF16),
            pltpu.VMEM((256, depth), BF16),
            pltpu.VMEM((bins * 32, 256), F32),
        ],
        compiler_params=pltpu.CompilerParams(vmem_limit_bytes=48 * 2**20),
        name="owner_sum",
    )(returned, wanted, backs, bg_ids)


def update_kernel(center_y, params, adam_m, adam_v, pulls, new_params, new_m, new_v, grads):
    chunk = params.shape[1]
    rows = [params[i : i + 1, :] for i in range(10)]
    made, pull_back = jax.vjp(lambda given: geometry(given, center_y), rows)
    color_pulls = [pulls[6 + c : 7 + c, :] for c in range(3)]
    given = [pulls[i : i + 1, :] for i in range(5)]
    for k in range(16):
        at = 11 + 3 * k
        total = color_pulls[0] * params[at : at + 1, :]
        total = total + color_pulls[1] * params[at + 1 : at + 2, :]
        total = total + color_pulls[2] * params[at + 2 : at + 3, :]
        given.append(total)
        for c in range(3):
            grads[at + c : at + c + 1, :] = made[5 + k] * color_pulls[c]
    for i, row in enumerate(pull_back(given)[0]):
        grads[i : i + 1, :] = row
    grads[10:11, :] = pulls[5:6, :] * (1.0 - jax.nn.sigmoid(params[10:11, :]))
    slope = grads[...]
    moment = 0.9 * adam_m[...] + 0.1 * slope
    spread_of = 0.999 * adam_v[...] + 0.001 * slope * slope
    update = moment / BIAS_ONE / (jnp.sqrt(spread_of / BIAS_TWO) + 1e-08)
    new_params[...] = params[...] - 0.05 * update
    new_m[...] = moment
    new_v[...] = spread_of


def update(params, adam_m, adam_v, pulls, center_y):
    count, g_local = params.shape
    chunk = 512
    block = pl.BlockSpec((count, chunk), lambda i: (0, i))
    shape = jax.ShapeDtypeStruct(params.shape, F32)
    return pl.pallas_call(
        functools.partial(update_kernel, center_y),
        grid=(g_local // chunk,),
        out_shape=(shape, shape, shape),
        in_specs=[block, block, block, pl.BlockSpec((16, chunk), lambda i: (0, i))],
        out_specs=(block, block, block),
        scratch_shapes=[pltpu.VMEM((count, chunk), F32)],
        name="update",
    )(params, adam_m, adam_v, pulls)


def per_device(
    devices,
    params,
    adam_m,
    adam_v,
    target,
    req_rows,
    tile_list,
    tile_len,
    tile_order,
    tile_pos,
    bg_ids,
):
    g_local = params.shape[1]
    tiles_here = tile_order.shape[0]
    center_y = 8.0 * (tiles_here * devices // TILES_X)
    ids = bg_ids.reshape(1, LANES)
    outer = devices // INNER
    splats, back = project_local(params, ids, center_y)
    wanted, inner_backs = communicate(
        request_kernel, 0, devices, req_rows, back, INNER, [], NEAR + INNER, pl.ANY
    )
    sent, back_part = owner_gather(splats, wanted, inner_backs)
    arrived, backs = communicate(
        supply_kernel, 1, devices, sent, back_part, outer, [], NEAR + outer, pl.ANY
    )
    slot_grads, back_grads = render_tiles(
        arrived, backs, tile_list, tile_order, tile_len, tile_pos, target
    )
    scratch = [pltpu.VMEM((INNER, 16, LANES), F32), pltpu.VMEM((16, LANES), F32)]
    returned, back_sums = communicate(
        return_kernel,
        2,
        devices,
        slot_grads,
        back_grads,
        outer,
        scratch,
        NEAR + INNER + outer,
        pltpu.VMEM,
    )
    pulls = owner_sum(returned, wanted, back_sums, ids, g_local)
    return update(params, adam_m, adam_v, pulls, center_y)


def solution(mesh):
    return jax.shard_map(
        functools.partial(per_device, mesh.shape["dev"]),
        mesh=mesh,
        in_specs=(
            P(None, "dev"),
            P(None, "dev"),
            P(None, "dev"),
            P(None, "dev"),
            P("dev", None),
            P("dev", None),
            P("dev"),
            P("dev", None),
            P("dev"),
            P(),
        ),
        out_specs=(P(None, "dev"), P(None, "dev"), P(None, "dev")),
        check_vma=False,
    )
```

```python
import functools

import jax
import jax.numpy as jnp
from jax import lax
from jax.experimental import pallas as pl
from jax.experimental.pallas import tpu as pltpu
from jax.sharding import PartitionSpec as P

TILES_X = 32
NEAR = 10
FOCAL = 512.0
BIAS_ONE = 1.0 - 0.9**10
BIAS_TWO = 1.0 - 0.999**10
MESH = pl.DeviceIdType.MESH
F32 = jnp.float32
BF16 = jnp.bfloat16
LANES = 128
INNER = 16
SPLAT = 9


def harmonics(dir_x, dir_y, dir_z):
    sq_x = dir_x * dir_x
    sq_y = dir_y * dir_y
    sq_z = dir_z * dir_z
    return [
        0.28209479177387814 + 0.0 * dir_x,
        -0.4886025119029199 * dir_y,
        0.4886025119029199 * dir_z,
        -0.4886025119029199 * dir_x,
        1.0925484305920792 * dir_x * dir_y,
        -1.0925484305920792 * dir_y * dir_z,
        0.31539156525252005 * (2.0 * sq_z - sq_x - sq_y),
        -1.0925484305920792 * dir_x * dir_z,
        0.5462742152960396 * (sq_x - sq_y),
        -0.5900435899266435 * dir_y * (3.0 * sq_x - sq_y),
        2.890611442640554 * dir_x * dir_y * dir_z,
        -0.4570457994644658 * dir_y * (4.0 * sq_z - sq_x - sq_y),
        0.3731763325901154 * dir_z * (2.0 * sq_z - 3.0 * sq_x - 3.0 * sq_y),
        -0.4570457994644658 * dir_x * (4.0 * sq_z - sq_x - sq_y),
        1.445305721320277 * dir_z * (sq_x - sq_y),
        -0.5900435899266435 * dir_x * (sq_x - 3.0 * sq_y),
    ]


def geometry(rows, center_y):
    pos_x, pos_y, depth = (rows[0], rows[1], rows[2])
    stretches = (jnp.exp(rows[3]), jnp.exp(rows[4]), jnp.exp(rows[5]))
    quat_norm = jnp.sqrt(
        rows[6] * rows[6] + rows[7] * rows[7] + rows[8] * rows[8] + rows[9] * rows[9]
    )
    inv_norm = 1.0 / quat_norm
    quat_w = rows[6] * inv_norm
    quat_x = rows[7] * inv_norm
    quat_y = rows[8] * inv_norm
    quat_z = rows[9] * inv_norm
    rotation = (
        (
            1.0 - 2.0 * (quat_y * quat_y + quat_z * quat_z),
            2.0 * (quat_x * quat_y - quat_w * quat_z),
            2.0 * (quat_x * quat_z + quat_w * quat_y),
        ),
        (
            2.0 * (quat_x * quat_y + quat_w * quat_z),
            1.0 - 2.0 * (quat_x * quat_x + quat_z * quat_z),
            2.0 * (quat_y * quat_z - quat_w * quat_x),
        ),
        (
            2.0 * (quat_x * quat_z - quat_w * quat_y),
            2.0 * (quat_y * quat_z + quat_w * quat_x),
            1.0 - 2.0 * (quat_x * quat_x + quat_y * quat_y),
        ),
    )
    inv_depth = 1.0 / depth
    focal_z = FOCAL * inv_depth
    slope_x = pos_x * inv_depth
    slope_y = pos_y * inv_depth
    cov_a = 0.3
    cov_b = 0.0
    cov_c = 0.3
    for column in range(3):
        axis_x = rotation[0][column] * stretches[column]
        axis_y = rotation[1][column] * stretches[column]
        axis_z = rotation[2][column] * stretches[column]
        image_u = focal_z * (axis_x - slope_x * axis_z)
        image_v = focal_z * (axis_y - slope_y * axis_z)
        cov_a = cov_a + image_u * image_u
        cov_b = cov_b + image_u * image_v
        cov_c = cov_c + image_v * image_v
    inv_determ = 1.0 / (cov_a * cov_c - cov_b * cov_b)
    center_u = FOCAL * slope_x + 8.0 * TILES_X
    center_v = FOCAL * slope_y + center_y
    inv_distance = 1.0 / jnp.sqrt(pos_x * pos_x + pos_y * pos_y + depth * depth)
    basis = harmonics(pos_x * inv_distance, pos_y * inv_distance, depth * inv_distance)
    conic = [cov_c * inv_determ, -cov_b * inv_determ, cov_a * inv_determ]
    return [center_u, center_v] + conic + basis


def lane_gather(source, index):
    numbers = lax.GatherDimensionNumbers(
        offset_dims=(),
        collapsed_slice_dims=(1,),
        start_index_map=(1,),
        operand_batching_dims=(0,),
        start_indices_batching_dims=(0,),
    )
    return lax.gather(
        source,
        index[..., None],
        numbers,
        (1, 1),
        mode=lax.GatherScatterMode.PROMISE_IN_BOUNDS,
    )


def wide(row, rows=8):
    return jnp.broadcast_to(row, (rows, row.shape[-1]))


def pieces_of(value):
    first = value.astype(BF16)
    return first, (value - first.astype(F32)).astype(BF16)


def offsets_of(devices):
    lines = [0, 1, -1, 4, -4]
    return [(lines[w % 5] + w // 5 * (devices // 2)) % devices for w in range(NEAR)]


def window_copy(devices, w, direction, given, taken, send_sem, recv_sem, local_sem):
    offset = offsets_of(devices)[w]
    if offset == 0:
        return pltpu.make_async_copy(given, taken, local_sem)
    ahead = (offset * direction) % devices
    return pltpu.make_async_remote_copy(
        src_ref=given,
        dst_ref=taken,
        send_sem=send_sem.at[w],
        recv_sem=recv_sem.at[w],
        device_id=(lax.rem(lax.axis_index("dev") + ahead, devices),),
        device_id_type=MESH,
    )


def inner_partner(devices, me, k):
    return me // INNER * INNER + lax.rem(lax.rem(me, INNER) + k, INNER)


def outer_partner(devices, me, k):
    return lax.rem(me + INNER * k, devices)


def spread(devices, count, partner, given, taken, send_sem, recv_sem):
    return [
        pltpu.make_async_remote_copy(
            src_ref=given,
            dst_ref=taken.at[k],
            send_sem=send_sem.at[k],
            recv_sem=recv_sem.at[k],
            device_id=(partner(devices, lax.axis_index("dev"), k),),
            device_id_type=MESH,
        )
        for k in range(1, count)
    ]


def greet(devices):
    me = lax.axis_index("dev")
    partners = [lax.rem(me + offset, devices) for offset in offsets_of(devices) if offset]
    partners += [inner_partner(devices, me, k) for k in range(1, INNER)]
    partners += [outer_partner(devices, me, k) for k in range(1, devices // INNER)]
    barrier = pltpu.get_barrier_semaphore()
    for partner in partners:
        pl.semaphore_signal(barrier, inc=1, device_id=(partner,), device_id_type=MESH)
    return lambda: pl.semaphore_wait(barrier, len(partners))


def start(copies):
    for copy in copies:
        copy.start()


def finish(copies):
    for copy in copies:
        copy.wait()


def exchange_semaphores(devices):
    return [
        pltpu.SemaphoreType.DMA((NEAR,)),
        pltpu.SemaphoreType.DMA((NEAR,)),
        pltpu.SemaphoreType.DMA((INNER,)),
        pltpu.SemaphoreType.DMA((INNER,)),
        pltpu.SemaphoreType.DMA((devices // INNER,)),
        pltpu.SemaphoreType.DMA((devices // INNER,)),
        pltpu.SemaphoreType.DMA((3,)),
    ]


def feature(laid, f, block):
    first = (block // 2 * 16 + block % 2) * 8 + f % 8
    return laid[f // 8, pl.ds(first, 8, stride=16), :]


def lay_out(params, laid):
    count, g_local = params.shape

    @pl.loop(0, g_local // LANES)
    def _(c):
        columns = pl.ds(pl.multiple_of(c * LANES, LANES), LANES)
        first = pl.multiple_of(c * 8, 8)
        for group in range(count // 8):
            laid[group, pl.ds(first, 8), :] = params[group * 8 : group * 8 + 8, columns]
        over = count % 8
        laid[count // 8, pl.ds(first, over), :] = params[count - over :, columns]


def front_kernel(
    devices,
    center_y,
    params,
    bg_ids,
    req,
    arrived,
    backs,
    wanted,
    laid,
    splats,
    back,
    held,
    part,
    sent,
    index,
    ask_send,
    ask_recv,
    send_sem,
    recv_sem,
    inner_send,
    inner_recv,
    outer_send,
    outer_recv,
    local_sem,
):
    count, g_local = params.shape
    chunks = g_local // LANES
    cap = req.shape[1] // NEAR
    greeted = greet(devices)
    lay_out(params, laid)

    def project(block):
        rows = [feature(laid, f, block) for f in range(11)]
        made = geometry(rows, center_y)
        opacity = jax.nn.sigmoid(rows[10])
        colors = []
        for c in range(3):
            total = made[5] * feature(laid, 11 + c, block)
            for k in range(1, 16):
                total = total + made[5 + k] * feature(laid, 11 + 3 * k + c, block)
            colors.append(total + 0.5)
        for f, row in enumerate(made[:5] + [opacity] + colors):
            splats[f, block % 2, block // 2 * 8 : block // 2 * 8 + 8, :] = row

    project(0)
    greeted()
    asks = []
    for w in range(NEAR):
        columns = pl.ds(w * cap, cap)
        asks.append(
            window_copy(
                devices, w, 1, req.at[:, columns], wanted.at[:, columns], ask_send, ask_recv, local_sem.at[0]
            )
        )
    start(asks)
    for block in range(1, chunks // 8):
        project(block)

    local = wide(bg_ids[...] - lax.axis_index("dev") * g_local)
    high = jnp.right_shift(local, 7)
    low = jnp.bitwise_and(local, LANES - 1)
    eight = lax.broadcasted_iota(jnp.int32, (8, LANES), 0)
    back[...] = jnp.zeros_like(back)
    for f in range(SPLAT):
        total = jnp.zeros((8, LANES), F32)
        for block in range(chunks // 8):
            hb, half = block // 2, block % 2
            found = lane_gather(splats[f, half, hb * 8 : hb * 8 + 8, :], low)
            total = jnp.where(high == hb * 16 + 2 * eight + half, found, total)
        back[f : f + 1, :] = jnp.sum(total, axis=0, keepdims=True)
    inner = spread(devices, INNER, inner_partner, back, held, inner_send, inner_recv)
    start(inner)

    finish(asks)
    for r in range(wanted.shape[1] // LANES):
        index[r : r + 1, :] = wanted[:, r * LANES : (r + 1) * LANES]
    sends = []
    outer = []
    for i in reversed(range(NEAR // 2)):
        rows = index[i * 8 : i * 8 + 8, :]
        high = jnp.right_shift(rows, 7)
        low = jnp.bitwise_and(rows, LANES - 1)

        def pick(step, totals, high=high, low=low):
            totals = list(totals)
            for k in range(4):
                for half in range(2):
                    c = step * 4 + k
                    here = high == 2 * c + half
                    for f in range(SPLAT):
                        source = wide(splats[f, half, pl.ds(c, 1), :])
                        totals[f] = jnp.where(here, lane_gather(source, low), totals[f])
            return tuple(totals)

        none = tuple(jnp.zeros((8, LANES), F32) for _ in range(SPLAT))
        totals = lax.fori_loop(0, chunks // 8, pick, none)
        for half in range(2):
            w = i * 2 + half
            for f in range(SPLAT):
                sent[w, f * 4 : f * 4 + 4, :] = totals[f][half * 4 : half * 4 + 4, :]
            sent[w, 36:40, :] = jnp.zeros((4, LANES), F32)
            sends.append(
                window_copy(
                    devices, w, -1, sent.at[w], arrived.at[w], send_sem, recv_sem, local_sem.at[1]
                )
            )
        start(sends[-2:])
        if i == NEAR // 2 - 2:
            finish(inner)
            summed = back[...]
            for k in range(1, INNER):
                summed = summed + held[k]
            part[...] = summed
            outer = spread(
                devices, devices // INNER, outer_partner, part, backs, outer_send, outer_recv
            )
            start(outer)
            backs[0] = summed
    finish(outer)
    finish(sends)


def supply(devices, params, bg_ids, req_rows, center_y):
    count, g_local = params.shape
    slots = req_rows.shape[1]
    vmem = pl.BlockSpec(memory_space=pltpu.VMEM)
    return pl.pallas_call(
        functools.partial(front_kernel, devices, center_y),
        out_shape=(
            jax.ShapeDtypeStruct((NEAR, 40, LANES), F32),
            jax.ShapeDtypeStruct((devices // INNER, 16, LANES), F32),
            jax.ShapeDtypeStruct((1, slots), jnp.int32),
        ),
        in_specs=[vmem] * 3,
        out_specs=(vmem,) * 3,
        scratch_shapes=[
            pltpu.VMEM((8, g_local // 16, LANES), F32),
            pltpu.VMEM((SPLAT, 2, g_local // 256, LANES), F32),
            pltpu.VMEM((16, LANES), F32),
            pltpu.VMEM((INNER, 16, LANES), F32),
            pltpu.VMEM((16, LANES), F32),
            pltpu.VMEM((NEAR, 40, LANES), F32),
            pltpu.VMEM((slots // LANES, LANES), jnp.int32),
            pltpu.SemaphoreType.DMA((NEAR,)),
            pltpu.SemaphoreType.DMA((NEAR,)),
        ]
        + exchange_semaphores(devices),
        compiler_params=pltpu.CompilerParams(
            collective_id=0, has_side_effects=True, vmem_limit_bytes=48 * 2**20
        ),
        name="supply",
    )(params, bg_ids, req_rows)


def scatter_rows(bins):
    return 16 * (bins + -(-bins // 8))


def scatter_columns(index, eight, ninth, left, right, column, bins):
    high = wide(jnp.right_shift(index, 8))
    low = wide(jnp.bitwise_and(index, 255), 256)
    place = lax.broadcasted_iota(jnp.int32, (256, LANES), 0)
    right[:, pl.ds(column, LANES)] = jnp.where(place == low, 1.0, 0.0).astype(BF16)

    def put(at, here, value):
        first = value.astype(BF16).astype(F32)
        both = [jnp.where(here, first, 0.0), jnp.where(here, value - first, 0.0)]
        left[at : at + 16, pl.ds(column, LANES)] = jnp.concatenate(both, axis=0).astype(BF16)

    for h in range(bins):
        put(h * 16, high == h, eight)
    ninth = wide(ninth)
    for i in range(-(-bins // 8)):
        own = lax.broadcasted_iota(jnp.int32, (8, LANES), 0) + 8 * i
        put((bins + i) * 16, high == own, ninth)


def bin_values(product, half, h, bins):
    eight = product[half, h * 16 : h * 16 + 8, :] + product[half, h * 16 + 8 : h * 16 + 16, :]
    at = (bins + h // 8) * 16 + h % 8
    return eight, product[half, at : at + 1, :] + product[half, at + 8 : at + 9, :]


def scatter_product(left, right, product):
    depth = left.shape[1]
    step = 768 if depth % 768 == 0 else 1280
    product[...] = jnp.zeros_like(product)

    @pl.loop(0, depth // step)
    def _(i):
        columns = pl.ds(pl.multiple_of(i * step, LANES), step)
        made = lax.dot_general(
            left[:, columns],
            right[:, columns],
            (((1,), (1,)), ((), ())),
            preferred_element_type=F32,
        )
        product[0] += made[:, :LANES]
        product[1] += made[:, LANES:]


def tiles_kernel(
    arrived,
    backs,
    tile_list,
    tile_order,
    tile_len,
    tile_pos,
    target,
    slot_grads,
    back_grads,
    order,
    live,
    entries,
    wished_in,
    wished,
    alphas,
    split,
    sums,
    terms,
    carried,
    slopes,
    color_sums,
    entry_grads,
    before,
    after,
    left,
    right,
    product,
):
    tiles, list_len = tile_order.shape
    groups = list_len // LANES
    lasts = groups + 1
    back_row = tiles * groups

    eight = lax.broadcasted_iota(jnp.int32, (8, LANES), 0)
    lengths = jnp.zeros((8, LANES), jnp.int32)
    for t in range(tiles):
        lengths = jnp.where(lax.rem(eight, tiles) == t, tile_len[t], lengths)
    for pair in range(groups // 2):
        ranks = jnp.concatenate(
            [
                tile_order[:, (2 * pair) * LANES : (2 * pair + 1) * LANES],
                tile_order[:, (2 * pair + 1) * LANES : (2 * pair + 2) * LANES],
            ],
            axis=0,
        )
        high = jnp.right_shift(ranks, 7)
        low = jnp.bitwise_and(ranks, LANES - 1)
        named = jnp.zeros((8, LANES), jnp.int32)
        for c in range(groups):
            part = [
                tile_list[:, t * list_len + c * LANES : t * list_len + (c + 1) * LANES]
                for t in range(tiles)
            ]
            source = jnp.concatenate(part + part, axis=0)
            named = jnp.where(high == c, lane_gather(source, low), named)
        order[pair * 8 : pair * 8 + 8, :] = named
        live[pair * 8 : pair * 8 + 8, :] = jnp.where(ranks < lengths, 1.0, 0.0)

    @pl.loop(0, back_row // 8)
    def _(i):
        spots = pl.ds(pl.multiple_of(i * 8, 8), 8)
        slots = order[spots, :]
        high = jnp.right_shift(slots, 7)
        low = jnp.bitwise_and(slots, LANES - 1)

        def window(w, totals):
            totals = list(totals)
            for k in range(4):
                here = high == w * 4 + k
                for f in range(SPLAT):
                    source = wide(arrived[w, f * 4 + k : f * 4 + k + 1, :])
                    totals[f] = jnp.where(here, lane_gather(source, low), totals[f])
            return tuple(totals)

        none = tuple(jnp.zeros((8, LANES), F32) for _ in range(SPLAT))
        totals = lax.fori_loop(0, NEAR, window, none)
        for f in range(SPLAT):
            entries[f, spots, :] = totals[f] * live[spots, :] if f == 5 else totals[f]

    summed = backs[0]
    for k in range(1, backs.shape[0]):
        summed = summed + backs[k]
    for f in range(SPLAT):
        entries[f, back_row : back_row + 1, :] = summed[f : f + 1, :]

    wished_in[...] = jnp.zeros_like(wished_in)
    for t in range(tiles):
        wished_in[3 * t : 3 * t + 3, :] = target[:, t * 256 : (t + 1) * 256]
    columns = jnp.transpose(wished_in[...])
    for t in range(tiles):
        for c in range(3):
            one = columns[:, 3 * t + c : 3 * t + c + 1]
            wished[t * 3 + c] = jnp.broadcast_to(one, (256, LANES))

    row_at = jnp.bitwise_and(lax.broadcasted_iota(jnp.int32, (256, 256), 0), LANES - 1)
    col_at = lax.broadcasted_iota(jnp.int32, (256, 256), 1)
    before[...] = jnp.where((row_at < col_at) | (col_at >= LANES), 1.0, 0.0).astype(BF16)
    after[...] = jnp.where((row_at > col_at) | (col_at >= LANES), 1.0, 0.0).astype(BF16)
    entry_grads[...] = jnp.zeros_like(entry_grads)

    def row_of(t, j):
        listed = j // 2 * 8 + lax.rem(j, 2) * 4 + t
        return jnp.where(j == groups, back_row, listed)

    def entry(f, row):
        return wide(entries[f, pl.ds(row, 1), :])

    across = (
        lax.broadcasted_iota(jnp.int32, (2, 8, LANES), 0) * 8
        + lax.broadcasted_iota(jnp.int32, (2, 8, LANES), 1)
    ).astype(F32) + 0.5

    @pl.loop(0, tiles)
    def _(t):
        place = tile_pos[t]
        corner_x = (lax.rem(place, TILES_X) * 16).astype(F32)
        corner_y = (place // TILES_X * 16).astype(F32)

        @pl.loop(0, lasts)
        def _(j):
            row = row_of(t, j)
            delta_x = (across + corner_x) - entry(0, row)[None]
            center_v = entry(1, row)
            flat = -0.5 * entry(2, row)[None] * delta_x * delta_x
            mixed = -entry(3, row)[None] * delta_x
            half_c = -0.5 * entry(4, row)
            opacity = entry(5, row)[None]
            for y in range(16):
                delta_y = (corner_y + (y + 0.5)) - center_v
                slope = half_c * delta_y
                power = (mixed + slope[None]) * delta_y[None] + flat
                alpha = opacity * jnp.exp(power)
                keep = jnp.log(1.0 - alpha)
                spot = slice(y * 16, y * 16 + 16)
                alphas[j, spot, :] = alpha.reshape(16, LANES)
                first, second = pieces_of(keep.reshape(16, LANES))
                split[j, spot, :LANES] = first
                split[j, spot, LANES:] = second

        for j in range(lasts):
            sums[j] = jnp.dot(split[j], before[...], preferred_element_type=F32)

        @pl.loop(0, 8)
        def _(y):
            spot = pl.ds(pl.multiple_of(y * 32, 32), 32)
            gone = jnp.zeros((32, LANES), F32)
            seen = [jnp.zeros((4, 8, LANES), F32) for _ in range(3)]
            for j in range(lasts):
                row = row_of(t, j)
                transmit = jnp.exp(gone + sums[j, spot, :LANES])
                gone = gone + sums[j, spot, LANES:]
                weight = alphas[j, spot, :] * transmit
                terms[j, spot, :] = weight
                for c in range(3):
                    seen[c] = seen[c] + weight.reshape(4, 8, LANES) * entry(6 + c, row)[None]
            for c in range(3):
                slopes[c, spot, :] = seen[c].reshape(32, LANES)

        for c in range(3):
            color = jnp.sum(slopes[c], axis=1, keepdims=True)
            slopes[c] = 16.0 * (color - wished[t * 3 + c])

        @pl.loop(0, lasts)
        def _(j):
            row = row_of(t, j)
            colors = [entry(6 + c, row)[None] for c in range(3)]
            painted = [jnp.zeros((2, 8, LANES), F32) for _ in range(3)]
            for y in range(16):
                spot = slice(y * 16, y * 16 + 16)
                weight = terms[j, spot, :].reshape(2, 8, LANES)
                slope = [slopes[c, spot, :].reshape(2, 8, LANES) for c in range(3)]
                pull = slope[0] * colors[0] + slope[1] * colors[1] + slope[2] * colors[2]
                term = (pull * weight).reshape(16, LANES)
                terms[j, spot, :] = term
                first, second = pieces_of(term)
                split[j, spot, :LANES] = first
                split[j, spot, LANES:] = second
                for c in range(3):
                    painted[c] = painted[c] + slope[c] * weight
            for c in range(3):
                color_sums[c, j] = painted[c][0] + painted[c][1]

        for j in range(lasts):
            sums[j] = jnp.dot(split[j], after[...], preferred_element_type=F32)

        carried[...] = jnp.zeros_like(carried)

        @pl.loop(0, lasts)
        def _(back_j):
            j = groups - back_j
            row = row_of(t, j)
            delta_x = (across + corner_x) - entry(0, row)[None]
            center_v = entry(1, row)
            zero = jnp.zeros((2, 8, LANES), F32)
            sum_none, sum_y, sum_yy = zero, zero, zero
            for y in range(16):
                spot = slice(y * 16, y * 16 + 16)
                behind = carried[spot, :] + sums[j, spot, :LANES]
                carried[spot, :] += sums[j, spot, LANES:]
                alpha = alphas[j, spot, :]
                share = alpha / (1.0 - alpha)
                pull = (terms[j, spot, :] - behind * share).reshape(2, 8, LANES)
                delta_y = ((corner_y + (y + 0.5)) - center_v)[None]
                sum_none = sum_none + pull
                moved = pull * delta_y
                sum_y = sum_y + moved
                sum_yy = sum_yy + moved * delta_y

            def fold(value):
                return jnp.sum(value[0] + value[1], axis=0, keepdims=True)

            first_x = sum_none * delta_x
            in_none = fold(sum_none)
            in_x = fold(first_x)
            in_xx = fold(first_x * delta_x)
            in_xy = fold(sum_y * delta_x)
            in_y = fold(sum_y)
            in_yy = fold(sum_yy)
            con_a, con_b, con_c = (entries[f, pl.ds(row, 1), :] for f in (2, 3, 4))
            made = [
                con_a * in_x + con_b * in_y,
                con_c * in_y + con_b * in_x,
                -0.5 * in_xx,
                -in_xy,
                -0.5 * in_yy,
                in_none,
            ]
            made += [jnp.sum(color_sums[c, j], axis=0, keepdims=True) for c in range(3)]
            for f in range(SPLAT):
                entry_grads[row, f : f + 1, :] += made[f]

    back_grads[...] = entry_grads[back_row]

    @pl.loop(0, back_row)
    def _(r):
        column = pl.multiple_of(r * LANES, LANES)
        values = entry_grads[r]
        scatter_columns(
            order[pl.ds(r, 1), :], values[0:8], values[8:9], left, right, column, 2 * NEAR
        )

    scatter_product(left, right, product)
    for h in range(2 * NEAR):
        for half in range(2):
            eight, ninth = bin_values(product, half, h, 2 * NEAR)
            for f in range(SPLAT):
                at = f * 4 + (h % 2) * 2 + half
                slot_grads[h // 2, at : at + 1, :] = eight[f : f + 1] if f < 8 else ninth
    for w in range(NEAR):
        slot_grads[w, 36:40, :] = jnp.zeros((4, LANES), F32)


def render_tiles(arrived, backs, tile_list, tile_order, tile_len, tile_pos, target):
    tiles, list_len = tile_order.shape
    rows = tiles * list_len // LANES
    lasts = list_len // LANES + 1
    vmem = pl.BlockSpec(memory_space=pltpu.VMEM)
    smem = pl.BlockSpec(memory_space=pltpu.SMEM)
    return pl.pallas_call(
        tiles_kernel,
        out_shape=(
            jax.ShapeDtypeStruct((NEAR, 40, LANES), F32),
            jax.ShapeDtypeStruct((16, LANES), F32),
        ),
        in_specs=[vmem, vmem, vmem, vmem, smem, smem, vmem],
        out_specs=(vmem, vmem),
        scratch_shapes=[
            pltpu.VMEM((rows, LANES), jnp.int32),
            pltpu.VMEM((rows, LANES), F32),
            pltpu.VMEM((SPLAT, rows + 8, LANES), F32),
            pltpu.VMEM((LANES, 256), F32),
            pltpu.VMEM((tiles * 3, 256, LANES), F32),
            pltpu.VMEM((lasts, 256, LANES), F32),
            pltpu.VMEM((lasts, 256, 256), BF16),
            pltpu.VMEM((lasts, 256, 256), F32),
            pltpu.VMEM((lasts, 256, LANES), F32),
            pltpu.VMEM((256, LANES), F32),
            pltpu.VMEM((3, 256, LANES), F32),
            pltpu.VMEM((3, lasts, 8, LANES), F32),
            pltpu.VMEM((rows + 1, 16, LANES), F32),
            pltpu.VMEM((256, 256), BF16),
            pltpu.VMEM((256, 256), BF16),
            pltpu.VMEM((scatter_rows(2 * NEAR), rows * LANES), BF16),
            pltpu.VMEM((256, rows * LANES), BF16),
            pltpu.VMEM((2, scatter_rows(2 * NEAR), LANES), F32),
        ],
        compiler_params=pltpu.CompilerParams(vmem_limit_bytes=48 * 2**20),
        name="render_tiles",
    )(arrived, backs, tile_list, tile_order, tile_len, tile_pos, target)


def back_kernel(
    devices,
    g_local,
    grads,
    back,
    wanted,
    bg_ids,
    pulls,
    returned,
    gathered,
    held,
    part,
    left,
    right,
    product,
    send_sem,
    recv_sem,
    inner_send,
    inner_recv,
    outer_send,
    outer_recv,
    local_sem,
):
    bins = g_local // 256
    slots = wanted.shape[1]
    greet(devices)()
    inner = spread(devices, INNER, inner_partner, back, held, inner_send, inner_recv)
    start(inner)
    order = [9, 8, 7, 6, 5, 4, 3, 2, 1]
    copies = {
        w: window_copy(
            devices, w, 1, grads.at[w], returned.at[w], send_sem, recv_sem, local_sem.at[0]
        )
        for w in order
    }
    start(copies.values())

    def columns_of(w, source):
        for k in range(4):
            column = (w * 4 + k) * LANES
            eight = source[w, pl.ds(k, 8, stride=4), :]
            ninth = source[w, 32 + k : 33 + k, :]
            scatter_columns(
                wanted[:, column : column + LANES], eight, ninth, left, right, column, bins
            )

    columns_of(0, grads)
    finish(inner)
    summed = back[...]
    for k in range(1, INNER):
        summed = summed + held[k]
    part[...] = summed
    outer = spread(devices, devices // INNER, outer_partner, part, gathered, outer_send, outer_recv)
    start(outer)
    for w in reversed(order):
        copies[w].wait()
        columns_of(w, returned)
    finish(outer)
    summed = part[...]
    for k in range(1, devices // INNER):
        summed = summed + gathered[k]
    mine = bg_ids[...] - lax.axis_index("dev") * g_local
    scatter_columns(mine, summed[0:8], summed[8:9], left, right, slots, bins)
    left[:, slots + LANES :] = jnp.zeros((left.shape[0], LANES), BF16)
    right[:, slots + LANES :] = jnp.zeros((256, LANES), BF16)
    scatter_product(left, right, product)
    for hb in range(bins // 8):
        for half in range(2):
            spot = slice(hb * 8, hb * 8 + 8)
            for f in range(8):
                first = product[half, pl.ds(hb * 128 + f, 8, stride=16), :]
                second = product[half, pl.ds(hb * 128 + 8 + f, 8, stride=16), :]
                pulls[f, half, spot, :] = first + second
            at = (bins + hb) * 16
            ninth = product[half, at : at + 8, :] + product[half, at + 8 : at + 16, :]
            pulls[8, half, spot, :] = ninth


def collect(devices, slot_grads, back_grads, wanted, bg_ids, g_local):
    depth = wanted.shape[1] + 2 * LANES
    bins = g_local // 256
    vmem = pl.BlockSpec(memory_space=pltpu.VMEM)
    return pl.pallas_call(
        functools.partial(back_kernel, devices, g_local),
        out_shape=jax.ShapeDtypeStruct((SPLAT, 2, bins, LANES), F32),
        in_specs=[vmem] * 4,
        out_specs=vmem,
        scratch_shapes=[
            pltpu.VMEM((NEAR, 40, LANES), F32),
            pltpu.VMEM((devices // INNER, 16, LANES), F32),
            pltpu.VMEM((INNER, 16, LANES), F32),
            pltpu.VMEM((16, LANES), F32),
            pltpu.VMEM((scatter_rows(bins), depth), BF16),
            pltpu.VMEM((256, depth), BF16),
            pltpu.VMEM((2, scatter_rows(bins), LANES), F32),
        ]
        + exchange_semaphores(devices),
        compiler_params=pltpu.CompilerParams(
            collective_id=1, has_side_effects=True, vmem_limit_bytes=48 * 2**20
        ),
        name="collect",
    )(slot_grads, back_grads, wanted, bg_ids)


def update_kernel(
    center_y,
    params,
    adam_m,
    adam_v,
    pulls,
    new_params,
    new_m,
    new_v,
    laid,
    grads,
    held_params,
    held_m,
    held_v,
    sems,
):
    count, g_local = params.shape
    lay_out(params, laid)
    copies = []
    for hb in range(g_local // 2048):
        for half in range(2):
            block = hb * 2 + half
            rows = [feature(laid, f, block) for f in range(10)]
            made, pull_back = jax.vjp(lambda given: geometry(given, center_y), rows)
            got = [pulls[f, half, hb * 8 : hb * 8 + 8, :] for f in range(SPLAT)]

            def put(f, value):
                first = (hb * 16 + half) * 8 + f % 8
                grads[f // 8, pl.ds(first, 8, stride=16), :] = value

            given = got[:5]
            for k in range(16):
                at = 11 + 3 * k
                total = got[6] * feature(laid, at, block)
                total = total + got[7] * feature(laid, at + 1, block)
                total = total + got[8] * feature(laid, at + 2, block)
                given.append(total)
                for c in range(3):
                    put(at + c, made[5 + k] * got[6 + c])
            for f, row in enumerate(pull_back(given)[0]):
                put(f, row)
            put(10, got[5] * (1.0 - jax.nn.sigmoid(feature(laid, 10, block))))

        @pl.loop(0, 16)
        def _(chunk):
            c = hb * 16 + chunk
            columns = pl.ds(pl.multiple_of(c * LANES, LANES), LANES)
            first = pl.multiple_of(c * 8, 8)
            for group in range(-(-count // 8)):
                size = min(8, count - group * 8)
                spot = slice(group * 8, group * 8 + size)
                slope = grads[group, pl.ds(first, size), :]
                moment = 0.9 * adam_m[spot, columns] + 0.1 * slope
                power = 0.999 * adam_v[spot, columns] + 0.001 * slope * slope
                change = moment / BIAS_ONE / (jnp.sqrt(power / BIAS_TWO) + 1e-08)
                held_params[spot, columns] = params[spot, columns] - 0.05 * change
                held_m[spot, columns] = moment
                held_v[spot, columns] = power

        columns = pl.ds(hb * 2048, 2048)
        for i, (held, out) in enumerate(
            ((held_params, new_params), (held_m, new_m), (held_v, new_v))
        ):
            copies.append(
                pltpu.make_async_copy(held.at[:, columns], out.at[:, columns], sems.at[hb * 3 + i])
            )
        start(copies[-3:])
    finish(copies)


def update(params, adam_m, adam_v, pulls, center_y):
    count, g_local = params.shape
    vmem = pl.BlockSpec(memory_space=pltpu.VMEM)
    far = pl.BlockSpec(memory_space=pl.ANY)
    shape = jax.ShapeDtypeStruct(params.shape, F32)
    return pl.pallas_call(
        functools.partial(update_kernel, center_y),
        out_shape=(shape, shape, shape),
        in_specs=[vmem] * 4,
        out_specs=(far, far, far),
        scratch_shapes=[
            pltpu.VMEM((8, g_local // 16, LANES), F32),
            pltpu.VMEM((8, g_local // 16, LANES), F32),
            pltpu.VMEM((count, g_local), F32),
            pltpu.VMEM((count, g_local), F32),
            pltpu.VMEM((count, g_local), F32),
            pltpu.SemaphoreType.DMA((3 * (g_local // 2048),)),
        ],
        compiler_params=pltpu.CompilerParams(vmem_limit_bytes=48 * 2**20),
        name="update",
    )(params, adam_m, adam_v, pulls)


def per_device(
    devices,
    params,
    adam_m,
    adam_v,
    target,
    req_rows,
    tile_list,
    tile_len,
    tile_order,
    tile_pos,
    bg_ids,
):
    g_local = params.shape[1]
    tiles_here = tile_order.shape[0]
    center_y = 8.0 * (tiles_here * devices // TILES_X)
    ids = bg_ids.reshape(1, LANES)
    arrived, backs, wanted = supply(devices, params, ids, req_rows, center_y)
    slot_grads, back_grads = render_tiles(
        arrived, backs, tile_list, tile_order, tile_len, tile_pos, target
    )
    pulls = collect(devices, slot_grads, back_grads, wanted, ids, g_local)
    return update(params, adam_m, adam_v, pulls, center_y)


def solution(mesh):
    return jax.shard_map(
        functools.partial(per_device, mesh.shape["dev"]),
        mesh=mesh,
        in_specs=(
            P(None, "dev"),
            P(None, "dev"),
            P(None, "dev"),
            P(None, "dev"),
            P("dev", None),
            P("dev", None),
            P("dev"),
            P("dev", None),
            P("dev"),
            P(),
        ),
        out_specs=(P(None, "dev"), P(None, "dev"), P(None, "dev")),
        check_vma=False,
    )
```

```python
import functools

import jax
import jax.numpy as jnp
from jax import lax
from jax.experimental import pallas as pl
from jax.experimental.pallas import tpu as pltpu
from jax.sharding import PartitionSpec as P

TILES_X = 32
NEAR = 10
FOCAL = 512.0
BIAS_ONE = 1.0 - 0.9**10
BIAS_TWO = 1.0 - 0.999**10
MESH = pl.DeviceIdType.MESH
F32 = jnp.float32
BF16 = jnp.bfloat16
LANES = 128
INNER = 16
SPLAT = 9


def harmonics(dir_x, dir_y, dir_z):
    sq_x = dir_x * dir_x
    sq_y = dir_y * dir_y
    sq_z = dir_z * dir_z
    return [
        0.28209479177387814 + 0.0 * dir_x,
        -0.4886025119029199 * dir_y,
        0.4886025119029199 * dir_z,
        -0.4886025119029199 * dir_x,
        1.0925484305920792 * dir_x * dir_y,
        -1.0925484305920792 * dir_y * dir_z,
        0.31539156525252005 * (2.0 * sq_z - sq_x - sq_y),
        -1.0925484305920792 * dir_x * dir_z,
        0.5462742152960396 * (sq_x - sq_y),
        -0.5900435899266435 * dir_y * (3.0 * sq_x - sq_y),
        2.890611442640554 * dir_x * dir_y * dir_z,
        -0.4570457994644658 * dir_y * (4.0 * sq_z - sq_x - sq_y),
        0.3731763325901154 * dir_z * (2.0 * sq_z - 3.0 * sq_x - 3.0 * sq_y),
        -0.4570457994644658 * dir_x * (4.0 * sq_z - sq_x - sq_y),
        1.445305721320277 * dir_z * (sq_x - sq_y),
        -0.5900435899266435 * dir_x * (sq_x - 3.0 * sq_y),
    ]


def geometry(rows, center_y):
    pos_x, pos_y, depth = (rows[0], rows[1], rows[2])
    stretches = (jnp.exp(rows[3]), jnp.exp(rows[4]), jnp.exp(rows[5]))
    quat_norm = jnp.sqrt(
        rows[6] * rows[6] + rows[7] * rows[7] + rows[8] * rows[8] + rows[9] * rows[9]
    )
    inv_norm = 1.0 / quat_norm
    quat_w = rows[6] * inv_norm
    quat_x = rows[7] * inv_norm
    quat_y = rows[8] * inv_norm
    quat_z = rows[9] * inv_norm
    rotation = (
        (
            1.0 - 2.0 * (quat_y * quat_y + quat_z * quat_z),
            2.0 * (quat_x * quat_y - quat_w * quat_z),
            2.0 * (quat_x * quat_z + quat_w * quat_y),
        ),
        (
            2.0 * (quat_x * quat_y + quat_w * quat_z),
            1.0 - 2.0 * (quat_x * quat_x + quat_z * quat_z),
            2.0 * (quat_y * quat_z - quat_w * quat_x),
        ),
        (
            2.0 * (quat_x * quat_z - quat_w * quat_y),
            2.0 * (quat_y * quat_z + quat_w * quat_x),
            1.0 - 2.0 * (quat_x * quat_x + quat_y * quat_y),
        ),
    )
    inv_depth = 1.0 / depth
    focal_z = FOCAL * inv_depth
    slope_x = pos_x * inv_depth
    slope_y = pos_y * inv_depth
    cov_a = 0.3
    cov_b = 0.0
    cov_c = 0.3
    for column in range(3):
        axis_x = rotation[0][column] * stretches[column]
        axis_y = rotation[1][column] * stretches[column]
        axis_z = rotation[2][column] * stretches[column]
        image_u = focal_z * (axis_x - slope_x * axis_z)
        image_v = focal_z * (axis_y - slope_y * axis_z)
        cov_a = cov_a + image_u * image_u
        cov_b = cov_b + image_u * image_v
        cov_c = cov_c + image_v * image_v
    inv_determ = 1.0 / (cov_a * cov_c - cov_b * cov_b)
    center_u = FOCAL * slope_x + 8.0 * TILES_X
    center_v = FOCAL * slope_y + center_y
    inv_distance = 1.0 / jnp.sqrt(pos_x * pos_x + pos_y * pos_y + depth * depth)
    basis = harmonics(pos_x * inv_distance, pos_y * inv_distance, depth * inv_distance)
    conic = [cov_c * inv_determ, -cov_b * inv_determ, cov_a * inv_determ]
    return [center_u, center_v] + conic + basis


def lane_gather(source, index):
    numbers = lax.GatherDimensionNumbers(
        offset_dims=(),
        collapsed_slice_dims=(1,),
        start_index_map=(1,),
        operand_batching_dims=(0,),
        start_indices_batching_dims=(0,),
    )
    return lax.gather(
        source,
        index[..., None],
        numbers,
        (1, 1),
        mode=lax.GatherScatterMode.PROMISE_IN_BOUNDS,
    )


def wide(row, rows=8):
    return jnp.broadcast_to(row, (rows, row.shape[-1]))


def pieces_of(value):
    first = value.astype(BF16)
    return first, (value - first.astype(F32)).astype(BF16)


def offsets_of(devices):
    lines = [0, 1, -1, 4, -4]
    return [(lines[w % 5] + w // 5 * (devices // 2)) % devices for w in range(NEAR)]


def window_copy(devices, w, direction, given, taken, send_sem, recv_sem, local_sem):
    offset = offsets_of(devices)[w]
    if offset == 0:
        return pltpu.make_async_copy(given, taken, local_sem)
    ahead = (offset * direction) % devices
    return pltpu.make_async_remote_copy(
        src_ref=given,
        dst_ref=taken,
        send_sem=send_sem.at[w],
        recv_sem=recv_sem.at[w],
        device_id=(lax.rem(lax.axis_index("dev") + ahead, devices),),
        device_id_type=MESH,
    )


def inner_partner(devices, me, k):
    return me // INNER * INNER + lax.rem(lax.rem(me, INNER) + k, INNER)


def outer_partner(devices, me, k):
    return lax.rem(me + INNER * k, devices)


def spread(devices, count, partner, given, taken, send_sem, recv_sem):
    return [
        pltpu.make_async_remote_copy(
            src_ref=given,
            dst_ref=taken.at[k],
            send_sem=send_sem.at[k],
            recv_sem=recv_sem.at[k],
            device_id=(partner(devices, lax.axis_index("dev"), k),),
            device_id_type=MESH,
        )
        for k in range(1, count)
    ]


def greet(devices):
    me = lax.axis_index("dev")
    partners = [lax.rem(me + offset, devices) for offset in offsets_of(devices) if offset]
    partners += [inner_partner(devices, me, k) for k in range(1, INNER)]
    partners += [outer_partner(devices, me, k) for k in range(1, devices // INNER)]
    barrier = pltpu.get_barrier_semaphore()
    for partner in partners:
        pl.semaphore_signal(barrier, inc=1, device_id=(partner,), device_id_type=MESH)
    return lambda: pl.semaphore_wait(barrier, len(partners))


def start(copies):
    for copy in copies:
        copy.start()


def finish(copies):
    for copy in copies:
        copy.wait()


def sum_of(first, taken):
    total = first
    for k in range(1, taken.shape[0]):
        total = total + taken[k]
    return total


def feature(laid, f, block):
    first = (block // 2 * 16 + block % 2) * 8 + f % 8
    return laid[f // 8, pl.ds(first, 8, stride=16), :]


def lay_out(params, laid):
    count, g_local = params.shape

    @pl.loop(0, g_local // LANES)
    def _(c):
        columns = pl.ds(pl.multiple_of(c * LANES, LANES), LANES)
        first = pl.multiple_of(c * 8, 8)
        for group in range(count // 8):
            laid[group, pl.ds(first, 8), :] = params[group * 8 : group * 8 + 8, columns]
        over = count % 8
        laid[count // 8, pl.ds(first, over), :] = params[count - over :, columns]


def project(center_y, laid, splats, block):
    rows = [feature(laid, f, block) for f in range(11)]
    made = geometry(rows, center_y)
    opacity = jax.nn.sigmoid(rows[10])
    colors = []
    for c in range(3):
        total = made[5] * feature(laid, 11 + c, block)
        for k in range(1, 16):
            total = total + made[5 + k] * feature(laid, 11 + 3 * k + c, block)
        colors.append(total + 0.5)
    for f, row in enumerate(made[:5] + [opacity] + colors):
        splats[f, block % 2, block // 2 * 8 : block // 2 * 8 + 8, :] = row


def own_back(splats, mine, back):
    local = wide(mine)
    high = jnp.right_shift(local, 7)
    low = jnp.bitwise_and(local, LANES - 1)
    eight = lax.broadcasted_iota(jnp.int32, (8, LANES), 0)
    back[...] = jnp.zeros_like(back)
    for f in range(SPLAT):
        total = jnp.zeros((8, LANES), F32)
        for block in range(2 * splats.shape[2] // 8):
            hb, half = block // 2, block % 2
            found = lane_gather(splats[f, half, hb * 8 : hb * 8 + 8, :], low)
            total = jnp.where(high == hb * 16 + 2 * eight + half, found, total)
        back[f : f + 1, :] = jnp.sum(total, axis=0, keepdims=True)


def owner_gather(splats, wanted, i, sent):
    first = i * 8 * LANES
    rows = jnp.concatenate(
        [wanted[:, first + r * LANES : first + (r + 1) * LANES] for r in range(8)], axis=0
    )
    high = jnp.right_shift(rows, 7)
    low = jnp.bitwise_and(rows, LANES - 1)

    def pick(step, totals):
        totals = list(totals)
        for k in range(4):
            for half in range(2):
                c = step * 4 + k
                here = high == 2 * c + half
                for f in range(SPLAT):
                    source = wide(splats[f, half, pl.ds(c, 1), :])
                    totals[f] = jnp.where(here, lane_gather(source, low), totals[f])
        return tuple(totals)

    none = tuple(jnp.zeros((8, LANES), F32) for _ in range(SPLAT))
    totals = lax.fori_loop(0, splats.shape[2] // 4, pick, none)
    for half in range(2):
        for f in range(SPLAT):
            sent[i * 2 + half, f * 4 : f * 4 + 4, :] = totals[f][half * 4 : half * 4 + 4, :]
        sent[i * 2 + half, 36:40, :] = jnp.zeros((4, LANES), F32)


def scatter_rows(bins):
    return 16 * (bins + -(-bins // 8))


def scatter_columns(index, eight, ninth, left, right, column, bins):
    high = wide(jnp.right_shift(index, 8))
    low = wide(jnp.bitwise_and(index, 255), 256)
    place = lax.broadcasted_iota(jnp.int32, (256, LANES), 0)
    right[:, pl.ds(column, LANES)] = jnp.where(place == low, 1.0, 0.0).astype(BF16)

    def put(at, here, value):
        first = value.astype(BF16).astype(F32)
        both = [jnp.where(here, first, 0.0), jnp.where(here, value - first, 0.0)]
        left[at : at + 16, pl.ds(column, LANES)] = jnp.concatenate(both, axis=0).astype(BF16)

    for h in range(bins):
        put(h * 16, high == h, eight)
    ninth = wide(ninth)
    for i in range(-(-bins // 8)):
        own = lax.broadcasted_iota(jnp.int32, (8, LANES), 0) + 8 * i
        put((bins + i) * 16, high == own, ninth)


def bin_values(product, half, h, bins):
    eight = product[half, h * 16 : h * 16 + 8, :] + product[half, h * 16 + 8 : h * 16 + 16, :]
    at = (bins + h // 8) * 16 + h % 8
    return eight, product[half, at : at + 1, :] + product[half, at + 8 : at + 9, :]


def scatter_product(left, right, product):
    depth = left.shape[1]
    step = 768 if depth % 768 == 0 else 1280
    product[...] = jnp.zeros_like(product)

    @pl.loop(0, depth // step)
    def _(i):
        columns = pl.ds(pl.multiple_of(i * step, LANES), step)
        made = lax.dot_general(
            left[:, columns],
            right[:, columns],
            (((1,), (1,)), ((), ())),
            preferred_element_type=F32,
        )
        product[0] += made[:, :LANES]
        product[1] += made[:, LANES:]


def tiles_setup(
    tile_list, tile_order, tile_len, target, order, live, wished_in, wished, before, after
):
    tiles, list_len = tile_order.shape
    groups = list_len // LANES

    eight = lax.broadcasted_iota(jnp.int32, (8, LANES), 0)
    lengths = jnp.zeros((8, LANES), jnp.int32)
    for t in range(tiles):
        lengths = jnp.where(lax.rem(eight, tiles) == t, tile_len[t], lengths)
    for pair in range(groups // 2):
        ranks = jnp.concatenate(
            [
                tile_order[:, (2 * pair) * LANES : (2 * pair + 1) * LANES],
                tile_order[:, (2 * pair + 1) * LANES : (2 * pair + 2) * LANES],
            ],
            axis=0,
        )
        high = jnp.right_shift(ranks, 7)
        low = jnp.bitwise_and(ranks, LANES - 1)
        named = jnp.zeros((8, LANES), jnp.int32)
        for c in range(groups):
            part = [
                tile_list[:, t * list_len + c * LANES : t * list_len + (c + 1) * LANES]
                for t in range(tiles)
            ]
            source = jnp.concatenate(part + part, axis=0)
            named = jnp.where(high == c, lane_gather(source, low), named)
        order[pair * 8 : pair * 8 + 8, :] = named
        live[pair * 8 : pair * 8 + 8, :] = jnp.where(ranks < lengths, 1.0, 0.0)

    wished_in[...] = jnp.zeros_like(wished_in)
    for t in range(tiles):
        wished_in[3 * t : 3 * t + 3, :] = target[:, t * 256 : (t + 1) * 256]
    columns = jnp.transpose(wished_in[...])
    for t in range(tiles):
        for c in range(3):
            one = columns[:, 3 * t + c : 3 * t + c + 1]
            wished[t * 3 + c] = jnp.broadcast_to(one, (256, LANES))

    row_at = jnp.bitwise_and(lax.broadcasted_iota(jnp.int32, (256, 256), 0), LANES - 1)
    col_at = lax.broadcasted_iota(jnp.int32, (256, 256), 1)
    before[...] = jnp.where((row_at < col_at) | (col_at >= LANES), 1.0, 0.0).astype(BF16)
    after[...] = jnp.where((row_at > col_at) | (col_at >= LANES), 1.0, 0.0).astype(BF16)


def tiles_gather(w, arrived, order, entries):
    @pl.loop(0, order.shape[0] // 8)
    def _(i):
        spots = pl.ds(pl.multiple_of(i * 8, 8), 8)
        slots = order[spots, :]
        high = jnp.right_shift(slots, 7)
        low = jnp.bitwise_and(slots, LANES - 1)
        totals = [entries[f, spots, :] for f in range(SPLAT)]
        for k in range(4):
            here = high == w * 4 + k
            for f in range(SPLAT):
                source = wide(arrived[w, f * 4 + k : f * 4 + k + 1, :])
                totals[f] = jnp.where(here, lane_gather(source, low), totals[f])
        for f in range(SPLAT):
            entries[f, spots, :] = totals[f]


def tiles_render(
    tiles,
    tile_pos,
    entries,
    wished,
    alphas,
    split,
    sums,
    terms,
    carried,
    slopes,
    color_sums,
    entry_grads,
    before,
    after,
):
    lasts = alphas.shape[0]
    groups = lasts - 1
    back_row = tiles * groups
    entry_grads[...] = jnp.zeros_like(entry_grads)

    def row_of(t, j):
        listed = j // 2 * 8 + lax.rem(j, 2) * 4 + t
        return jnp.where(j == groups, back_row, listed)

    def entry(f, row):
        return wide(entries[f, pl.ds(row, 1), :])

    across = (
        lax.broadcasted_iota(jnp.int32, (2, 8, LANES), 0) * 8
        + lax.broadcasted_iota(jnp.int32, (2, 8, LANES), 1)
    ).astype(F32) + 0.5

    @pl.loop(0, tiles)
    def _(t):
        place = tile_pos[t]
        corner_x = (lax.rem(place, TILES_X) * 16).astype(F32)
        corner_y = (place // TILES_X * 16).astype(F32)

        @pl.loop(0, lasts)
        def _(j):
            row = row_of(t, j)
            delta_x = (across + corner_x) - entry(0, row)[None]
            center_v = entry(1, row)
            flat = -0.5 * entry(2, row)[None] * delta_x * delta_x
            mixed = -entry(3, row)[None] * delta_x
            half_c = -0.5 * entry(4, row)
            opacity = entry(5, row)[None]
            for y in range(16):
                delta_y = (corner_y + (y + 0.5)) - center_v
                slope = half_c * delta_y
                power = (mixed + slope[None]) * delta_y[None] + flat
                alpha = opacity * jnp.exp(power)
                keep = jnp.log(1.0 - alpha)
                spot = slice(y * 16, y * 16 + 16)
                alphas[j, spot, :] = alpha.reshape(16, LANES)
                first, second = pieces_of(keep.reshape(16, LANES))
                split[j, spot, :LANES] = first
                split[j, spot, LANES:] = second

        for j in range(lasts):
            sums[j] = jnp.dot(split[j], before[...], preferred_element_type=F32)

        @pl.loop(0, 8)
        def _(y):
            spot = pl.ds(pl.multiple_of(y * 32, 32), 32)
            gone = jnp.zeros((32, LANES), F32)
            seen = [jnp.zeros((4, 8, LANES), F32) for _ in range(3)]
            for j in range(lasts):
                row = row_of(t, j)
                transmit = jnp.exp(gone + sums[j, spot, :LANES])
                gone = gone + sums[j, spot, LANES:]
                weight = alphas[j, spot, :] * transmit
                terms[j, spot, :] = weight
                for c in range(3):
                    seen[c] = seen[c] + weight.reshape(4, 8, LANES) * entry(6 + c, row)[None]
            for c in range(3):
                slopes[c, spot, :] = seen[c].reshape(32, LANES)

        for c in range(3):
            color = jnp.sum(slopes[c], axis=1, keepdims=True)
            slopes[c] = 16.0 * (color - wished[t * 3 + c])

        @pl.loop(0, lasts)
        def _(j):
            row = row_of(t, j)
            colors = [entry(6 + c, row)[None] for c in range(3)]
            painted = [jnp.zeros((2, 8, LANES), F32) for _ in range(3)]
            for y in range(16):
                spot = slice(y * 16, y * 16 + 16)
                weight = terms[j, spot, :].reshape(2, 8, LANES)
                slope = [slopes[c, spot, :].reshape(2, 8, LANES) for c in range(3)]
                pull = slope[0] * colors[0] + slope[1] * colors[1] + slope[2] * colors[2]
                term = (pull * weight).reshape(16, LANES)
                terms[j, spot, :] = term
                first, second = pieces_of(term)
                split[j, spot, :LANES] = first
                split[j, spot, LANES:] = second
                for c in range(3):
                    painted[c] = painted[c] + slope[c] * weight
            for c in range(3):
                color_sums[c, j] = painted[c][0] + painted[c][1]

        for j in range(lasts):
            sums[j] = jnp.dot(split[j], after[...], preferred_element_type=F32)

        carried[...] = jnp.zeros_like(carried)

        @pl.loop(0, lasts)
        def _(back_j):
            j = groups - back_j
            row = row_of(t, j)
            delta_x = (across + corner_x) - entry(0, row)[None]
            center_v = entry(1, row)
            zero = jnp.zeros((2, 8, LANES), F32)
            sum_none, sum_y, sum_yy = zero, zero, zero
            for y in range(16):
                spot = slice(y * 16, y * 16 + 16)
                behind = carried[spot, :] + sums[j, spot, :LANES]
                carried[spot, :] += sums[j, spot, LANES:]
                alpha = alphas[j, spot, :]
                share = alpha / (1.0 - alpha)
                pull = (terms[j, spot, :] - behind * share).reshape(2, 8, LANES)
                delta_y = ((corner_y + (y + 0.5)) - center_v)[None]
                sum_none = sum_none + pull
                moved = pull * delta_y
                sum_y = sum_y + moved
                sum_yy = sum_yy + moved * delta_y

            def fold(value):
                return jnp.sum(value[0] + value[1], axis=0, keepdims=True)

            first_x = sum_none * delta_x
            in_none = fold(sum_none)
            in_x = fold(first_x)
            in_xx = fold(first_x * delta_x)
            in_xy = fold(sum_y * delta_x)
            in_y = fold(sum_y)
            in_yy = fold(sum_yy)
            con_a, con_b, con_c = (entries[f, pl.ds(row, 1), :] for f in (2, 3, 4))
            made = [
                con_a * in_x + con_b * in_y,
                con_c * in_y + con_b * in_x,
                -0.5 * in_xx,
                -in_xy,
                -0.5 * in_yy,
                in_none,
            ]
            made += [jnp.sum(color_sums[c, j], axis=0, keepdims=True) for c in range(3)]
            for f in range(SPLAT):
                entry_grads[row, f : f + 1, :] += made[f]


def slot_columns(order, entry_grads, left, right):
    @pl.loop(0, order.shape[0])
    def _(r):
        column = pl.multiple_of(r * LANES, LANES)
        values = entry_grads[r]
        scatter_columns(
            order[pl.ds(r, 1), :], values[0:8], values[8:9], left, right, column, 2 * NEAR
        )


def slot_values(product, slot_grads):
    for h in range(2 * NEAR):
        for half in range(2):
            eight, ninth = bin_values(product, half, h, 2 * NEAR)
            for f in range(SPLAT):
                at = f * 4 + (h % 2) * 2 + half
                slot_grads[h // 2, at : at + 1, :] = eight[f : f + 1] if f < 8 else ninth
    for w in range(NEAR):
        slot_grads[w, 36:40, :] = jnp.zeros((4, LANES), F32)


def owner_columns(w, source, wanted, left, right, bins):
    for k in range(4):
        column = (w * 4 + k) * LANES
        eight = source[w, pl.ds(k, 8, stride=4), :]
        ninth = source[w, 32 + k : 33 + k, :]
        index = wanted[:, column : column + LANES]
        scatter_columns(index, eight, ninth, left, right, column, bins)


def owner_values(product, bins, pulls):
    for hb in range(bins // 8):
        for half in range(2):
            spot = slice(hb * 8, hb * 8 + 8)
            for f in range(8):
                first = product[half, pl.ds(hb * 128 + f, 8, stride=16), :]
                second = product[half, pl.ds(hb * 128 + 8 + f, 8, stride=16), :]
                pulls[f, half, spot, :] = first + second
            at = (bins + hb) * 16
            ninth = product[half, at : at + 8, :] + product[half, at + 8 : at + 16, :]
            pulls[8, half, spot, :] = ninth


def step_kernel(
    devices,
    center_y,
    far_params,
    far_m,
    far_v,
    far_target,
    far_req,
    far_list,
    tile_len,
    far_order,
    tile_pos,
    far_ids,
    pulls,
    laid,
    params,
    adam_m,
    adam_v,
    target,
    req,
    tile_list,
    tile_order,
    bg_ids,
    splats,
    wanted,
    sent,
    arrived,
    slot_grads,
    returned,
    backs,
    inner_held,
    outer_held,
    order,
    live,
    entries,
    wished_in,
    wished,
    alphas,
    split,
    sums,
    terms,
    carried,
    slopes,
    color_sums,
    entry_grads,
    before,
    after,
    left,
    right,
    product,
    owner_left,
    owner_right,
    owner_product,
    load_sem,
    local_sem,
    ask_send,
    ask_recv,
    send_sem,
    recv_sem,
    turn_send,
    turn_recv,
    inner_send,
    inner_recv,
    outer_send,
    outer_recv,
):
    g_local = params.shape[1]
    bins = g_local // 256
    slots = req.shape[1]
    cap = slots // NEAR
    tiles, list_len = tile_order.shape
    back_row = tiles * list_len // LANES
    me = lax.axis_index("dev")
    pairs = [
        (far_params, params),
        (far_req, req),
        (far_ids, bg_ids),
        (far_list, tile_list),
        (far_order, tile_order),
        (far_target, target),
        (far_m, adam_m),
        (far_v, adam_v),
    ]
    loads = [
        pltpu.make_async_copy(given, taken, load_sem.at[i]) for i, (given, taken) in enumerate(pairs)
    ]
    start(loads)
    greeted = greet(devices)

    finish(loads[:3])
    lay_out(params, laid)
    for block in range(g_local // 1024):
        project(center_y, laid, splats, block)
    greeted()
    asks = []
    for w in range(NEAR):
        columns = pl.ds(w * cap, cap)
        given, taken = req.at[:, columns], wanted.at[:, columns]
        asks.append(window_copy(devices, w, 1, given, taken, ask_send, ask_recv, local_sem.at[0]))
    start(asks)
    mine = bg_ids[...] - me * g_local
    own_back(splats, mine, backs.at[0])

    def spread_inner(stage):
        return spread(
            devices,
            INNER,
            inner_partner,
            backs.at[2 * stage],
            inner_held.at[stage],
            inner_send.at[stage],
            inner_recv.at[stage],
        )

    def spread_outer(stage):
        return spread(
            devices,
            devices // INNER,
            outer_partner,
            backs.at[2 * stage + 1],
            outer_held.at[stage],
            outer_send.at[stage],
            outer_recv.at[stage],
        )

    inner = spread_inner(0)
    start(inner)
    finish(loads[3:6])
    tiles_setup(
        tile_list, tile_order, tile_len, target, order, live, wished_in, wished, before, after
    )
    entries[...] = jnp.zeros_like(entries)

    finish(asks)
    supplies = {
        w: window_copy(
            devices, w, -1, sent.at[w], arrived.at[w], send_sem, recv_sem, local_sem.at[1]
        )
        for w in range(NEAR)
    }
    for i in reversed(range(NEAR // 2)):
        owner_gather(splats, wanted, i, sent)
        start([supplies[2 * i], supplies[2 * i + 1]])
    finish(inner)
    backs[1] = sum_of(backs[0], inner_held.at[0])
    outer = spread_outer(0)
    start(outer)
    for w in (0, 1, 2, 9, 8, 7, 6, 5, 4, 3):
        supplies[w].wait()
        tiles_gather(w, arrived, order, entries)
    entries[5, 0:back_row, :] = entries[5, 0:back_row, :] * live[...]
    finish(outer)
    summed = sum_of(backs[1], outer_held.at[0])
    for f in range(SPLAT):
        entries[f, back_row : back_row + 1, :] = summed[f : f + 1, :]

    tiles_render(
        tiles,
        tile_pos,
        entries,
        wished,
        alphas,
        split,
        sums,
        terms,
        carried,
        slopes,
        color_sums,
        entry_grads,
        before,
        after,
    )

    backs[2] = entry_grads[back_row]
    inner = spread_inner(1)
    start(inner)
    slot_columns(order, entry_grads, left, right)
    finish(inner)
    backs[3] = sum_of(backs[2], inner_held.at[1])
    outer = spread_outer(1)
    start(outer)
    scatter_product(left, right, product)
    slot_values(product, slot_grads)
    turns = {
        w: window_copy(
            devices, w, 1, slot_grads.at[w], returned.at[w], turn_send, turn_recv, local_sem.at[2]
        )
        for w in range(1, NEAR)
    }
    start([turns[w] for w in reversed(range(1, NEAR))])
    owner_columns(0, slot_grads, wanted, owner_left, owner_right, bins)
    finish(outer)
    summed = sum_of(backs[3], outer_held.at[1])
    scatter_columns(mine, summed[0:8], summed[8:9], owner_left, owner_right, slots, bins)
    owner_left[:, slots + LANES :] = jnp.zeros((owner_left.shape[0], LANES), BF16)
    owner_right[:, slots + LANES :] = jnp.zeros((256, LANES), BF16)
    for w in (1, 2, 3, 4, 9, 8, 7, 6, 5):
        turns[w].wait()
        owner_columns(w, returned, wanted, owner_left, owner_right, bins)
    scatter_product(owner_left, owner_right, owner_product)
    owner_values(owner_product, bins, pulls)
    finish(loads[6:])


def step(devices, center_y, *args):
    params, adam_m, adam_v, target, req_rows, tile_list, tile_len, tile_order, tile_pos, ids = args
    count, g_local = params.shape
    slots = req_rows.shape[1]
    tiles, list_len = tile_order.shape
    rows = tiles * list_len // LANES
    lasts = list_len // LANES + 1
    bins = g_local // 256
    depth = slots + 2 * LANES
    outers = devices // INNER
    far = pl.BlockSpec(memory_space=pltpu.HBM)
    near = pl.BlockSpec(memory_space=pltpu.VMEM)
    smem = pl.BlockSpec(memory_space=pltpu.SMEM)
    dma = pltpu.SemaphoreType.DMA
    shape = jax.ShapeDtypeStruct
    vmem = pltpu.VMEM
    return pl.pallas_call(
        functools.partial(step_kernel, devices, center_y),
        out_shape=(
            shape((SPLAT, 2, bins, LANES), F32),
            shape((8, g_local // 16, LANES), F32),
            shape(params.shape, F32),
            shape(params.shape, F32),
            shape(params.shape, F32),
        ),
        in_specs=[far] * 6 + [smem, far, smem, far],
        out_specs=(near,) * 5,
        scratch_shapes=[
            vmem(target.shape, F32),
            vmem(req_rows.shape, jnp.int32),
            vmem(tile_list.shape, jnp.int32),
            vmem(tile_order.shape, jnp.int32),
            vmem(ids.shape, jnp.int32),
            vmem((SPLAT, 2, g_local // 256, LANES), F32),
            vmem(req_rows.shape, jnp.int32),
            vmem((NEAR, 40, LANES), F32),
            vmem((NEAR, 40, LANES), F32),
            vmem((NEAR, 40, LANES), F32),
            vmem((NEAR, 40, LANES), F32),
            vmem((4, 16, LANES), F32),
            vmem((2, INNER, 16, LANES), F32),
            vmem((2, outers, 16, LANES), F32),
            vmem((rows, LANES), jnp.int32),
            vmem((rows, LANES), F32),
            vmem((SPLAT, rows + 8, LANES), F32),
            vmem((LANES, 256), F32),
            vmem((tiles * 3, 256, LANES), F32),
            vmem((lasts, 256, LANES), F32),
            vmem((lasts, 256, 256), BF16),
            vmem((lasts, 256, 256), F32),
            vmem((lasts, 256, LANES), F32),
            vmem((256, LANES), F32),
            vmem((3, 256, LANES), F32),
            vmem((3, lasts, 8, LANES), F32),
            vmem((rows + 1, 16, LANES), F32),
            vmem((256, 256), BF16),
            vmem((256, 256), BF16),
            vmem((scatter_rows(2 * NEAR), rows * LANES), BF16),
            vmem((256, rows * LANES), BF16),
            vmem((2, scatter_rows(2 * NEAR), LANES), F32),
            vmem((scatter_rows(bins), depth), BF16),
            vmem((256, depth), BF16),
            vmem((2, scatter_rows(bins), LANES), F32),
            dma((8,)),
            dma((3,)),
            dma((NEAR,)),
            dma((NEAR,)),
            dma((NEAR,)),
            dma((NEAR,)),
            dma((NEAR,)),
            dma((NEAR,)),
            dma((2, INNER)),
            dma((2, INNER)),
            dma((2, outers)),
            dma((2, outers)),
        ],
        compiler_params=pltpu.CompilerParams(
            collective_id=0, has_side_effects=True, vmem_limit_bytes=48 * 2**20
        ),
        name="step",
    )(*args)


def update_kernel(
    center_y,
    params,
    adam_m,
    adam_v,
    pulls,
    laid,
    new_params,
    new_m,
    new_v,
    grads,
    held_params,
    held_m,
    held_v,
    sems,
):
    count, g_local = params.shape
    copies = []
    for hb in range(g_local // 2048):
        for half in range(2):
            block = hb * 2 + half
            rows = [feature(laid, f, block) for f in range(10)]
            made, pull_back = jax.vjp(lambda given: geometry(given, center_y), rows)
            got = [pulls[f, half, hb * 8 : hb * 8 + 8, :] for f in range(SPLAT)]

            def put(f, value):
                first = (hb * 16 + half) * 8 + f % 8
                grads[f // 8, pl.ds(first, 8, stride=16), :] = value

            given = got[:5]
            for k in range(16):
                at = 11 + 3 * k
                total = got[6] * feature(laid, at, block)
                total = total + got[7] * feature(laid, at + 1, block)
                total = total + got[8] * feature(laid, at + 2, block)
                given.append(total)
                for c in range(3):
                    put(at + c, made[5 + k] * got[6 + c])
            for f, row in enumerate(pull_back(given)[0]):
                put(f, row)
            put(10, got[5] * (1.0 - jax.nn.sigmoid(feature(laid, 10, block))))

        @pl.loop(0, 16)
        def _(chunk):
            c = hb * 16 + chunk
            columns = pl.ds(pl.multiple_of(c * LANES, LANES), LANES)
            first = pl.multiple_of(c * 8, 8)
            for group in range(-(-count // 8)):
                size = min(8, count - group * 8)
                spot = slice(group * 8, group * 8 + size)
                slope = grads[group, pl.ds(first, size), :]
                moment = 0.9 * adam_m[spot, columns] + 0.1 * slope
                power = 0.999 * adam_v[spot, columns] + 0.001 * slope * slope
                change = moment / BIAS_ONE / (jnp.sqrt(power / BIAS_TWO) + 1e-08)
                held_params[spot, columns] = params[spot, columns] - 0.05 * change
                held_m[spot, columns] = moment
                held_v[spot, columns] = power

        columns = pl.ds(hb * 2048, 2048)
        for i, (held, out) in enumerate(
            ((held_params, new_params), (held_m, new_m), (held_v, new_v))
        ):
            copies.append(
                pltpu.make_async_copy(held.at[:, columns], out.at[:, columns], sems.at[hb * 3 + i])
            )
        start(copies[-3:])
    finish(copies)


def update(params, adam_m, adam_v, pulls, laid, center_y):
    count, g_local = params.shape
    vmem = pl.BlockSpec(memory_space=pltpu.VMEM)
    far = pl.BlockSpec(memory_space=pl.ANY)
    shape = jax.ShapeDtypeStruct(params.shape, F32)
    return pl.pallas_call(
        functools.partial(update_kernel, center_y),
        out_shape=(shape, shape, shape),
        in_specs=[vmem] * 5,
        out_specs=(far, far, far),
        scratch_shapes=[
            pltpu.VMEM((8, g_local // 16, LANES), F32),
            pltpu.VMEM((count, g_local), F32),
            pltpu.VMEM((count, g_local), F32),
            pltpu.VMEM((count, g_local), F32),
            pltpu.SemaphoreType.DMA((3 * (g_local // 2048),)),
        ],
        compiler_params=pltpu.CompilerParams(vmem_limit_bytes=48 * 2**20),
        name="update",
    )(params, adam_m, adam_v, pulls, laid)


def per_device(
    devices,
    params,
    adam_m,
    adam_v,
    target,
    req_rows,
    tile_list,
    tile_len,
    tile_order,
    tile_pos,
    bg_ids,
):
    center_y = 8.0 * (tile_order.shape[0] * devices // TILES_X)
    pulls, laid, near_params, near_m, near_v = step(
        devices,
        center_y,
        params,
        adam_m,
        adam_v,
        target,
        req_rows,
        tile_list,
        tile_len,
        tile_order,
        tile_pos,
        bg_ids.reshape(1, LANES),
    )
    return update(near_params, near_m, near_v, pulls, laid, center_y)


def solution(mesh):
    return jax.shard_map(
        functools.partial(per_device, mesh.shape["dev"]),
        mesh=mesh,
        in_specs=(
            P(None, "dev"),
            P(None, "dev"),
            P(None, "dev"),
            P(None, "dev"),
            P("dev", None),
            P("dev", None),
            P("dev"),
            P("dev", None),
            P("dev"),
            P(),
        ),
        out_specs=(P(None, "dev"), P(None, "dev"), P(None, "dev")),
        check_vma=False,
    )
```

```python
import functools

import jax
import jax.numpy as jnp
from jax import lax
from jax.experimental import pallas as pl
from jax.experimental.pallas import tpu as pltpu
from jax.sharding import PartitionSpec as P

TILES_X = 32
NEAR = 10
FOCAL = 512.0
BIAS_ONE = 1.0 - 0.9**10
BIAS_TWO = 1.0 - 0.999**10
MESH = pl.DeviceIdType.MESH
F32 = jnp.float32
BF16 = jnp.bfloat16
LANES = 128
INNER = 16
SPLAT = 9


def harmonics(dir_x, dir_y, dir_z):
    sq_x = dir_x * dir_x
    sq_y = dir_y * dir_y
    sq_z = dir_z * dir_z
    return [
        0.28209479177387814 + 0.0 * dir_x,
        -0.4886025119029199 * dir_y,
        0.4886025119029199 * dir_z,
        -0.4886025119029199 * dir_x,
        1.0925484305920792 * dir_x * dir_y,
        -1.0925484305920792 * dir_y * dir_z,
        0.31539156525252005 * (2.0 * sq_z - sq_x - sq_y),
        -1.0925484305920792 * dir_x * dir_z,
        0.5462742152960396 * (sq_x - sq_y),
        -0.5900435899266435 * dir_y * (3.0 * sq_x - sq_y),
        2.890611442640554 * dir_x * dir_y * dir_z,
        -0.4570457994644658 * dir_y * (4.0 * sq_z - sq_x - sq_y),
        0.3731763325901154 * dir_z * (2.0 * sq_z - 3.0 * sq_x - 3.0 * sq_y),
        -0.4570457994644658 * dir_x * (4.0 * sq_z - sq_x - sq_y),
        1.445305721320277 * dir_z * (sq_x - sq_y),
        -0.5900435899266435 * dir_x * (sq_x - 3.0 * sq_y),
    ]


def geometry(rows, center_y):
    pos_x, pos_y, depth = (rows[0], rows[1], rows[2])
    stretches = (jnp.exp(rows[3]), jnp.exp(rows[4]), jnp.exp(rows[5]))
    quat_norm = jnp.sqrt(
        rows[6] * rows[6] + rows[7] * rows[7] + rows[8] * rows[8] + rows[9] * rows[9]
    )
    inv_norm = 1.0 / quat_norm
    quat_w = rows[6] * inv_norm
    quat_x = rows[7] * inv_norm
    quat_y = rows[8] * inv_norm
    quat_z = rows[9] * inv_norm
    rotation = (
        (
            1.0 - 2.0 * (quat_y * quat_y + quat_z * quat_z),
            2.0 * (quat_x * quat_y - quat_w * quat_z),
            2.0 * (quat_x * quat_z + quat_w * quat_y),
        ),
        (
            2.0 * (quat_x * quat_y + quat_w * quat_z),
            1.0 - 2.0 * (quat_x * quat_x + quat_z * quat_z),
            2.0 * (quat_y * quat_z - quat_w * quat_x),
        ),
        (
            2.0 * (quat_x * quat_z - quat_w * quat_y),
            2.0 * (quat_y * quat_z + quat_w * quat_x),
            1.0 - 2.0 * (quat_x * quat_x + quat_y * quat_y),
        ),
    )
    inv_depth = 1.0 / depth
    focal_z = FOCAL * inv_depth
    slope_x = pos_x * inv_depth
    slope_y = pos_y * inv_depth
    cov_a = 0.3
    cov_b = 0.0
    cov_c = 0.3
    for column in range(3):
        axis_x = rotation[0][column] * stretches[column]
        axis_y = rotation[1][column] * stretches[column]
        axis_z = rotation[2][column] * stretches[column]
        image_u = focal_z * (axis_x - slope_x * axis_z)
        image_v = focal_z * (axis_y - slope_y * axis_z)
        cov_a = cov_a + image_u * image_u
        cov_b = cov_b + image_u * image_v
        cov_c = cov_c + image_v * image_v
    inv_determ = 1.0 / (cov_a * cov_c - cov_b * cov_b)
    center_u = FOCAL * slope_x + 8.0 * TILES_X
    center_v = FOCAL * slope_y + center_y
    inv_distance = 1.0 / jnp.sqrt(pos_x * pos_x + pos_y * pos_y + depth * depth)
    basis = harmonics(pos_x * inv_distance, pos_y * inv_distance, depth * inv_distance)
    conic = [cov_c * inv_determ, -cov_b * inv_determ, cov_a * inv_determ]
    return [center_u, center_v] + conic + basis


def lane_gather(source, index):
    numbers = lax.GatherDimensionNumbers(
        offset_dims=(),
        collapsed_slice_dims=(1,),
        start_index_map=(1,),
        operand_batching_dims=(0,),
        start_indices_batching_dims=(0,),
    )
    return lax.gather(
        source,
        index[..., None],
        numbers,
        (1, 1),
        mode=lax.GatherScatterMode.PROMISE_IN_BOUNDS,
    )


def wide(row, rows=8):
    return jnp.broadcast_to(row, (rows, row.shape[-1]))


def pieces_of(value):
    first = value.astype(BF16)
    return first, (value - first.astype(F32)).astype(BF16)


def offsets_of(devices):
    lines = [0, 1, -1, 4, -4]
    return [(lines[w % 5] + w // 5 * (devices // 2)) % devices for w in range(NEAR)]


def window_copy(devices, w, direction, given, taken, send_sem, recv_sem, local_sem):
    offset = offsets_of(devices)[w]
    if offset == 0:
        return pltpu.make_async_copy(given, taken, local_sem)
    ahead = (offset * direction) % devices
    return pltpu.make_async_remote_copy(
        src_ref=given,
        dst_ref=taken,
        send_sem=send_sem.at[w],
        recv_sem=recv_sem.at[w],
        device_id=(lax.rem(lax.axis_index("dev") + ahead, devices),),
        device_id_type=MESH,
    )


def inner_partner(devices, me, k):
    return me // INNER * INNER + lax.rem(lax.rem(me, INNER) + k, INNER)


def outer_partner(devices, me, k):
    return lax.rem(me + INNER * k, devices)


def spread(devices, count, partner, given, taken, send_sem, recv_sem):
    return [
        pltpu.make_async_remote_copy(
            src_ref=given,
            dst_ref=taken.at[k],
            send_sem=send_sem.at[k],
            recv_sem=recv_sem.at[k],
            device_id=(partner(devices, lax.axis_index("dev"), k),),
            device_id_type=MESH,
        )
        for k in range(1, count)
    ]


def greet(devices):
    me = lax.axis_index("dev")
    partners = [lax.rem(me + offset, devices) for offset in offsets_of(devices) if offset]
    partners += [inner_partner(devices, me, k) for k in range(1, INNER)]
    partners += [outer_partner(devices, me, k) for k in range(1, devices // INNER)]
    barrier = pltpu.get_barrier_semaphore()
    for partner in partners:
        pl.semaphore_signal(barrier, inc=1, device_id=(partner,), device_id_type=MESH)
    return lambda: pl.semaphore_wait(barrier, len(partners))


def start(copies):
    for copy in copies:
        copy.start()


def finish(copies):
    for copy in copies:
        copy.wait()


def receive(copies):
    for copy in copies:
        if copy.is_remote:
            copy.wait_recv()
        else:
            copy.wait()


def sent_off(copies):
    for copy in copies:
        if copy.is_remote:
            copy.wait_send()


def sum_of(first, taken):
    total = first
    for k in range(1, taken.shape[0]):
        total = total + taken[k]
    return total


def feature(laid, f, block):
    first = (block // 2 * 16 + block % 2) * 8 + f % 8
    return laid[f // 8, pl.ds(first, 8, stride=16), :]


def lay_out(params, laid):
    count, g_local = params.shape

    @pl.loop(0, g_local // LANES)
    def _(c):
        columns = pl.ds(pl.multiple_of(c * LANES, LANES), LANES)
        first = pl.multiple_of(c * 8, 8)
        for group in range(count // 8):
            laid[group, pl.ds(first, 8), :] = params[group * 8 : group * 8 + 8, columns]
        over = count % 8
        laid[count // 8, pl.ds(first, over), :] = params[count - over :, columns]


def project(center_y, laid, splats, block):
    rows = [feature(laid, f, block) for f in range(11)]
    made = geometry(rows, center_y)
    opacity = jax.nn.sigmoid(rows[10])
    colors = []
    for c in range(3):
        total = made[5] * feature(laid, 11 + c, block)
        for k in range(1, 16):
            total = total + made[5 + k] * feature(laid, 11 + 3 * k + c, block)
        colors.append(total + 0.5)
    for f, row in enumerate(made[:5] + [opacity] + colors):
        splats[f, block % 2, block // 2 * 8 : block // 2 * 8 + 8, :] = row


def own_back(splats, mine, back):
    local = wide(mine)
    high = jnp.right_shift(local, 7)
    low = jnp.bitwise_and(local, LANES - 1)
    eight = lax.broadcasted_iota(jnp.int32, (8, LANES), 0)
    back[...] = jnp.zeros_like(back)
    for f in range(SPLAT):
        total = jnp.zeros((8, LANES), F32)
        for block in range(2 * splats.shape[2] // 8):
            hb, half = block // 2, block % 2
            found = lane_gather(splats[f, half, hb * 8 : hb * 8 + 8, :], low)
            total = jnp.where(high == hb * 16 + 2 * eight + half, found, total)
        back[f : f + 1, :] = jnp.sum(total, axis=0, keepdims=True)


def owner_gather(splats, wanted, i, sent):
    first = i * 8 * LANES
    rows = jnp.concatenate(
        [wanted[:, first + r * LANES : first + (r + 1) * LANES] for r in range(8)], axis=0
    )
    high = jnp.right_shift(rows, 7)
    low = jnp.bitwise_and(rows, LANES - 1)

    def pick(step, totals):
        totals = list(totals)
        for k in range(4):
            for half in range(2):
                c = step * 4 + k
                here = high == 2 * c + half
                for f in range(SPLAT):
                    source = wide(splats[f, half, pl.ds(c, 1), :])
                    totals[f] = jnp.where(here, lane_gather(source, low), totals[f])
        return tuple(totals)

    none = tuple(jnp.zeros((8, LANES), F32) for _ in range(SPLAT))
    totals = lax.fori_loop(0, splats.shape[2] // 4, pick, none)
    for half in range(2):
        for f in range(SPLAT):
            sent[i * 2 + half, f * 4 : f * 4 + 4, :] = totals[f][half * 4 : half * 4 + 4, :]
        sent[i * 2 + half, 36:40, :] = jnp.zeros((4, LANES), F32)


def scatter_rows(bins):
    return 16 * (bins + -(-bins // 8))


def scatter_lanes(index, right, column):
    low = wide(jnp.bitwise_and(index, 255), 256)
    place = lax.broadcasted_iota(jnp.int32, (256, LANES), 0)
    right[:, pl.ds(column, LANES)] = jnp.where(place == low, 1.0, 0.0).astype(BF16)


def scatter_bins(index, eight, ninth, left, column, bins):
    high = wide(jnp.right_shift(index, 8))

    def put(at, here, value):
        first = value.astype(BF16).astype(F32)
        both = [jnp.where(here, first, 0.0), jnp.where(here, value - first, 0.0)]
        left[at : at + 16, pl.ds(column, LANES)] = jnp.concatenate(both, axis=0).astype(BF16)

    for h in range(bins):
        put(h * 16, high == h, eight)
    ninth = wide(ninth)
    for i in range(-(-bins // 8)):
        own = lax.broadcasted_iota(jnp.int32, (8, LANES), 0) + 8 * i
        put((bins + i) * 16, high == own, ninth)


def bin_values(product, half, h, bins):
    eight = product[half, h * 16 : h * 16 + 8, :] + product[half, h * 16 + 8 : h * 16 + 16, :]
    at = (bins + h // 8) * 16 + h % 8
    return eight, product[half, at : at + 1, :] + product[half, at + 8 : at + 9, :]


def scatter_product(left, right, product):
    depth = left.shape[1]
    step = 768 if depth % 768 == 0 else 1280
    product[...] = jnp.zeros_like(product)

    @pl.loop(0, depth // step)
    def _(i):
        columns = pl.ds(pl.multiple_of(i * step, LANES), step)
        made = lax.dot_general(
            left[:, columns],
            right[:, columns],
            (((1,), (1,)), ((), ())),
            preferred_element_type=F32,
        )
        product[0] += made[:, :LANES]
        product[1] += made[:, LANES:]


def tiles_setup(
    tile_list, tile_order, tile_len, target, order, live, wished_in, wished, before, after
):
    tiles, list_len = tile_order.shape
    groups = list_len // LANES

    eight = lax.broadcasted_iota(jnp.int32, (8, LANES), 0)
    lengths = jnp.zeros((8, LANES), jnp.int32)
    for t in range(tiles):
        lengths = jnp.where(lax.rem(eight, tiles) == t, tile_len[t], lengths)
    for pair in range(groups // 2):
        ranks = jnp.concatenate(
            [
                tile_order[:, (2 * pair) * LANES : (2 * pair + 1) * LANES],
                tile_order[:, (2 * pair + 1) * LANES : (2 * pair + 2) * LANES],
            ],
            axis=0,
        )
        high = jnp.right_shift(ranks, 7)
        low = jnp.bitwise_and(ranks, LANES - 1)
        named = jnp.zeros((8, LANES), jnp.int32)
        for c in range(groups):
            part = [
                tile_list[:, t * list_len + c * LANES : t * list_len + (c + 1) * LANES]
                for t in range(tiles)
            ]
            source = jnp.concatenate(part + part, axis=0)
            named = jnp.where(high == c, lane_gather(source, low), named)
        order[pair * 8 : pair * 8 + 8, :] = named
        live[pair * 8 : pair * 8 + 8, :] = jnp.where(ranks < lengths, 1.0, 0.0)

    wished_in[...] = jnp.zeros_like(wished_in)
    for t in range(tiles):
        wished_in[3 * t : 3 * t + 3, :] = target[:, t * 256 : (t + 1) * 256]
    columns = jnp.transpose(wished_in[...])
    for t in range(tiles):
        for c in range(3):
            one = columns[:, 3 * t + c : 3 * t + c + 1]
            wished[t * 3 + c] = jnp.broadcast_to(one, (256, LANES))

    row_at = jnp.bitwise_and(lax.broadcasted_iota(jnp.int32, (256, 256), 0), LANES - 1)
    col_at = lax.broadcasted_iota(jnp.int32, (256, 256), 1)
    before[...] = jnp.where((row_at < col_at) | (col_at >= LANES), 1.0, 0.0).astype(BF16)
    after[...] = jnp.where((row_at > col_at) | (col_at >= LANES), 1.0, 0.0).astype(BF16)


def tiles_gather(w, arrived, order, entries):
    @pl.loop(0, order.shape[0] // 8)
    def _(i):
        spots = pl.ds(pl.multiple_of(i * 8, 8), 8)
        slots = order[spots, :]
        high = jnp.right_shift(slots, 7)
        low = jnp.bitwise_and(slots, LANES - 1)
        totals = [entries[f, spots, :] for f in range(SPLAT)]
        for k in range(4):
            here = high == w * 4 + k
            for f in range(SPLAT):
                source = wide(arrived[w, f * 4 + k : f * 4 + k + 1, :])
                totals[f] = jnp.where(here, lane_gather(source, low), totals[f])
        for f in range(SPLAT):
            entries[f, spots, :] = totals[f]


def tiles_render(
    tiles,
    tile_pos,
    entries,
    wished,
    alphas,
    split,
    sums,
    terms,
    carried,
    slopes,
    color_sums,
    entry_grads,
    before,
    after,
):
    lasts = alphas.shape[0]
    groups = lasts - 1
    back_row = tiles * groups
    entry_grads[...] = jnp.zeros_like(entry_grads)

    def row_of(t, j):
        listed = j // 2 * 8 + lax.rem(j, 2) * 4 + t
        return jnp.where(j == groups, back_row, listed)

    def entry(f, row):
        return wide(entries[f, pl.ds(row, 1), :])

    across = (
        lax.broadcasted_iota(jnp.int32, (2, 8, LANES), 0) * 8
        + lax.broadcasted_iota(jnp.int32, (2, 8, LANES), 1)
    ).astype(F32) + 0.5

    @pl.loop(0, tiles)
    def _(t):
        place = tile_pos[t]
        corner_x = (lax.rem(place, TILES_X) * 16).astype(F32)
        corner_y = (place // TILES_X * 16).astype(F32)

        @pl.loop(0, lasts)
        def _(j):
            last = jnp.maximum(j - 1, 0)
            sums[last] = jnp.dot(split[last], before[...], preferred_element_type=F32)
            row = row_of(t, j)
            delta_x = (across + corner_x) - entry(0, row)[None]
            center_v = entry(1, row)
            flat = -0.5 * entry(2, row)[None] * delta_x * delta_x
            mixed = -entry(3, row)[None] * delta_x
            half_c = -0.5 * entry(4, row)
            opacity = entry(5, row)[None]
            for y in range(16):
                delta_y = (corner_y + (y + 0.5)) - center_v
                slope = half_c * delta_y
                power = (mixed + slope[None]) * delta_y[None] + flat
                alpha = opacity * jnp.exp(power)
                keep = jnp.log(1.0 - alpha)
                spot = slice(y * 16, y * 16 + 16)
                alphas[j, spot, :] = alpha.reshape(16, LANES)
                first, second = pieces_of(keep.reshape(16, LANES))
                split[j, spot, :LANES] = first
                split[j, spot, LANES:] = second

        sums[groups] = jnp.dot(split[groups], before[...], preferred_element_type=F32)

        @pl.loop(0, 8)
        def _(y):
            spot = pl.ds(pl.multiple_of(y * 32, 32), 32)
            gone = jnp.zeros((32, LANES), F32)
            seen = [jnp.zeros((4, 8, LANES), F32) for _ in range(3)]
            for j in range(lasts):
                row = row_of(t, j)
                transmit = jnp.exp(gone + sums[j, spot, :LANES])
                gone = gone + sums[j, spot, LANES:]
                weight = alphas[j, spot, :] * transmit
                terms[j, spot, :] = weight
                for c in range(3):
                    seen[c] = seen[c] + weight.reshape(4, 8, LANES) * entry(6 + c, row)[None]
            for c in range(3):
                slopes[c, spot, :] = seen[c].reshape(32, LANES)

        for c in range(3):
            color = jnp.sum(slopes[c], axis=1, keepdims=True)
            slopes[c] = 16.0 * (color - wished[t * 3 + c])

        @pl.loop(0, lasts)
        def _(j):
            last = jnp.maximum(j - 1, 0)
            sums[last] = jnp.dot(split[last], after[...], preferred_element_type=F32)
            row = row_of(t, j)
            colors = [entry(6 + c, row)[None] for c in range(3)]
            painted = [jnp.zeros((2, 8, LANES), F32) for _ in range(3)]
            for y in range(16):
                spot = slice(y * 16, y * 16 + 16)
                weight = terms[j, spot, :].reshape(2, 8, LANES)
                slope = [slopes[c, spot, :].reshape(2, 8, LANES) for c in range(3)]
                pull = slope[0] * colors[0] + slope[1] * colors[1] + slope[2] * colors[2]
                term = (pull * weight).reshape(16, LANES)
                terms[j, spot, :] = term
                first, second = pieces_of(term)
                split[j, spot, :LANES] = first
                split[j, spot, LANES:] = second
                for c in range(3):
                    painted[c] = painted[c] + slope[c] * weight
            for c in range(3):
                color_sums[c, j] = painted[c][0] + painted[c][1]

        sums[groups] = jnp.dot(split[groups], after[...], preferred_element_type=F32)

        carried[...] = jnp.zeros_like(carried)

        @pl.loop(0, lasts)
        def _(back_j):
            j = groups - back_j
            row = row_of(t, j)
            delta_x = (across + corner_x) - entry(0, row)[None]
            center_v = entry(1, row)
            zero = jnp.zeros((2, 8, LANES), F32)
            sum_none, sum_y, sum_yy = zero, zero, zero
            for y in range(16):
                spot = slice(y * 16, y * 16 + 16)
                behind = carried[spot, :] + sums[j, spot, :LANES]
                carried[spot, :] += sums[j, spot, LANES:]
                alpha = alphas[j, spot, :]
                share = alpha / (1.0 - alpha)
                pull = (terms[j, spot, :] - behind * share).reshape(2, 8, LANES)
                delta_y = ((corner_y + (y + 0.5)) - center_v)[None]
                sum_none = sum_none + pull
                moved = pull * delta_y
                sum_y = sum_y + moved
                sum_yy = sum_yy + moved * delta_y

            def fold(value):
                return jnp.sum(value[0] + value[1], axis=0, keepdims=True)

            first_x = sum_none * delta_x
            in_none = fold(sum_none)
            in_x = fold(first_x)
            in_xx = fold(first_x * delta_x)
            in_xy = fold(sum_y * delta_x)
            in_y = fold(sum_y)
            in_yy = fold(sum_yy)
            con_a, con_b, con_c = (entries[f, pl.ds(row, 1), :] for f in (2, 3, 4))
            made = [
                con_a * in_x + con_b * in_y,
                con_c * in_y + con_b * in_x,
                -0.5 * in_xx,
                -in_xy,
                -0.5 * in_yy,
                in_none,
            ]
            made += [jnp.sum(color_sums[c, j], axis=0, keepdims=True) for c in range(3)]
            for f in range(SPLAT):
                entry_grads[row, f : f + 1, :] += made[f]


def slot_columns(order, entry_grads, left, right):
    @pl.loop(0, order.shape[0])
    def _(r):
        column = pl.multiple_of(r * LANES, LANES)
        values = entry_grads[r]
        index = order[pl.ds(r, 1), :]
        scatter_lanes(index, right, column)
        for half in range(2):
            own = index - half * NEAR * 256
            scatter_bins(own, values[0:8], values[8:9], left.at[half], column, NEAR)


def slot_values(product, part, slot_grads):
    for h in range(NEAR):
        w = part * 5 + h // 2
        for half in range(2):
            eight, ninth = bin_values(product, half, h, NEAR)
            for f in range(SPLAT):
                at = f * 4 + (h % 2) * 2 + half
                slot_grads[w, at : at + 1, :] = eight[f : f + 1] if f < 8 else ninth
        slot_grads[w, 36:40, :] = jnp.zeros((4, LANES), F32)


def owner_columns(w, source, wanted, left, right, bins):
    for k in range(4):
        column = (w * 4 + k) * LANES
        eight = source[w, pl.ds(k, 8, stride=4), :]
        ninth = source[w, 32 + k : 33 + k, :]
        index = wanted[:, column : column + LANES]
        scatter_lanes(index, right, column)
        scatter_bins(index, eight, ninth, left, column, bins)


def owner_values(product, bins, pulls):
    for hb in range(bins // 8):
        for half in range(2):
            spot = slice(hb * 8, hb * 8 + 8)
            for f in range(8):
                first = product[half, pl.ds(hb * 128 + f, 8, stride=16), :]
                second = product[half, pl.ds(hb * 128 + 8 + f, 8, stride=16), :]
                pulls[f, half, spot, :] = first + second
            at = (bins + hb) * 16
            ninth = product[half, at : at + 8, :] + product[half, at + 8 : at + 16, :]
            pulls[8, half, spot, :] = ninth


def step_kernel(
    devices,
    center_y,
    far_params,
    far_target,
    far_req,
    far_list,
    tile_len,
    far_order,
    tile_pos,
    far_ids,
    pulls,
    laid,
    params,
    target,
    req,
    tile_list,
    tile_order,
    bg_ids,
    splats,
    wanted,
    sent,
    arrived,
    slot_grads,
    returned,
    backs,
    inner_held,
    outer_held,
    order,
    live,
    entries,
    wished_in,
    wished,
    alphas,
    split,
    sums,
    terms,
    carried,
    slopes,
    color_sums,
    entry_grads,
    before,
    after,
    left,
    right,
    product,
    owner_left,
    owner_right,
    owner_product,
    load_sem,
    local_sem,
    ask_send,
    ask_recv,
    send_sem,
    recv_sem,
    turn_send,
    turn_recv,
    inner_send,
    inner_recv,
    outer_send,
    outer_recv,
):
    g_local = params.shape[1]
    bins = g_local // 256
    slots = req.shape[1]
    cap = slots // NEAR
    tiles, list_len = tile_order.shape
    back_row = tiles * list_len // LANES
    me = lax.axis_index("dev")
    pairs = [
        (far_params, params),
        (far_req, req),
        (far_ids, bg_ids),
        (far_list, tile_list),
        (far_order, tile_order),
        (far_target, target),
    ]
    loads = [
        pltpu.make_async_copy(given, taken, load_sem.at[i]) for i, (given, taken) in enumerate(pairs)
    ]
    start(loads)
    greeted = greet(devices)

    finish(loads[:3])
    lay_out(params, laid)
    for block in range(g_local // 1024):
        project(center_y, laid, splats, block)
    greeted()
    asks = []
    for w in range(NEAR):
        columns = pl.ds(w * cap, cap)
        given, taken = req.at[:, columns], wanted.at[:, columns]
        asks.append(window_copy(devices, w, 1, given, taken, ask_send, ask_recv, local_sem.at[0]))
    start(asks)
    mine = bg_ids[...] - me * g_local
    own_back(splats, mine, backs.at[0])

    def spread_inner(stage):
        return spread(
            devices,
            INNER,
            inner_partner,
            backs.at[2 * stage],
            inner_held.at[stage],
            inner_send.at[stage],
            inner_recv.at[stage],
        )

    def spread_outer(stage):
        return spread(
            devices,
            devices // INNER,
            outer_partner,
            backs.at[2 * stage + 1],
            outer_held.at[stage],
            outer_send.at[stage],
            outer_recv.at[stage],
        )

    inner = spread_inner(0)
    start(inner)
    finish(loads[3:6])
    tiles_setup(
        tile_list, tile_order, tile_len, target, order, live, wished_in, wished, before, after
    )
    entries[...] = jnp.zeros_like(entries)

    receive(asks)
    supplies = {
        w: window_copy(
            devices, w, -1, sent.at[w], arrived.at[w], send_sem, recv_sem, local_sem.at[1]
        )
        for w in range(NEAR)
    }
    for i in reversed(range(NEAR // 2)):
        owner_gather(splats, wanted, i, sent)
        start([supplies[2 * i], supplies[2 * i + 1]])
    receive(inner)
    backs[1] = sum_of(backs[0], inner_held.at[0])
    outer = spread_outer(0)
    start(outer)
    for w in (0, 1, 2, 9, 8, 7, 6, 5, 4, 3):
        receive([supplies[w]])
        tiles_gather(w, arrived, order, entries)
    entries[5, 0:back_row, :] = entries[5, 0:back_row, :] * live[...]
    receive(outer)
    summed = sum_of(backs[1], outer_held.at[0])
    for f in range(SPLAT):
        entries[f, back_row : back_row + 1, :] = summed[f : f + 1, :]

    tiles_render(
        tiles,
        tile_pos,
        entries,
        wished,
        alphas,
        split,
        sums,
        terms,
        carried,
        slopes,
        color_sums,
        entry_grads,
        before,
        after,
    )

    backs[2] = entry_grads[back_row]
    started = asks + list(supplies.values()) + inner + outer
    inner = spread_inner(1)
    start(inner)
    slot_columns(order, entry_grads, left, right)
    receive(inner)
    backs[3] = sum_of(backs[2], inner_held.at[1])
    outer = spread_outer(1)
    start(outer)
    turns = {
        w: window_copy(
            devices, w, 1, slot_grads.at[w], returned.at[w], turn_send, turn_recv, local_sem.at[2]
        )
        for w in range(1, NEAR)
    }
    for half in reversed(range(2)):
        scatter_product(left.at[half], right, product)
        slot_values(product, half, slot_grads)
        start([turns[w] for w in reversed(range(max(1, half * 5), half * 5 + 5))])
    owner_columns(0, slot_grads, wanted, owner_left, owner_right, bins)
    receive(outer)
    summed = sum_of(backs[3], outer_held.at[1])
    scatter_lanes(mine, owner_right, slots)
    scatter_bins(mine, summed[0:8], summed[8:9], owner_left, slots, bins)
    owner_left[:, slots + LANES :] = jnp.zeros((owner_left.shape[0], LANES), BF16)
    owner_right[:, slots + LANES :] = jnp.zeros((256, LANES), BF16)
    for w in (1, 2, 3, 4, 9, 8, 7, 6, 5):
        receive([turns[w]])
        owner_columns(w, returned, wanted, owner_left, owner_right, bins)
    scatter_product(owner_left, owner_right, owner_product)
    owner_values(owner_product, bins, pulls)
    sent_off(started + inner + outer + list(turns.values()))


def step(devices, center_y, *args):
    params, target, req_rows, tile_list, tile_len, tile_order, tile_pos, ids = args
    count, g_local = params.shape
    slots = req_rows.shape[1]
    tiles, list_len = tile_order.shape
    rows = tiles * list_len // LANES
    lasts = list_len // LANES + 1
    bins = g_local // 256
    depth = slots + 2 * LANES
    outers = devices // INNER
    far = pl.BlockSpec(memory_space=pltpu.HBM)
    near = pl.BlockSpec(memory_space=pltpu.VMEM)
    smem = pl.BlockSpec(memory_space=pltpu.SMEM)
    dma = pltpu.SemaphoreType.DMA
    shape = jax.ShapeDtypeStruct
    vmem = pltpu.VMEM
    return pl.pallas_call(
        functools.partial(step_kernel, devices, center_y),
        out_shape=shape((SPLAT, 2, bins, LANES), F32),
        in_specs=[far] * 4 + [smem, far, smem, far],
        out_specs=near,
        scratch_shapes=[
            vmem((8, g_local // 16, LANES), F32),
            vmem(params.shape, F32),
            vmem(target.shape, F32),
            vmem(req_rows.shape, jnp.int32),
            vmem(tile_list.shape, jnp.int32),
            vmem(tile_order.shape, jnp.int32),
            vmem(ids.shape, jnp.int32),
            vmem((SPLAT, 2, g_local // 256, LANES), F32),
            vmem(req_rows.shape, jnp.int32),
            vmem((NEAR, 40, LANES), F32),
            vmem((NEAR, 40, LANES), F32),
            vmem((NEAR, 40, LANES), F32),
            vmem((NEAR, 40, LANES), F32),
            vmem((4, 16, LANES), F32),
            vmem((2, INNER, 16, LANES), F32),
            vmem((2, outers, 16, LANES), F32),
            vmem((rows, LANES), jnp.int32),
            vmem((rows, LANES), F32),
            vmem((SPLAT, rows + 8, LANES), F32),
            vmem((LANES, 256), F32),
            vmem((tiles * 3, 256, LANES), F32),
            vmem((lasts, 256, LANES), F32),
            vmem((lasts, 256, 256), BF16),
            vmem((lasts, 256, 256), F32),
            vmem((lasts, 256, LANES), F32),
            vmem((256, LANES), F32),
            vmem((3, 256, LANES), F32),
            vmem((3, lasts, 8, LANES), F32),
            vmem((rows + 1, 16, LANES), F32),
            vmem((256, 256), BF16),
            vmem((256, 256), BF16),
            vmem((2, scatter_rows(NEAR), rows * LANES), BF16),
            vmem((256, rows * LANES), BF16),
            vmem((2, scatter_rows(NEAR), LANES), F32),
            vmem((scatter_rows(bins), depth), BF16),
            vmem((256, depth), BF16),
            vmem((2, scatter_rows(bins), LANES), F32),
            dma((6,)),
            dma((3,)),
            dma((NEAR,)),
            dma((NEAR,)),
            dma((NEAR,)),
            dma((NEAR,)),
            dma((NEAR,)),
            dma((NEAR,)),
            dma((2, INNER)),
            dma((2, INNER)),
            dma((2, outers)),
            dma((2, outers)),
        ],
        compiler_params=pltpu.CompilerParams(
            collective_id=0, has_side_effects=True, vmem_limit_bytes=60 * 2**20
        ),
        name="step",
    )(*args)


def update_kernel(
    center_y,
    far_params,
    far_m,
    far_v,
    far_pulls,
    new_params,
    new_m,
    new_v,
    params,
    adam_m,
    adam_v,
    pulls,
    laid,
    grads,
    held_params,
    held_m,
    held_v,
    load_sem,
    sems,
):
    count, g_local = params.shape
    pairs = [(far_params, params), (far_pulls, pulls), (far_m, adam_m), (far_v, adam_v)]
    loads = [
        pltpu.make_async_copy(given, taken, load_sem.at[i]) for i, (given, taken) in enumerate(pairs)
    ]
    start(loads)
    copies = []
    finish(loads[:2])
    lay_out(params, laid)
    for hb in range(g_local // 2048):
        for half in range(2):
            block = hb * 2 + half
            rows = [feature(laid, f, block) for f in range(10)]
            made, pull_back = jax.vjp(lambda given: geometry(given, center_y), rows)
            got = [pulls[f, half, hb * 8 : hb * 8 + 8, :] for f in range(SPLAT)]

            def put(f, value):
                first = (hb * 16 + half) * 8 + f % 8
                grads[f // 8, pl.ds(first, 8, stride=16), :] = value

            given = got[:5]
            for k in range(16):
                at = 11 + 3 * k
                total = got[6] * feature(laid, at, block)
                total = total + got[7] * feature(laid, at + 1, block)
                total = total + got[8] * feature(laid, at + 2, block)
                given.append(total)
                for c in range(3):
                    put(at + c, made[5 + k] * got[6 + c])
            for f, row in enumerate(pull_back(given)[0]):
                put(f, row)
            put(10, got[5] * (1.0 - jax.nn.sigmoid(feature(laid, 10, block))))

        if hb == 0:
            finish(loads[2:])

        @pl.loop(0, 16)
        def _(chunk):
            c = hb * 16 + chunk
            columns = pl.ds(pl.multiple_of(c * LANES, LANES), LANES)
            first = pl.multiple_of(c * 8, 8)
            for group in range(-(-count // 8)):
                size = min(8, count - group * 8)
                spot = slice(group * 8, group * 8 + size)
                slope = grads[group, pl.ds(first, size), :]
                moment = 0.9 * adam_m[spot, columns] + 0.1 * slope
                power = 0.999 * adam_v[spot, columns] + 0.001 * slope * slope
                change = moment / BIAS_ONE / (jnp.sqrt(power / BIAS_TWO) + 1e-08)
                held_params[spot, columns] = params[spot, columns] - 0.05 * change
                held_m[spot, columns] = moment
                held_v[spot, columns] = power

        columns = pl.ds(hb * 2048, 2048)
        for i, (held, out) in enumerate(
            ((held_params, new_params), (held_m, new_m), (held_v, new_v))
        ):
            copies.append(
                pltpu.make_async_copy(held.at[:, columns], out.at[:, columns], sems.at[hb * 3 + i])
            )
        start(copies[-3:])
    finish(copies)


def update(params, adam_m, adam_v, pulls, center_y):
    count, g_local = params.shape
    far = pl.BlockSpec(memory_space=pltpu.HBM)
    shape = jax.ShapeDtypeStruct(params.shape, F32)
    return pl.pallas_call(
        functools.partial(update_kernel, center_y),
        out_shape=(shape, shape, shape),
        in_specs=[far] * 4,
        out_specs=(far, far, far),
        scratch_shapes=[
            pltpu.VMEM((count, g_local), F32),
            pltpu.VMEM((count, g_local), F32),
            pltpu.VMEM((count, g_local), F32),
            pltpu.VMEM(pulls.shape, F32),
            pltpu.VMEM((8, g_local // 16, LANES), F32),
            pltpu.VMEM((8, g_local // 16, LANES), F32),
            pltpu.VMEM((count, g_local), F32),
            pltpu.VMEM((count, g_local), F32),
            pltpu.VMEM((count, g_local), F32),
            pltpu.SemaphoreType.DMA((4,)),
            pltpu.SemaphoreType.DMA((3 * (g_local // 2048),)),
        ],
        compiler_params=pltpu.CompilerParams(vmem_limit_bytes=60 * 2**20),
        name="update",
    )(params, adam_m, adam_v, pulls)


def per_device(
    devices,
    params,
    adam_m,
    adam_v,
    target,
    req_rows,
    tile_list,
    tile_len,
    tile_order,
    tile_pos,
    bg_ids,
):
    center_y = 8.0 * (tile_order.shape[0] * devices // TILES_X)
    pulls = step(
        devices,
        center_y,
        params,
        target,
        req_rows,
        tile_list,
        tile_len,
        tile_order,
        tile_pos,
        bg_ids.reshape(1, LANES),
    )
    return update(params, adam_m, adam_v, pulls, center_y)


def solution(mesh):
    return jax.shard_map(
        functools.partial(per_device, mesh.shape["dev"]),
        mesh=mesh,
        in_specs=(
            P(None, "dev"),
            P(None, "dev"),
            P(None, "dev"),
            P(None, "dev"),
            P("dev", None),
            P("dev", None),
            P("dev"),
            P("dev", None),
            P("dev"),
            P(),
        ),
        out_specs=(P(None, "dev"), P(None, "dev"), P(None, "dev")),
        check_vma=False,
    )
```

```python
import functools

import jax
import jax.numpy as jnp
from jax import lax
from jax.experimental import pallas as pl
from jax.experimental.pallas import tpu as pltpu
from jax.sharding import PartitionSpec as P

TILES_X = 32
NEAR = 10
FOCAL = 512.0
BIAS_ONE = 1.0 - 0.9**10
BIAS_TWO = 1.0 - 0.999**10
MESH = pl.DeviceIdType.MESH
F32 = jnp.float32
BF16 = jnp.bfloat16
LANES = 128
INNER = 16
SPLAT = 9


def harmonics(dir_x, dir_y, dir_z):
    sq_x = dir_x * dir_x
    sq_y = dir_y * dir_y
    sq_z = dir_z * dir_z
    return [
        0.28209479177387814 + 0.0 * dir_x,
        -0.4886025119029199 * dir_y,
        0.4886025119029199 * dir_z,
        -0.4886025119029199 * dir_x,
        1.0925484305920792 * dir_x * dir_y,
        -1.0925484305920792 * dir_y * dir_z,
        0.31539156525252005 * (2.0 * sq_z - sq_x - sq_y),
        -1.0925484305920792 * dir_x * dir_z,
        0.5462742152960396 * (sq_x - sq_y),
        -0.5900435899266435 * dir_y * (3.0 * sq_x - sq_y),
        2.890611442640554 * dir_x * dir_y * dir_z,
        -0.4570457994644658 * dir_y * (4.0 * sq_z - sq_x - sq_y),
        0.3731763325901154 * dir_z * (2.0 * sq_z - 3.0 * sq_x - 3.0 * sq_y),
        -0.4570457994644658 * dir_x * (4.0 * sq_z - sq_x - sq_y),
        1.445305721320277 * dir_z * (sq_x - sq_y),
        -0.5900435899266435 * dir_x * (sq_x - 3.0 * sq_y),
    ]


def geometry(rows, center_y):
    pos_x, pos_y, depth = (rows[0], rows[1], rows[2])
    stretches = (jnp.exp(rows[3]), jnp.exp(rows[4]), jnp.exp(rows[5]))
    quat_norm = jnp.sqrt(
        rows[6] * rows[6] + rows[7] * rows[7] + rows[8] * rows[8] + rows[9] * rows[9]
    )
    inv_norm = 1.0 / quat_norm
    quat_w = rows[6] * inv_norm
    quat_x = rows[7] * inv_norm
    quat_y = rows[8] * inv_norm
    quat_z = rows[9] * inv_norm
    rotation = (
        (
            1.0 - 2.0 * (quat_y * quat_y + quat_z * quat_z),
            2.0 * (quat_x * quat_y - quat_w * quat_z),
            2.0 * (quat_x * quat_z + quat_w * quat_y),
        ),
        (
            2.0 * (quat_x * quat_y + quat_w * quat_z),
            1.0 - 2.0 * (quat_x * quat_x + quat_z * quat_z),
            2.0 * (quat_y * quat_z - quat_w * quat_x),
        ),
        (
            2.0 * (quat_x * quat_z - quat_w * quat_y),
            2.0 * (quat_y * quat_z + quat_w * quat_x),
            1.0 - 2.0 * (quat_x * quat_x + quat_y * quat_y),
        ),
    )
    inv_depth = 1.0 / depth
    focal_z = FOCAL * inv_depth
    slope_x = pos_x * inv_depth
    slope_y = pos_y * inv_depth
    cov_a = 0.3
    cov_b = 0.0
    cov_c = 0.3
    for column in range(3):
        axis_x = rotation[0][column] * stretches[column]
        axis_y = rotation[1][column] * stretches[column]
        axis_z = rotation[2][column] * stretches[column]
        image_u = focal_z * (axis_x - slope_x * axis_z)
        image_v = focal_z * (axis_y - slope_y * axis_z)
        cov_a = cov_a + image_u * image_u
        cov_b = cov_b + image_u * image_v
        cov_c = cov_c + image_v * image_v
    inv_determ = 1.0 / (cov_a * cov_c - cov_b * cov_b)
    center_u = FOCAL * slope_x + 8.0 * TILES_X
    center_v = FOCAL * slope_y + center_y
    inv_distance = 1.0 / jnp.sqrt(pos_x * pos_x + pos_y * pos_y + depth * depth)
    basis = harmonics(pos_x * inv_distance, pos_y * inv_distance, depth * inv_distance)
    conic = [cov_c * inv_determ, -cov_b * inv_determ, cov_a * inv_determ]
    return [center_u, center_v] + conic + basis


def lane_gather(source, index):
    numbers = lax.GatherDimensionNumbers(
        offset_dims=(),
        collapsed_slice_dims=(1,),
        start_index_map=(1,),
        operand_batching_dims=(0,),
        start_indices_batching_dims=(0,),
    )
    return lax.gather(
        source,
        index[..., None],
        numbers,
        (1, 1),
        mode=lax.GatherScatterMode.PROMISE_IN_BOUNDS,
    )


def wide(row, rows=8):
    return jnp.broadcast_to(row, (rows, row.shape[-1]))


def pieces_of(value):
    first = value.astype(BF16)
    return first, (value - first.astype(F32)).astype(BF16)


def offsets_of(devices):
    lines = [0, 1, -1, 4, -4]
    return [(lines[w % 5] + w // 5 * (devices // 2)) % devices for w in range(NEAR)]


def window_copy(devices, w, direction, given, taken, send_sem, recv_sem, local_sem):
    offset = offsets_of(devices)[w]
    if offset == 0:
        return pltpu.make_async_copy(given, taken, local_sem)
    ahead = (offset * direction) % devices
    return pltpu.make_async_remote_copy(
        src_ref=given,
        dst_ref=taken,
        send_sem=send_sem.at[w],
        recv_sem=recv_sem.at[w],
        device_id=(lax.rem(lax.axis_index("dev") + ahead, devices),),
        device_id_type=MESH,
    )


def inner_partner(devices, me, k):
    return me // INNER * INNER + lax.rem(lax.rem(me, INNER) + k, INNER)


def outer_partner(devices, me, k):
    return lax.rem(me + INNER * k, devices)


def spread(devices, count, partner, given, taken, send_sem, recv_sem):
    return [
        pltpu.make_async_remote_copy(
            src_ref=given,
            dst_ref=taken.at[k],
            send_sem=send_sem.at[k],
            recv_sem=recv_sem.at[k],
            device_id=(partner(devices, lax.axis_index("dev"), k),),
            device_id_type=MESH,
        )
        for k in range(1, count)
    ]


def greet(devices):
    me = lax.axis_index("dev")
    partners = [lax.rem(me + offset, devices) for offset in offsets_of(devices) if offset]
    partners += [inner_partner(devices, me, k) for k in range(1, INNER)]
    partners += [outer_partner(devices, me, k) for k in range(1, devices // INNER)]
    barrier = pltpu.get_barrier_semaphore()
    for partner in partners:
        pl.semaphore_signal(barrier, inc=1, device_id=(partner,), device_id_type=MESH)
    return lambda: pl.semaphore_wait(barrier, len(partners))


def start(copies):
    for copy in copies:
        copy.start()


def finish(copies):
    for copy in copies:
        copy.wait()


def receive(copies):
    for copy in copies:
        if copy.is_remote:
            copy.wait_recv()
        else:
            copy.wait()


def sent_off(copies):
    for copy in copies:
        if copy.is_remote:
            copy.wait_send()


def sum_of(first, taken):
    total = first
    for k in range(1, taken.shape[0]):
        total = total + taken[k]
    return total


def feature(laid, f, block):
    first = (block // 2 * 16 + block % 2) * 8 + f % 8
    return laid[f // 8, pl.ds(first, 8, stride=16), :]


def lay_out(params, laid):
    count, g_local = params.shape

    @pl.loop(0, g_local // LANES)
    def _(c):
        columns = pl.ds(pl.multiple_of(c * LANES, LANES), LANES)
        first = pl.multiple_of(c * 8, 8)
        for group in range(count // 8):
            laid[group, pl.ds(first, 8), :] = params[group * 8 : group * 8 + 8, columns]
        over = count % 8
        laid[count // 8, pl.ds(first, over), :] = params[count - over :, columns]


def project(center_y, laid, splats, block):
    rows = [feature(laid, f, block) for f in range(11)]
    made = geometry(rows, center_y)
    opacity = jax.nn.sigmoid(rows[10])
    colors = []
    for c in range(3):
        total = made[5] * feature(laid, 11 + c, block)
        for k in range(1, 16):
            total = total + made[5 + k] * feature(laid, 11 + 3 * k + c, block)
        colors.append(total + 0.5)
    for f, row in enumerate(made[:5] + [opacity] + colors):
        splats[f, block % 2, block // 2 * 8 : block // 2 * 8 + 8, :] = row


def own_back(splats, mine, back):
    local = wide(mine)
    high = jnp.right_shift(local, 7)
    low = jnp.bitwise_and(local, LANES - 1)
    eight = lax.broadcasted_iota(jnp.int32, (8, LANES), 0)
    back[...] = jnp.zeros_like(back)
    for f in range(SPLAT):
        total = jnp.zeros((8, LANES), F32)
        for block in range(2 * splats.shape[2] // 8):
            hb, half = block // 2, block % 2
            found = lane_gather(splats[f, half, hb * 8 : hb * 8 + 8, :], low)
            total = jnp.where(high == hb * 16 + 2 * eight + half, found, total)
        back[f : f + 1, :] = jnp.sum(total, axis=0, keepdims=True)


def owner_gather(splats, wanted, i, sent):
    first = i * 8 * LANES
    rows = jnp.concatenate(
        [wanted[:, first + r * LANES : first + (r + 1) * LANES] for r in range(8)], axis=0
    )
    high = jnp.right_shift(rows, 7)
    low = jnp.bitwise_and(rows, LANES - 1)

    def pick(step, totals):
        totals = list(totals)
        for k in range(4):
            for half in range(2):
                c = step * 4 + k
                here = high == 2 * c + half
                for f in range(SPLAT):
                    source = wide(splats[f, half, pl.ds(c, 1), :])
                    totals[f] = jnp.where(here, lane_gather(source, low), totals[f])
        return tuple(totals)

    none = tuple(jnp.zeros((8, LANES), F32) for _ in range(SPLAT))
    totals = lax.fori_loop(0, splats.shape[2] // 4, pick, none)
    for half in range(2):
        for f in range(SPLAT):
            sent[i * 2 + half, f * 4 : f * 4 + 4, :] = totals[f][half * 4 : half * 4 + 4, :]
        sent[i * 2 + half, 36:40, :] = jnp.zeros((4, LANES), F32)


def scatter_rows(bins):
    return 16 * (bins + -(-bins // 8))


def scatter_lanes(index, right, column):
    low = wide(jnp.bitwise_and(index, 255), 256)
    place = lax.broadcasted_iota(jnp.int32, (256, LANES), 0)
    right[:, pl.ds(column, LANES)] = jnp.where(place == low, 1.0, 0.0).astype(BF16)


def scatter_bins(index, eight, ninth, left, column, bins):
    high = wide(jnp.right_shift(index, 8))

    def put(at, here, value):
        first = value.astype(BF16).astype(F32)
        both = [jnp.where(here, first, 0.0), jnp.where(here, value - first, 0.0)]
        left[at : at + 16, pl.ds(column, LANES)] = jnp.concatenate(both, axis=0).astype(BF16)

    for h in range(bins):
        put(h * 16, high == h, eight)
    ninth = wide(ninth)
    for i in range(-(-bins // 8)):
        own = lax.broadcasted_iota(jnp.int32, (8, LANES), 0) + 8 * i
        put((bins + i) * 16, high == own, ninth)


def bin_values(product, half, h, bins):
    eight = product[half, h * 16 : h * 16 + 8, :] + product[half, h * 16 + 8 : h * 16 + 16, :]
    at = (bins + h // 8) * 16 + h % 8
    return eight, product[half, at : at + 1, :] + product[half, at + 8 : at + 9, :]


def add_product(left, right, first, depth, product):
    columns = pl.ds(first, depth)
    made = lax.dot_general(
        left[:, columns],
        right[:, columns],
        (((1,), (1,)), ((), ())),
        preferred_element_type=F32,
    )
    product[0] += made[:, :LANES]
    product[1] += made[:, LANES:]


def scatter_product(left, right, product):
    step = 1280
    product[...] = jnp.zeros_like(product)

    @pl.loop(0, left.shape[1] // step)
    def _(i):
        add_product(left, right, pl.multiple_of(i * step, LANES), step, product)


def tiles_setup(
    tile_list, tile_order, tile_len, target, order, live, wished_in, wished, before, after
):
    tiles, list_len = tile_order.shape
    groups = list_len // LANES

    eight = lax.broadcasted_iota(jnp.int32, (8, LANES), 0)
    lengths = jnp.zeros((8, LANES), jnp.int32)
    for t in range(tiles):
        lengths = jnp.where(lax.rem(eight, tiles) == t, tile_len[t], lengths)
    for pair in range(groups // 2):
        ranks = jnp.concatenate(
            [
                tile_order[:, (2 * pair) * LANES : (2 * pair + 1) * LANES],
                tile_order[:, (2 * pair + 1) * LANES : (2 * pair + 2) * LANES],
            ],
            axis=0,
        )
        high = jnp.right_shift(ranks, 7)
        low = jnp.bitwise_and(ranks, LANES - 1)
        named = jnp.zeros((8, LANES), jnp.int32)
        for c in range(groups):
            part = [
                tile_list[:, t * list_len + c * LANES : t * list_len + (c + 1) * LANES]
                for t in range(tiles)
            ]
            source = jnp.concatenate(part + part, axis=0)
            named = jnp.where(high == c, lane_gather(source, low), named)
        order[pair * 8 : pair * 8 + 8, :] = named
        live[pair * 8 : pair * 8 + 8, :] = jnp.where(ranks < lengths, 1.0, 0.0)

    wished_in[...] = jnp.zeros_like(wished_in)
    for t in range(tiles):
        wished_in[3 * t : 3 * t + 3, :] = target[:, t * 256 : (t + 1) * 256]
    columns = jnp.transpose(wished_in[...])
    for t in range(tiles):
        for c in range(3):
            one = columns[:, 3 * t + c : 3 * t + c + 1]
            wished[t * 3 + c] = jnp.broadcast_to(one, (256, LANES))

    row_at = jnp.bitwise_and(lax.broadcasted_iota(jnp.int32, (256, 256), 0), LANES - 1)
    col_at = lax.broadcasted_iota(jnp.int32, (256, 256), 1)
    before[...] = jnp.where((row_at < col_at) | (col_at >= LANES), 1.0, 0.0).astype(BF16)
    after[...] = jnp.where((row_at > col_at) | (col_at >= LANES), 1.0, 0.0).astype(BF16)


def tiles_gather(w, arrived, order, entries):
    @pl.loop(0, order.shape[0] // 8)
    def _(i):
        spots = pl.ds(pl.multiple_of(i * 8, 8), 8)
        slots = order[spots, :]
        high = jnp.right_shift(slots, 7)
        low = jnp.bitwise_and(slots, LANES - 1)
        totals = [entries[f, spots, :] for f in range(SPLAT)]
        for k in range(4):
            here = high == w * 4 + k
            for f in range(SPLAT):
                source = wide(arrived[w, f * 4 + k : f * 4 + k + 1, :])
                totals[f] = jnp.where(here, lane_gather(source, low), totals[f])
        for f in range(SPLAT):
            entries[f, spots, :] = totals[f]


def tiles_render(
    tiles,
    tile_pos,
    entries,
    wished,
    alphas,
    split,
    sums,
    terms,
    carried,
    slopes,
    color_sums,
    entry_grads,
    before,
    after,
):
    lasts = alphas.shape[0]
    groups = lasts - 1
    back_row = tiles * groups
    entry_grads[...] = jnp.zeros_like(entry_grads)

    def row_of(t, j):
        listed = j // 2 * 8 + lax.rem(j, 2) * 4 + t
        return jnp.where(j == groups, back_row, listed)

    def entry(f, row):
        return wide(entries[f, pl.ds(row, 1), :])

    across = (
        lax.broadcasted_iota(jnp.int32, (2, 8, LANES), 0) * 8
        + lax.broadcasted_iota(jnp.int32, (2, 8, LANES), 1)
    ).astype(F32) + 0.5

    @pl.loop(0, tiles)
    def _(t):
        place = tile_pos[t]
        corner_x = (lax.rem(place, TILES_X) * 16).astype(F32)
        corner_y = (place // TILES_X * 16).astype(F32)

        @pl.loop(0, lasts)
        def _(j):
            row = row_of(t, j)
            delta_x = (across + corner_x) - entry(0, row)[None]
            center_v = entry(1, row)
            flat = -0.5 * entry(2, row)[None] * delta_x * delta_x
            mixed = -entry(3, row)[None] * delta_x
            half_c = -0.5 * entry(4, row)
            opacity = entry(5, row)[None]
            for y in range(16):
                delta_y = (corner_y + (y + 0.5)) - center_v
                slope = half_c * delta_y
                power = (mixed + slope[None]) * delta_y[None] + flat
                alpha = opacity * jnp.exp(power)
                keep = jnp.log(1.0 - alpha)
                spot = slice(y * 16, y * 16 + 16)
                alphas[j, spot, :] = alpha.reshape(16, LANES)
                first, second = pieces_of(keep.reshape(16, LANES))
                split[j, spot, :LANES] = first
                split[j, spot, LANES:] = second

        for j in range(lasts):
            sums[j] = jnp.dot(split[j], before[...], preferred_element_type=F32)

        @pl.loop(0, 8)
        def _(y):
            spot = pl.ds(pl.multiple_of(y * 32, 32), 32)
            gone = jnp.zeros((32, LANES), F32)
            seen = [jnp.zeros((4, 8, LANES), F32) for _ in range(3)]
            for j in range(lasts):
                row = row_of(t, j)
                transmit = jnp.exp(gone + sums[j, spot, :LANES])
                gone = gone + sums[j, spot, LANES:]
                weight = alphas[j, spot, :] * transmit
                terms[j, spot, :] = weight
                for c in range(3):
                    seen[c] = seen[c] + weight.reshape(4, 8, LANES) * entry(6 + c, row)[None]
            for c in range(3):
                slopes[c, spot, :] = seen[c].reshape(32, LANES)

        for c in range(3):
            color = jnp.sum(slopes[c], axis=1, keepdims=True)
            slopes[c] = 16.0 * (color - wished[t * 3 + c])

        @pl.loop(0, lasts)
        def _(j):
            row = row_of(t, j)
            colors = [entry(6 + c, row)[None] for c in range(3)]
            painted = [jnp.zeros((2, 8, LANES), F32) for _ in range(3)]
            for y in range(16):
                spot = slice(y * 16, y * 16 + 16)
                weight = terms[j, spot, :].reshape(2, 8, LANES)
                slope = [slopes[c, spot, :].reshape(2, 8, LANES) for c in range(3)]
                pull = slope[0] * colors[0] + slope[1] * colors[1] + slope[2] * colors[2]
                term = (pull * weight).reshape(16, LANES)
                terms[j, spot, :] = term
                first, second = pieces_of(term)
                split[j, spot, :LANES] = first
                split[j, spot, LANES:] = second
                for c in range(3):
                    painted[c] = painted[c] + slope[c] * weight
            for c in range(3):
                color_sums[c, j] = painted[c][0] + painted[c][1]

        for j in range(lasts):
            sums[j] = jnp.dot(split[j], after[...], preferred_element_type=F32)

        carried[...] = jnp.zeros_like(carried)

        @pl.loop(0, lasts)
        def _(back_j):
            j = groups - back_j
            row = row_of(t, j)
            delta_x = (across + corner_x) - entry(0, row)[None]
            center_v = entry(1, row)
            zero = jnp.zeros((2, 8, LANES), F32)
            sum_none, sum_y, sum_yy = zero, zero, zero
            for y in range(16):
                spot = slice(y * 16, y * 16 + 16)
                behind = carried[spot, :] + sums[j, spot, :LANES]
                carried[spot, :] += sums[j, spot, LANES:]
                alpha = alphas[j, spot, :]
                share = alpha / (1.0 - alpha)
                pull = (terms[j, spot, :] - behind * share).reshape(2, 8, LANES)
                delta_y = ((corner_y + (y + 0.5)) - center_v)[None]
                sum_none = sum_none + pull
                moved = pull * delta_y
                sum_y = sum_y + moved
                sum_yy = sum_yy + moved * delta_y

            def fold(value):
                return jnp.sum(value[0] + value[1], axis=0, keepdims=True)

            first_x = sum_none * delta_x
            in_none = fold(sum_none)
            in_x = fold(first_x)
            in_xx = fold(first_x * delta_x)
            in_xy = fold(sum_y * delta_x)
            in_y = fold(sum_y)
            in_yy = fold(sum_yy)
            con_a, con_b, con_c = (entries[f, pl.ds(row, 1), :] for f in (2, 3, 4))
            made = [
                con_a * in_x + con_b * in_y,
                con_c * in_y + con_b * in_x,
                -0.5 * in_xx,
                -in_xy,
                -0.5 * in_yy,
                in_none,
            ]
            made += [jnp.sum(color_sums[c, j], axis=0, keepdims=True) for c in range(3)]
            for f in range(SPLAT):
                entry_grads[row, f : f + 1, :] += made[f]


def slot_columns(order, entry_grads, left, right):
    @pl.loop(0, order.shape[0])
    def _(r):
        column = pl.multiple_of(r * LANES, LANES)
        values = entry_grads[r]
        index = order[pl.ds(r, 1), :]
        scatter_lanes(index, right, column)
        for half in range(2):
            own = index - half * NEAR * 256
            scatter_bins(own, values[0:8], values[8:9], left.at[half], column, NEAR)


def slot_values(product, part, slot_grads):
    for h in range(NEAR):
        w = part * 5 + h // 2
        for half in range(2):
            eight, ninth = bin_values(product, half, h, NEAR)
            for f in range(SPLAT):
                at = f * 4 + (h % 2) * 2 + half
                slot_grads[w, at : at + 1, :] = eight[f : f + 1] if f < 8 else ninth
        slot_grads[w, 36:40, :] = jnp.zeros((4, LANES), F32)


def owner_columns(w, source, wanted, left, right, bins):
    for k in range(4):
        column = (w * 4 + k) * LANES
        eight = source[w, pl.ds(k, 8, stride=4), :]
        ninth = source[w, 32 + k : 33 + k, :]
        index = wanted[:, column : column + LANES]
        scatter_lanes(index, right, column)
        scatter_bins(index, eight, ninth, left, column, bins)


def owner_values(product, bins, pulls):
    for hb in range(bins // 8):
        for half in range(2):
            spot = slice(hb * 8, hb * 8 + 8)
            for f in range(8):
                first = product[half, pl.ds(hb * 128 + f, 8, stride=16), :]
                second = product[half, pl.ds(hb * 128 + 8 + f, 8, stride=16), :]
                pulls[f, half, spot, :] = first + second
            at = (bins + hb) * 16
            ninth = product[half, at : at + 8, :] + product[half, at + 8 : at + 16, :]
            pulls[8, half, spot, :] = ninth


def step_kernel(
    devices,
    center_y,
    far_params,
    far_target,
    far_req,
    far_list,
    tile_len,
    far_order,
    tile_pos,
    far_ids,
    pulls,
    laid,
    params,
    target,
    req,
    tile_list,
    tile_order,
    bg_ids,
    splats,
    wanted,
    sent,
    arrived,
    slot_grads,
    returned,
    backs,
    inner_held,
    outer_held,
    order,
    live,
    entries,
    wished_in,
    wished,
    alphas,
    split,
    sums,
    terms,
    carried,
    slopes,
    color_sums,
    entry_grads,
    before,
    after,
    left,
    right,
    product,
    owner_left,
    owner_right,
    owner_product,
    load_sem,
    local_sem,
    ask_send,
    ask_recv,
    send_sem,
    recv_sem,
    turn_send,
    turn_recv,
    inner_send,
    inner_recv,
    outer_send,
    outer_recv,
):
    g_local = params.shape[1]
    bins = g_local // 256
    slots = req.shape[1]
    cap = slots // NEAR
    tiles, list_len = tile_order.shape
    back_row = tiles * list_len // LANES
    me = lax.axis_index("dev")
    pairs = [
        (far_params, params),
        (far_req, req),
        (far_ids, bg_ids),
        (far_list, tile_list),
        (far_order, tile_order),
        (far_target, target),
    ]
    loads = [
        pltpu.make_async_copy(given, taken, load_sem.at[i]) for i, (given, taken) in enumerate(pairs)
    ]
    start(loads)
    greeted = greet(devices)

    finish(loads[:3])
    lay_out(params, laid)
    for block in range(g_local // 1024):
        project(center_y, laid, splats, block)
    greeted()
    asks = []
    for w in range(NEAR):
        columns = pl.ds(w * cap, cap)
        given, taken = req.at[:, columns], wanted.at[:, columns]
        asks.append(window_copy(devices, w, 1, given, taken, ask_send, ask_recv, local_sem.at[0]))
    start(asks)
    mine = bg_ids[...] - me * g_local
    own_back(splats, mine, backs.at[0])

    def spread_inner(stage):
        return spread(
            devices,
            INNER,
            inner_partner,
            backs.at[2 * stage],
            inner_held.at[stage],
            inner_send.at[stage],
            inner_recv.at[stage],
        )

    def spread_outer(stage):
        return spread(
            devices,
            devices // INNER,
            outer_partner,
            backs.at[2 * stage + 1],
            outer_held.at[stage],
            outer_send.at[stage],
            outer_recv.at[stage],
        )

    inner = spread_inner(0)
    start(inner)
    finish(loads[3:6])
    tiles_setup(
        tile_list, tile_order, tile_len, target, order, live, wished_in, wished, before, after
    )
    entries[...] = jnp.zeros_like(entries)

    supplies = {
        w: window_copy(
            devices, w, -1, sent.at[w], arrived.at[w], send_sem, recv_sem, local_sem.at[1]
        )
        for w in range(NEAR)
    }

    def answer(i):
        receive(asks[2 * i : 2 * i + 2])
        owner_gather(splats, wanted, i, sent)
        start([supplies[2 * i], supplies[2 * i + 1]])

    answer(0)
    answer(1)
    receive(inner)
    backs[1] = sum_of(backs[0], inner_held.at[0])
    outer = spread_outer(0)
    start(outer)
    for i in (4, 3, 2):
        answer(i)
    for w in (0, 1, 2, 3, 5, 4, 7, 6, 9, 8):
        receive([supplies[w]])
        tiles_gather(w, arrived, order, entries)
    entries[5, 0:back_row, :] = entries[5, 0:back_row, :] * live[...]
    receive(outer)
    summed = sum_of(backs[1], outer_held.at[0])
    for f in range(SPLAT):
        entries[f, back_row : back_row + 1, :] = summed[f : f + 1, :]

    tiles_render(
        tiles,
        tile_pos,
        entries,
        wished,
        alphas,
        split,
        sums,
        terms,
        carried,
        slopes,
        color_sums,
        entry_grads,
        before,
        after,
    )

    backs[2] = entry_grads[back_row]
    started = asks + list(supplies.values()) + inner + outer
    inner = spread_inner(1)
    start(inner)
    slot_columns(order, entry_grads, left, right)
    turns = {
        w: window_copy(
            devices, w, 1, slot_grads.at[w], returned.at[w], turn_send, turn_recv, local_sem.at[2]
        )
        for w in range(1, NEAR)
    }
    for half in reversed(range(2)):
        scatter_product(left.at[half], right, product)
        slot_values(product, half, slot_grads)
        start([turns[w] for w in reversed(range(max(1, half * 5), half * 5 + 5))])
        if half == 1:
            receive(inner)
            backs[3] = sum_of(backs[2], inner_held.at[1])
            outer = spread_outer(1)
            start(outer)
    owner_product[...] = jnp.zeros_like(owner_product)
    owner_columns(0, slot_grads, wanted, owner_left, owner_right, bins)
    add_product(owner_left, owner_right, 0, cap, owner_product)
    for w in (5, 1, 2, 3, 4, 7, 6, 9, 8):
        receive([turns[w]])
        owner_columns(w, returned, wanted, owner_left, owner_right, bins)
        add_product(owner_left, owner_right, w * cap, cap, owner_product)
        if w == 4:
            receive(outer)
            summed = sum_of(backs[3], outer_held.at[1])
            scatter_lanes(mine, owner_right, slots)
            scatter_bins(mine, summed[0:8], summed[8:9], owner_left, slots, bins)
            add_product(owner_left, owner_right, slots, LANES, owner_product)
    owner_values(owner_product, bins, pulls)
    sent_off(started + inner + outer + list(turns.values()))


def step(devices, center_y, *args):
    params, target, req_rows, tile_list, tile_len, tile_order, tile_pos, ids = args
    count, g_local = params.shape
    slots = req_rows.shape[1]
    tiles, list_len = tile_order.shape
    rows = tiles * list_len // LANES
    lasts = list_len // LANES + 1
    bins = g_local // 256
    depth = slots + LANES
    outers = devices // INNER
    far = pl.BlockSpec(memory_space=pltpu.HBM)
    near = pl.BlockSpec(memory_space=pltpu.VMEM)
    smem = pl.BlockSpec(memory_space=pltpu.SMEM)
    dma = pltpu.SemaphoreType.DMA
    shape = jax.ShapeDtypeStruct
    vmem = pltpu.VMEM
    return pl.pallas_call(
        functools.partial(step_kernel, devices, center_y),
        out_shape=shape((SPLAT, 2, bins, LANES), F32),
        in_specs=[far] * 4 + [smem, far, smem, far],
        out_specs=near,
        scratch_shapes=[
            vmem((8, g_local // 16, LANES), F32),
            vmem(params.shape, F32),
            vmem(target.shape, F32),
            vmem(req_rows.shape, jnp.int32),
            vmem(tile_list.shape, jnp.int32),
            vmem(tile_order.shape, jnp.int32),
            vmem(ids.shape, jnp.int32),
            vmem((SPLAT, 2, g_local // 256, LANES), F32),
            vmem(req_rows.shape, jnp.int32),
            vmem((NEAR, 40, LANES), F32),
            vmem((NEAR, 40, LANES), F32),
            vmem((NEAR, 40, LANES), F32),
            vmem((NEAR, 40, LANES), F32),
            vmem((4, 16, LANES), F32),
            vmem((2, INNER, 16, LANES), F32),
            vmem((2, outers, 16, LANES), F32),
            vmem((rows, LANES), jnp.int32),
            vmem((rows, LANES), F32),
            vmem((SPLAT, rows + 8, LANES), F32),
            vmem((LANES, 256), F32),
            vmem((tiles * 3, 256, LANES), F32),
            vmem((lasts, 256, LANES), F32),
            vmem((lasts, 256, 256), BF16),
            vmem((lasts, 256, 256), F32),
            vmem((lasts, 256, LANES), F32),
            vmem((256, LANES), F32),
            vmem((3, 256, LANES), F32),
            vmem((3, lasts, 8, LANES), F32),
            vmem((rows + 1, 16, LANES), F32),
            vmem((256, 256), BF16),
            vmem((256, 256), BF16),
            vmem((2, scatter_rows(NEAR), rows * LANES), BF16),
            vmem((256, rows * LANES), BF16),
            vmem((2, scatter_rows(NEAR), LANES), F32),
            vmem((scatter_rows(bins), depth), BF16),
            vmem((256, depth), BF16),
            vmem((2, scatter_rows(bins), LANES), F32),
            dma((6,)),
            dma((3,)),
            dma((NEAR,)),
            dma((NEAR,)),
            dma((NEAR,)),
            dma((NEAR,)),
            dma((NEAR,)),
            dma((NEAR,)),
            dma((2, INNER)),
            dma((2, INNER)),
            dma((2, outers)),
            dma((2, outers)),
        ],
        compiler_params=pltpu.CompilerParams(
            collective_id=0, has_side_effects=True, vmem_limit_bytes=60 * 2**20
        ),
        name="step",
    )(*args)


def update_kernel(
    center_y,
    far_params,
    far_m,
    far_v,
    far_pulls,
    new_params,
    new_m,
    new_v,
    params,
    adam_m,
    adam_v,
    pulls,
    laid,
    grads,
    held_params,
    held_m,
    held_v,
    load_sem,
    sems,
):
    count, g_local = params.shape
    pairs = [(far_params, params), (far_pulls, pulls), (far_m, adam_m), (far_v, adam_v)]
    loads = [
        pltpu.make_async_copy(given, taken, load_sem.at[i]) for i, (given, taken) in enumerate(pairs)
    ]
    start(loads)
    copies = []
    finish(loads[:2])
    lay_out(params, laid)
    for hb in range(g_local // 2048):
        for half in range(2):
            block = hb * 2 + half
            rows = [feature(laid, f, block) for f in range(10)]
            made, pull_back = jax.vjp(lambda given: geometry(given, center_y), rows)
            got = [pulls[f, half, hb * 8 : hb * 8 + 8, :] for f in range(SPLAT)]

            def put(f, value):
                first = (hb * 16 + half) * 8 + f % 8
                grads[f // 8, pl.ds(first, 8, stride=16), :] = value

            given = got[:5]
            for k in range(16):
                at = 11 + 3 * k
                total = got[6] * feature(laid, at, block)
                total = total + got[7] * feature(laid, at + 1, block)
                total = total + got[8] * feature(laid, at + 2, block)
                given.append(total)
                for c in range(3):
                    put(at + c, made[5 + k] * got[6 + c])
            for f, row in enumerate(pull_back(given)[0]):
                put(f, row)
            put(10, got[5] * (1.0 - jax.nn.sigmoid(feature(laid, 10, block))))

        if hb == 0:
            finish(loads[2:])

        @pl.loop(0, 16)
        def _(chunk):
            c = hb * 16 + chunk
            columns = pl.ds(pl.multiple_of(c * LANES, LANES), LANES)
            first = pl.multiple_of(c * 8, 8)
            for group in range(-(-count // 8)):
                size = min(8, count - group * 8)
                spot = slice(group * 8, group * 8 + size)
                slope = grads[group, pl.ds(first, size), :]
                moment = 0.9 * adam_m[spot, columns] + 0.1 * slope
                power = 0.999 * adam_v[spot, columns] + 0.001 * slope * slope
                change = moment / BIAS_ONE / (jnp.sqrt(power / BIAS_TWO) + 1e-08)
                held_params[spot, columns] = params[spot, columns] - 0.05 * change
                held_m[spot, columns] = moment
                held_v[spot, columns] = power

        columns = pl.ds(hb * 2048, 2048)
        for i, (held, out) in enumerate(
            ((held_params, new_params), (held_m, new_m), (held_v, new_v))
        ):
            copies.append(
                pltpu.make_async_copy(held.at[:, columns], out.at[:, columns], sems.at[hb * 3 + i])
            )
        start(copies[-3:])
    finish(copies)


def update(params, adam_m, adam_v, pulls, center_y):
    count, g_local = params.shape
    far = pl.BlockSpec(memory_space=pltpu.HBM)
    shape = jax.ShapeDtypeStruct(params.shape, F32)
    return pl.pallas_call(
        functools.partial(update_kernel, center_y),
        out_shape=(shape, shape, shape),
        in_specs=[far] * 4,
        out_specs=(far, far, far),
        scratch_shapes=[
            pltpu.VMEM((count, g_local), F32),
            pltpu.VMEM((count, g_local), F32),
            pltpu.VMEM((count, g_local), F32),
            pltpu.VMEM(pulls.shape, F32),
            pltpu.VMEM((8, g_local // 16, LANES), F32),
            pltpu.VMEM((8, g_local // 16, LANES), F32),
            pltpu.VMEM((count, g_local), F32),
            pltpu.VMEM((count, g_local), F32),
            pltpu.VMEM((count, g_local), F32),
            pltpu.SemaphoreType.DMA((4,)),
            pltpu.SemaphoreType.DMA((3 * (g_local // 2048),)),
        ],
        compiler_params=pltpu.CompilerParams(vmem_limit_bytes=60 * 2**20),
        name="update",
    )(params, adam_m, adam_v, pulls)


def per_device(
    devices,
    params,
    adam_m,
    adam_v,
    target,
    req_rows,
    tile_list,
    tile_len,
    tile_order,
    tile_pos,
    bg_ids,
):
    center_y = 8.0 * (tile_order.shape[0] * devices // TILES_X)
    pulls = step(
        devices,
        center_y,
        params,
        target,
        req_rows,
        tile_list,
        tile_len,
        tile_order,
        tile_pos,
        bg_ids.reshape(1, LANES),
    )
    return update(params, adam_m, adam_v, pulls, center_y)


def solution(mesh):
    return jax.shard_map(
        functools.partial(per_device, mesh.shape["dev"]),
        mesh=mesh,
        in_specs=(
            P(None, "dev"),
            P(None, "dev"),
            P(None, "dev"),
            P(None, "dev"),
            P("dev", None),
            P("dev", None),
            P("dev"),
            P("dev", None),
            P("dev"),
            P(),
        ),
        out_specs=(P(None, "dev"), P(None, "dev"), P(None, "dev")),
        check_vma=False,
    )
```

```python
import functools

import jax
import jax.numpy as jnp
from jax import lax
from jax.experimental import pallas as pl
from jax.experimental.pallas import tpu as pltpu
from jax.sharding import PartitionSpec as P

TILES_X = 32
NEAR = 10
FOCAL = 512.0
BIAS_ONE = 1.0 - 0.9**10
BIAS_TWO = 1.0 - 0.999**10
MESH = pl.DeviceIdType.MESH
F32 = jnp.float32
BF16 = jnp.bfloat16
LANES = 128
INNER = 16
SPLAT = 9


def harmonics(dir_x, dir_y, dir_z):
    sq_x = dir_x * dir_x
    sq_y = dir_y * dir_y
    sq_z = dir_z * dir_z
    return [
        0.28209479177387814 + 0.0 * dir_x,
        -0.4886025119029199 * dir_y,
        0.4886025119029199 * dir_z,
        -0.4886025119029199 * dir_x,
        1.0925484305920792 * dir_x * dir_y,
        -1.0925484305920792 * dir_y * dir_z,
        0.31539156525252005 * (2.0 * sq_z - sq_x - sq_y),
        -1.0925484305920792 * dir_x * dir_z,
        0.5462742152960396 * (sq_x - sq_y),
        -0.5900435899266435 * dir_y * (3.0 * sq_x - sq_y),
        2.890611442640554 * dir_x * dir_y * dir_z,
        -0.4570457994644658 * dir_y * (4.0 * sq_z - sq_x - sq_y),
        0.3731763325901154 * dir_z * (2.0 * sq_z - 3.0 * sq_x - 3.0 * sq_y),
        -0.4570457994644658 * dir_x * (4.0 * sq_z - sq_x - sq_y),
        1.445305721320277 * dir_z * (sq_x - sq_y),
        -0.5900435899266435 * dir_x * (sq_x - 3.0 * sq_y),
    ]


def geometry(rows, center_y):
    pos_x, pos_y, depth = (rows[0], rows[1], rows[2])
    stretches = (jnp.exp(rows[3]), jnp.exp(rows[4]), jnp.exp(rows[5]))
    quat_norm = jnp.sqrt(
        rows[6] * rows[6] + rows[7] * rows[7] + rows[8] * rows[8] + rows[9] * rows[9]
    )
    inv_norm = 1.0 / quat_norm
    quat_w = rows[6] * inv_norm
    quat_x = rows[7] * inv_norm
    quat_y = rows[8] * inv_norm
    quat_z = rows[9] * inv_norm
    rotation = (
        (
            1.0 - 2.0 * (quat_y * quat_y + quat_z * quat_z),
            2.0 * (quat_x * quat_y - quat_w * quat_z),
            2.0 * (quat_x * quat_z + quat_w * quat_y),
        ),
        (
            2.0 * (quat_x * quat_y + quat_w * quat_z),
            1.0 - 2.0 * (quat_x * quat_x + quat_z * quat_z),
            2.0 * (quat_y * quat_z - quat_w * quat_x),
        ),
        (
            2.0 * (quat_x * quat_z - quat_w * quat_y),
            2.0 * (quat_y * quat_z + quat_w * quat_x),
            1.0 - 2.0 * (quat_x * quat_x + quat_y * quat_y),
        ),
    )
    inv_depth = 1.0 / depth
    focal_z = FOCAL * inv_depth
    slope_x = pos_x * inv_depth
    slope_y = pos_y * inv_depth
    cov_a = 0.3
    cov_b = 0.0
    cov_c = 0.3
    for column in range(3):
        axis_x = rotation[0][column] * stretches[column]
        axis_y = rotation[1][column] * stretches[column]
        axis_z = rotation[2][column] * stretches[column]
        image_u = focal_z * (axis_x - slope_x * axis_z)
        image_v = focal_z * (axis_y - slope_y * axis_z)
        cov_a = cov_a + image_u * image_u
        cov_b = cov_b + image_u * image_v
        cov_c = cov_c + image_v * image_v
    inv_determ = 1.0 / (cov_a * cov_c - cov_b * cov_b)
    center_u = FOCAL * slope_x + 8.0 * TILES_X
    center_v = FOCAL * slope_y + center_y
    inv_distance = 1.0 / jnp.sqrt(pos_x * pos_x + pos_y * pos_y + depth * depth)
    basis = harmonics(pos_x * inv_distance, pos_y * inv_distance, depth * inv_distance)
    conic = [cov_c * inv_determ, -cov_b * inv_determ, cov_a * inv_determ]
    return [center_u, center_v] + conic + basis


def lane_gather(source, index):
    numbers = lax.GatherDimensionNumbers(
        offset_dims=(),
        collapsed_slice_dims=(1,),
        start_index_map=(1,),
        operand_batching_dims=(0,),
        start_indices_batching_dims=(0,),
    )
    return lax.gather(
        source,
        index[..., None],
        numbers,
        (1, 1),
        mode=lax.GatherScatterMode.PROMISE_IN_BOUNDS,
    )


def wide(row, rows=8):
    return jnp.broadcast_to(row, (rows, row.shape[-1]))


def pieces_of(value):
    first = value.astype(BF16)
    return first, (value - first.astype(F32)).astype(BF16)


def offsets_of(devices):
    lines = [0, 1, -1, 4, -4]
    return [(lines[w % 5] + w // 5 * (devices // 2)) % devices for w in range(NEAR)]


def window_copy(devices, w, direction, given, taken, send_sem, recv_sem, local_sem):
    offset = offsets_of(devices)[w]
    if offset == 0:
        return pltpu.make_async_copy(given, taken, local_sem)
    ahead = (offset * direction) % devices
    return pltpu.make_async_remote_copy(
        src_ref=given,
        dst_ref=taken,
        send_sem=send_sem.at[w],
        recv_sem=recv_sem.at[w],
        device_id=(lax.rem(lax.axis_index("dev") + ahead, devices),),
        device_id_type=MESH,
    )


def inner_partner(devices, me, k):
    return me // INNER * INNER + lax.rem(lax.rem(me, INNER) + k, INNER)


def outer_partner(devices, me, k):
    return lax.rem(me + INNER * k, devices)


def spread(devices, count, partner, given, taken, send_sem, recv_sem):
    return [
        pltpu.make_async_remote_copy(
            src_ref=given,
            dst_ref=taken.at[k],
            send_sem=send_sem.at[k],
            recv_sem=recv_sem.at[k],
            device_id=(partner(devices, lax.axis_index("dev"), k),),
            device_id_type=MESH,
        )
        for k in range(1, count)
    ]


def greet(devices):
    me = lax.axis_index("dev")
    partners = [lax.rem(me + offset, devices) for offset in offsets_of(devices) if offset]
    partners += [inner_partner(devices, me, k) for k in range(1, INNER)]
    partners += [outer_partner(devices, me, k) for k in range(1, devices // INNER)]
    barrier = pltpu.get_barrier_semaphore()
    for partner in partners:
        pl.semaphore_signal(barrier, inc=1, device_id=(partner,), device_id_type=MESH)
    return lambda: pl.semaphore_wait(barrier, len(partners))


def start(copies):
    for copy in copies:
        copy.start()


def finish(copies):
    for copy in copies:
        copy.wait()


def receive(copies):
    for copy in copies:
        if copy.is_remote:
            copy.wait_recv()
        else:
            copy.wait()


def sent_off(copies):
    for copy in copies:
        if copy.is_remote:
            copy.wait_send()


def sum_of(first, taken):
    total = first
    for k in range(1, taken.shape[0]):
        total = total + taken[k]
    return total


def feature(laid, f, block):
    first = (block // 2 * 16 + block % 2) * 8 + f % 8
    return laid[f // 8, pl.ds(first, 8, stride=16), :]


def lay_out(params, laid, first_chunk, last_chunk):
    count = params.shape[0]

    @pl.loop(first_chunk, last_chunk)
    def _(c):
        columns = pl.ds(pl.multiple_of(c * LANES, LANES), LANES)
        first = pl.multiple_of(c * 8, 8)
        for group in range(count // 8):
            laid[group, pl.ds(first, 8), :] = params[group * 8 : group * 8 + 8, columns]
        over = count % 8
        laid[count // 8, pl.ds(first, over), :] = params[count - over :, columns]


def project(center_y, laid, splats, block):
    rows = [feature(laid, f, block) for f in range(11)]
    made = geometry(rows, center_y)
    opacity = jax.nn.sigmoid(rows[10])
    colors = []
    for c in range(3):
        total = made[5] * feature(laid, 11 + c, block)
        for k in range(1, 16):
            total = total + made[5 + k] * feature(laid, 11 + 3 * k + c, block)
        colors.append(total + 0.5)
    for f, row in enumerate(made[:5] + [opacity] + colors):
        splats[f, block % 2, block // 2 * 8 : block // 2 * 8 + 8, :] = row


def own_back(splats, mine, back):
    local = wide(mine)
    high = jnp.right_shift(local, 7)
    low = jnp.bitwise_and(local, LANES - 1)
    eight = lax.broadcasted_iota(jnp.int32, (8, LANES), 0)
    back[...] = jnp.zeros_like(back)
    for f in range(SPLAT):
        total = jnp.zeros((8, LANES), F32)
        for block in range(2 * splats.shape[2] // 8):
            hb, half = block // 2, block % 2
            found = lane_gather(splats[f, half, hb * 8 : hb * 8 + 8, :], low)
            total = jnp.where(high == hb * 16 + 2 * eight + half, found, total)
        back[f : f + 1, :] = jnp.sum(total, axis=0, keepdims=True)


def owner_gather(splats, wanted, i, sent):
    first = i * 8 * LANES
    rows = jnp.concatenate(
        [wanted[:, first + r * LANES : first + (r + 1) * LANES] for r in range(8)], axis=0
    )
    high = jnp.right_shift(rows, 7)
    low = jnp.bitwise_and(rows, LANES - 1)

    def pick(step, totals):
        totals = list(totals)
        for k in range(4):
            for half in range(2):
                c = step * 4 + k
                here = high == 2 * c + half
                for f in range(SPLAT):
                    source = wide(splats[f, half, pl.ds(c, 1), :])
                    totals[f] = jnp.where(here, lane_gather(source, low), totals[f])
        return tuple(totals)

    none = tuple(jnp.zeros((8, LANES), F32) for _ in range(SPLAT))
    totals = lax.fori_loop(0, splats.shape[2] // 4, pick, none)
    for half in range(2):
        for f in range(SPLAT):
            sent[i * 2 + half, f * 4 : f * 4 + 4, :] = totals[f][half * 4 : half * 4 + 4, :]
        sent[i * 2 + half, 36:40, :] = jnp.zeros((4, LANES), F32)


def scatter_rows(bins):
    return 16 * (bins + -(-bins // 8))


def scatter_lanes(index, right, column):
    low = wide(jnp.bitwise_and(index, 255), 256)
    place = lax.broadcasted_iota(jnp.int32, (256, LANES), 0)
    right[:, pl.ds(column, LANES)] = jnp.where(place == low, 1.0, 0.0).astype(BF16)


def scatter_bins(index, eight, ninth, left, column, bins):
    high = wide(jnp.right_shift(index, 8))

    def put(at, here, value):
        first = value.astype(BF16).astype(F32)
        both = [jnp.where(here, first, 0.0), jnp.where(here, value - first, 0.0)]
        left[at : at + 16, pl.ds(column, LANES)] = jnp.concatenate(both, axis=0).astype(BF16)

    for h in range(bins):
        put(h * 16, high == h, eight)
    ninth = wide(ninth)
    for i in range(-(-bins // 8)):
        own = lax.broadcasted_iota(jnp.int32, (8, LANES), 0) + 8 * i
        put((bins + i) * 16, high == own, ninth)


def bin_values(product, half, h, bins):
    eight = product[half, h * 16 : h * 16 + 8, :] + product[half, h * 16 + 8 : h * 16 + 16, :]
    at = (bins + h // 8) * 16 + h % 8
    return eight, product[half, at : at + 1, :] + product[half, at + 8 : at + 9, :]


def add_product(left, right, first, depth, product):
    columns = pl.ds(first, depth)
    made = lax.dot_general(
        left[:, columns],
        right[:, columns],
        (((1,), (1,)), ((), ())),
        preferred_element_type=F32,
    )
    product[0] += made[:, :LANES]
    product[1] += made[:, LANES:]


def scatter_product(left, right, product):
    product[...] = jnp.zeros_like(product)
    add_product(left, right, 0, left.shape[1], product)


def tiles_setup(
    tile_list, tile_order, tile_len, target, order, live, wished_in, wished, before, after
):
    tiles, list_len = tile_order.shape
    groups = list_len // LANES

    eight = lax.broadcasted_iota(jnp.int32, (8, LANES), 0)
    lengths = jnp.zeros((8, LANES), jnp.int32)
    for t in range(tiles):
        lengths = jnp.where(lax.rem(eight, tiles) == t, tile_len[t], lengths)
    for pair in range(groups // 2):
        ranks = jnp.concatenate(
            [
                tile_order[:, (2 * pair) * LANES : (2 * pair + 1) * LANES],
                tile_order[:, (2 * pair + 1) * LANES : (2 * pair + 2) * LANES],
            ],
            axis=0,
        )
        high = jnp.right_shift(ranks, 7)
        low = jnp.bitwise_and(ranks, LANES - 1)
        named = jnp.zeros((8, LANES), jnp.int32)
        for c in range(groups):
            part = [
                tile_list[:, t * list_len + c * LANES : t * list_len + (c + 1) * LANES]
                for t in range(tiles)
            ]
            source = jnp.concatenate(part + part, axis=0)
            named = jnp.where(high == c, lane_gather(source, low), named)
        order[pair * 8 : pair * 8 + 8, :] = named
        live[pair * 8 : pair * 8 + 8, :] = jnp.where(ranks < lengths, 1.0, 0.0)

    wished_in[...] = jnp.zeros_like(wished_in)
    for t in range(tiles):
        wished_in[3 * t : 3 * t + 3, :] = target[:, t * 256 : (t + 1) * 256]
    columns = jnp.transpose(wished_in[...])
    for t in range(tiles):
        for c in range(3):
            one = columns[:, 3 * t + c : 3 * t + c + 1]
            wished[t * 3 + c] = jnp.broadcast_to(one, (256, LANES))

    row_at = jnp.bitwise_and(lax.broadcasted_iota(jnp.int32, (256, 256), 0), LANES - 1)
    col_at = lax.broadcasted_iota(jnp.int32, (256, 256), 1)
    before[...] = jnp.where((row_at < col_at) | (col_at >= LANES), 1.0, 0.0).astype(BF16)
    after[...] = jnp.where((row_at > col_at) | (col_at >= LANES), 1.0, 0.0).astype(BF16)


def tiles_gather(w, arrived, order, entries):
    for i in range(order.shape[0] // 8):
        spots = pl.ds(i * 8, 8)
        slots = order[spots, :]
        high = jnp.right_shift(slots, 7)
        low = jnp.bitwise_and(slots, LANES - 1)
        totals = [entries[f, spots, :] for f in range(SPLAT)]
        for k in range(4):
            here = high == w * 4 + k
            for f in range(SPLAT):
                source = wide(arrived[w, f * 4 + k : f * 4 + k + 1, :])
                totals[f] = jnp.where(here, lane_gather(source, low), totals[f])
        for f in range(SPLAT):
            entries[f, spots, :] = totals[f]


def tiles_render(
    tiles,
    tile_pos,
    entries,
    wished,
    alphas,
    split,
    sums,
    terms,
    carried,
    slopes,
    color_sums,
    entry_grads,
    before,
    after,
):
    lasts = alphas.shape[0]
    groups = lasts - 1
    back_row = tiles * groups
    entry_grads[...] = jnp.zeros_like(entry_grads)

    def row_of(t, j):
        listed = j // 2 * 8 + lax.rem(j, 2) * 4 + t
        return jnp.where(j == groups, back_row, listed)

    def entry(f, row):
        return wide(entries[f, pl.ds(row, 1), :])

    across = (
        lax.broadcasted_iota(jnp.int32, (2, 8, LANES), 0) * 8
        + lax.broadcasted_iota(jnp.int32, (2, 8, LANES), 1)
    ).astype(F32) + 0.5

    @pl.loop(0, tiles)
    def _(t):
        place = tile_pos[t]
        corner_x = (lax.rem(place, TILES_X) * 16).astype(F32)
        corner_y = (place // TILES_X * 16).astype(F32)

        @pl.loop(0, lasts)
        def _(j):
            row = row_of(t, j)
            delta_x = (across + corner_x) - entry(0, row)[None]
            center_v = entry(1, row)
            flat = -0.5 * entry(2, row)[None] * delta_x * delta_x
            mixed = -entry(3, row)[None] * delta_x
            half_c = -0.5 * entry(4, row)
            opacity = entry(5, row)[None]
            for y in range(16):
                delta_y = (corner_y + (y + 0.5)) - center_v
                slope = half_c * delta_y
                power = (mixed + slope[None]) * delta_y[None] + flat
                alpha = opacity * jnp.exp(power)
                keep = jnp.log(1.0 - alpha)
                spot = slice(y * 16, y * 16 + 16)
                alphas[j, spot, :] = alpha.reshape(16, LANES)
                first, second = pieces_of(keep.reshape(16, LANES))
                split[j, spot, :LANES] = first
                split[j, spot, LANES:] = second

        for j in range(lasts):
            sums[j] = jnp.dot(split[j], before[...], preferred_element_type=F32)

        @pl.loop(0, 4)
        def _(y):
            spot = pl.ds(pl.multiple_of(y * 64, 64), 64)
            gone = jnp.zeros((64, LANES), F32)
            seen = [jnp.zeros((8, 8, LANES), F32) for _ in range(3)]
            for j in range(lasts):
                row = row_of(t, j)
                transmit = jnp.exp(gone + sums[j, spot, :LANES])
                gone = gone + sums[j, spot, LANES:]
                weight = alphas[j, spot, :] * transmit
                terms[j, spot, :] = weight
                for c in range(3):
                    seen[c] = seen[c] + weight.reshape(8, 8, LANES) * entry(6 + c, row)[None]
            for c in range(3):
                slopes[c, spot, :] = seen[c].reshape(64, LANES)

        for c in range(3):
            color = jnp.sum(slopes[c], axis=1, keepdims=True)
            slopes[c] = 16.0 * (color - wished[t * 3 + c])

        @pl.loop(0, lasts)
        def _(j):
            row = row_of(t, j)
            colors = [entry(6 + c, row)[None] for c in range(3)]
            painted = [jnp.zeros((2, 8, LANES), F32) for _ in range(3)]
            for y in range(16):
                spot = slice(y * 16, y * 16 + 16)
                weight = terms[j, spot, :].reshape(2, 8, LANES)
                slope = [slopes[c, spot, :].reshape(2, 8, LANES) for c in range(3)]
                pull = slope[0] * colors[0] + slope[1] * colors[1] + slope[2] * colors[2]
                term = (pull * weight).reshape(16, LANES)
                terms[j, spot, :] = term
                first, second = pieces_of(term)
                split[j, spot, :LANES] = first
                split[j, spot, LANES:] = second
                for c in range(3):
                    painted[c] = painted[c] + slope[c] * weight
            for c in range(3):
                color_sums[c, j] = painted[c][0] + painted[c][1]

        for j in range(lasts):
            sums[j] = jnp.dot(split[j], after[...], preferred_element_type=F32)

        carried[...] = jnp.zeros_like(carried)

        @pl.loop(0, lasts)
        def _(back_j):
            j = groups - back_j
            row = row_of(t, j)
            delta_x = (across + corner_x) - entry(0, row)[None]
            center_v = entry(1, row)
            zero = jnp.zeros((2, 8, LANES), F32)
            sum_none, sum_y, sum_yy = zero, zero, zero
            for y in range(16):
                spot = slice(y * 16, y * 16 + 16)
                behind = carried[spot, :] + sums[j, spot, :LANES]
                carried[spot, :] += sums[j, spot, LANES:]
                alpha = alphas[j, spot, :]
                share = alpha / (1.0 - alpha)
                pull = (terms[j, spot, :] - behind * share).reshape(2, 8, LANES)
                delta_y = ((corner_y + (y + 0.5)) - center_v)[None]
                sum_none = sum_none + pull
                moved = pull * delta_y
                sum_y = sum_y + moved
                sum_yy = sum_yy + moved * delta_y

            def fold(value):
                return jnp.sum(value[0] + value[1], axis=0, keepdims=True)

            first_x = sum_none * delta_x
            in_none = fold(sum_none)
            in_x = fold(first_x)
            in_xx = fold(first_x * delta_x)
            in_xy = fold(sum_y * delta_x)
            in_y = fold(sum_y)
            in_yy = fold(sum_yy)
            con_a, con_b, con_c = (entries[f, pl.ds(row, 1), :] for f in (2, 3, 4))
            made = [
                con_a * in_x + con_b * in_y,
                con_c * in_y + con_b * in_x,
                -0.5 * in_xx,
                -in_xy,
                -0.5 * in_yy,
                in_none,
            ]
            made += [jnp.sum(color_sums[c, j], axis=0, keepdims=True) for c in range(3)]
            for f in range(SPLAT):
                entry_grads[row, f : f + 1, :] += made[f]


def slot_columns(order, entry_grads, left, right):
    @pl.loop(0, order.shape[0])
    def _(r):
        column = pl.multiple_of(r * LANES, LANES)
        values = entry_grads[r]
        index = order[pl.ds(r, 1), :]
        scatter_lanes(index, right, column)
        for half in range(2):
            own = index - half * NEAR * 256
            scatter_bins(own, values[0:8], values[8:9], left.at[half], column, NEAR)


def slot_values(product, part, slot_grads):
    for h in range(NEAR):
        w = part * 5 + h // 2
        for half in range(2):
            eight, ninth = bin_values(product, half, h, NEAR)
            for f in range(SPLAT):
                at = f * 4 + (h % 2) * 2 + half
                slot_grads[w, at : at + 1, :] = eight[f : f + 1] if f < 8 else ninth
        slot_grads[w, 36:40, :] = jnp.zeros((4, LANES), F32)


def owner_columns(w, source, wanted, left, right, bins):
    for k in range(4):
        column = (w * 4 + k) * LANES
        eight = source[w, pl.ds(k, 8, stride=4), :]
        ninth = source[w, 32 + k : 33 + k, :]
        index = wanted[:, column : column + LANES]
        scatter_lanes(index, right, column)
        scatter_bins(index, eight, ninth, left, column, bins)


def owner_values(product, bins, pulls):
    for hb in range(bins // 8):
        for half in range(2):
            spot = slice(hb * 8, hb * 8 + 8)
            for f in range(8):
                first = product[half, pl.ds(hb * 128 + f, 8, stride=16), :]
                second = product[half, pl.ds(hb * 128 + 8 + f, 8, stride=16), :]
                pulls[f, half, spot, :] = first + second
            at = (bins + hb) * 16
            ninth = product[half, at : at + 8, :] + product[half, at + 8 : at + 16, :]
            pulls[8, half, spot, :] = ninth


def step_kernel(
    devices,
    center_y,
    far_params,
    far_target,
    far_req,
    far_list,
    tile_len,
    far_order,
    tile_pos,
    far_ids,
    pulls,
    laid,
    params,
    target,
    req,
    tile_list,
    tile_order,
    bg_ids,
    splats,
    wanted,
    sent,
    arrived,
    slot_grads,
    returned,
    backs,
    inner_held,
    outer_held,
    order,
    live,
    entries,
    wished_in,
    wished,
    alphas,
    split,
    sums,
    terms,
    carried,
    slopes,
    color_sums,
    entry_grads,
    before,
    after,
    left,
    right,
    product,
    owner_left,
    owner_right,
    owner_product,
    load_sem,
    local_sem,
    ask_send,
    ask_recv,
    send_sem,
    recv_sem,
    turn_send,
    turn_recv,
    inner_send,
    inner_recv,
    outer_send,
    outer_recv,
):
    g_local = params.shape[1]
    bins = g_local // 256
    slots = req.shape[1]
    cap = slots // NEAR
    tiles, list_len = tile_order.shape
    back_row = tiles * list_len // LANES
    me = lax.axis_index("dev")
    pairs = [
        (far_params, params),
        (far_req, req),
        (far_ids, bg_ids),
        (far_list, tile_list),
        (far_order, tile_order),
        (far_target, target),
    ]
    loads = [
        pltpu.make_async_copy(given, taken, load_sem.at[i]) for i, (given, taken) in enumerate(pairs)
    ]
    start(loads)
    greeted = greet(devices)

    finish(loads[:3])
    lay_out(params, laid, 0, g_local // LANES)
    for block in range(g_local // 1024):
        project(center_y, laid, splats, block)
    greeted()
    asks = []
    for w in range(NEAR):
        columns = pl.ds(w * cap, cap)
        given, taken = req.at[:, columns], wanted.at[:, columns]
        asks.append(window_copy(devices, w, 1, given, taken, ask_send, ask_recv, local_sem.at[0]))
    start(asks)
    mine = bg_ids[...] - me * g_local
    own_back(splats, mine, backs.at[0])

    def spread_inner(stage):
        return spread(
            devices,
            INNER,
            inner_partner,
            backs.at[2 * stage],
            inner_held.at[stage],
            inner_send.at[stage],
            inner_recv.at[stage],
        )

    def spread_outer(stage):
        return spread(
            devices,
            devices // INNER,
            outer_partner,
            backs.at[2 * stage + 1],
            outer_held.at[stage],
            outer_send.at[stage],
            outer_recv.at[stage],
        )

    inner = spread_inner(0)
    start(inner)
    finish(loads[3:6])
    tiles_setup(
        tile_list, tile_order, tile_len, target, order, live, wished_in, wished, before, after
    )
    entries[...] = jnp.zeros_like(entries)

    supplies = {
        w: window_copy(
            devices, w, -1, sent.at[w], arrived.at[w], send_sem, recv_sem, local_sem.at[1]
        )
        for w in range(NEAR)
    }

    def answer(i):
        receive(asks[2 * i : 2 * i + 2])
        owner_gather(splats, wanted, i, sent)
        start([supplies[2 * i], supplies[2 * i + 1]])

    answer(0)
    answer(1)
    receive(inner)
    backs[1] = sum_of(backs[0], inner_held.at[0])
    outer = spread_outer(0)
    start(outer)
    for i in (4, 3, 2):
        answer(i)
    for w in (0, 1, 2, 3, 5, 4, 7, 6, 9, 8):
        receive([supplies[w]])
        tiles_gather(w, arrived, order, entries)
    entries[5, 0:back_row, :] = entries[5, 0:back_row, :] * live[...]
    receive(outer)
    summed = sum_of(backs[1], outer_held.at[0])
    for f in range(SPLAT):
        entries[f, back_row : back_row + 1, :] = summed[f : f + 1, :]

    tiles_render(
        tiles,
        tile_pos,
        entries,
        wished,
        alphas,
        split,
        sums,
        terms,
        carried,
        slopes,
        color_sums,
        entry_grads,
        before,
        after,
    )

    backs[2] = entry_grads[back_row]
    started = asks + list(supplies.values()) + inner + outer
    inner = spread_inner(1)
    start(inner)
    slot_columns(order, entry_grads, left, right)
    turns = {
        w: window_copy(
            devices, w, 1, slot_grads.at[w], returned.at[w], turn_send, turn_recv, local_sem.at[2]
        )
        for w in range(1, NEAR)
    }
    for half in reversed(range(2)):
        scatter_product(left.at[half], right, product)
        slot_values(product, half, slot_grads)
        start([turns[w] for w in reversed(range(max(1, half * 5), half * 5 + 5))])
        if half == 1:
            receive(inner)
            backs[3] = sum_of(backs[2], inner_held.at[1])
            outer = spread_outer(1)
            start(outer)
    owner_product[...] = jnp.zeros_like(owner_product)
    owner_columns(0, slot_grads, wanted, owner_left, owner_right, bins)
    add_product(owner_left, owner_right, 0, cap, owner_product)
    for w in (5, 1, 2, 3, 4, 7, 6, 9, 8):
        receive([turns[w]])
        owner_columns(w, returned, wanted, owner_left, owner_right, bins)
        add_product(owner_left, owner_right, w * cap, cap, owner_product)
        if w == 4:
            receive(outer)
            summed = sum_of(backs[3], outer_held.at[1])
            scatter_lanes(mine, owner_right, slots)
            scatter_bins(mine, summed[0:8], summed[8:9], owner_left, slots, bins)
            add_product(owner_left, owner_right, slots, LANES, owner_product)
    owner_values(owner_product, bins, pulls)
    sent_off(started + inner + outer + list(turns.values()))


def step(devices, center_y, *args):
    params, target, req_rows, tile_list, tile_len, tile_order, tile_pos, ids = args
    count, g_local = params.shape
    slots = req_rows.shape[1]
    tiles, list_len = tile_order.shape
    rows = tiles * list_len // LANES
    lasts = list_len // LANES + 1
    bins = g_local // 256
    depth = slots + LANES
    outers = devices // INNER
    far = pl.BlockSpec(memory_space=pltpu.HBM)
    near = pl.BlockSpec(memory_space=pltpu.VMEM)
    smem = pl.BlockSpec(memory_space=pltpu.SMEM)
    dma = pltpu.SemaphoreType.DMA
    shape = jax.ShapeDtypeStruct
    vmem = pltpu.VMEM
    return pl.pallas_call(
        functools.partial(step_kernel, devices, center_y),
        out_shape=shape((SPLAT, 2, bins, LANES), F32),
        in_specs=[far] * 4 + [smem, far, smem, far],
        out_specs=near,
        scratch_shapes=[
            vmem((8, g_local // 16, LANES), F32),
            vmem(params.shape, F32),
            vmem(target.shape, F32),
            vmem(req_rows.shape, jnp.int32),
            vmem(tile_list.shape, jnp.int32),
            vmem(tile_order.shape, jnp.int32),
            vmem(ids.shape, jnp.int32),
            vmem((SPLAT, 2, g_local // 256, LANES), F32),
            vmem(req_rows.shape, jnp.int32),
            vmem((NEAR, 40, LANES), F32),
            vmem((NEAR, 40, LANES), F32),
            vmem((NEAR, 40, LANES), F32),
            vmem((NEAR, 40, LANES), F32),
            vmem((4, 16, LANES), F32),
            vmem((2, INNER, 16, LANES), F32),
            vmem((2, outers, 16, LANES), F32),
            vmem((rows, LANES), jnp.int32),
            vmem((rows, LANES), F32),
            vmem((SPLAT, rows + 8, LANES), F32),
            vmem((LANES, 256), F32),
            vmem((tiles * 3, 256, LANES), F32),
            vmem((lasts, 256, LANES), F32),
            vmem((lasts, 256, 256), BF16),
            vmem((lasts, 256, 256), F32),
            vmem((lasts, 256, LANES), F32),
            vmem((256, LANES), F32),
            vmem((3, 256, LANES), F32),
            vmem((3, lasts, 8, LANES), F32),
            vmem((rows + 1, 16, LANES), F32),
            vmem((256, 256), BF16),
            vmem((256, 256), BF16),
            vmem((2, scatter_rows(NEAR), rows * LANES), BF16),
            vmem((256, rows * LANES), BF16),
            vmem((2, scatter_rows(NEAR), LANES), F32),
            vmem((scatter_rows(bins), depth), BF16),
            vmem((256, depth), BF16),
            vmem((2, scatter_rows(bins), LANES), F32),
            dma((6,)),
            dma((3,)),
            dma((NEAR,)),
            dma((NEAR,)),
            dma((NEAR,)),
            dma((NEAR,)),
            dma((NEAR,)),
            dma((NEAR,)),
            dma((2, INNER)),
            dma((2, INNER)),
            dma((2, outers)),
            dma((2, outers)),
        ],
        compiler_params=pltpu.CompilerParams(
            collective_id=0, has_side_effects=True, vmem_limit_bytes=60 * 2**20
        ),
        name="step",
    )(*args)


def update_kernel(
    center_y,
    far_params,
    far_m,
    far_v,
    far_pulls,
    new_params,
    new_m,
    new_v,
    params,
    adam_m,
    adam_v,
    pulls,
    laid,
    grads,
    held_params,
    held_m,
    held_v,
    load_sem,
    sems,
):
    count, g_local = params.shape
    loads = [pltpu.make_async_copy(far_pulls, pulls, load_sem.at[0])]
    for hb in range(g_local // 2048):
        columns = pl.ds(hb * 2048, 2048)
        for given, taken in ((far_params, params), (far_m, adam_m), (far_v, adam_v)):
            given, taken = given.at[:, columns], taken.at[:, columns]
            loads.append(pltpu.make_async_copy(given, taken, load_sem.at[len(loads)]))
    start(loads)
    copies = []
    finish(loads[:1])
    for hb in range(g_local // 2048):
        finish(loads[1 + 3 * hb : 2 + 3 * hb])
        lay_out(params, laid, hb * 16, hb * 16 + 16)
        for half in range(2):
            block = hb * 2 + half
            rows = [feature(laid, f, block) for f in range(10)]
            made, pull_back = jax.vjp(lambda given: geometry(given, center_y), rows)
            got = [pulls[f, half, hb * 8 : hb * 8 + 8, :] for f in range(SPLAT)]

            def put(f, value):
                first = (hb * 16 + half) * 8 + f % 8
                grads[f // 8, pl.ds(first, 8, stride=16), :] = value

            given = got[:5]
            for k in range(16):
                at = 11 + 3 * k
                total = got[6] * feature(laid, at, block)
                total = total + got[7] * feature(laid, at + 1, block)
                total = total + got[8] * feature(laid, at + 2, block)
                given.append(total)
                for c in range(3):
                    put(at + c, made[5 + k] * got[6 + c])
            for f, row in enumerate(pull_back(given)[0]):
                put(f, row)
            put(10, got[5] * (1.0 - jax.nn.sigmoid(feature(laid, 10, block))))

        finish(loads[2 + 3 * hb : 4 + 3 * hb])

        @pl.loop(0, 16)
        def _(chunk):
            c = hb * 16 + chunk
            columns = pl.ds(pl.multiple_of(c * LANES, LANES), LANES)
            first = pl.multiple_of(c * 8, 8)
            for group in range(-(-count // 8)):
                size = min(8, count - group * 8)
                spot = slice(group * 8, group * 8 + size)
                slope = grads[group, pl.ds(first, size), :]
                moment = 0.9 * adam_m[spot, columns] + 0.1 * slope
                power = 0.999 * adam_v[spot, columns] + 0.001 * slope * slope
                change = moment / BIAS_ONE / (jnp.sqrt(power / BIAS_TWO) + 1e-08)
                held_params[spot, columns] = params[spot, columns] - 0.05 * change
                held_m[spot, columns] = moment
                held_v[spot, columns] = power

        columns = pl.ds(hb * 2048, 2048)
        for i, (held, out) in enumerate(
            ((held_params, new_params), (held_m, new_m), (held_v, new_v))
        ):
            copies.append(
                pltpu.make_async_copy(held.at[:, columns], out.at[:, columns], sems.at[hb * 3 + i])
            )
        start(copies[-3:])
    finish(copies)


def update(params, adam_m, adam_v, pulls, center_y):
    count, g_local = params.shape
    far = pl.BlockSpec(memory_space=pltpu.HBM)
    shape = jax.ShapeDtypeStruct(params.shape, F32)
    return pl.pallas_call(
        functools.partial(update_kernel, center_y),
        out_shape=(shape, shape, shape),
        in_specs=[far] * 4,
        out_specs=(far, far, far),
        scratch_shapes=[
            pltpu.VMEM((count, g_local), F32),
            pltpu.VMEM((count, g_local), F32),
            pltpu.VMEM((count, g_local), F32),
            pltpu.VMEM(pulls.shape, F32),
            pltpu.VMEM((8, g_local // 16, LANES), F32),
            pltpu.VMEM((8, g_local // 16, LANES), F32),
            pltpu.VMEM((count, g_local), F32),
            pltpu.VMEM((count, g_local), F32),
            pltpu.VMEM((count, g_local), F32),
            pltpu.SemaphoreType.DMA((1 + 3 * (g_local // 2048),)),
            pltpu.SemaphoreType.DMA((3 * (g_local // 2048),)),
        ],
        compiler_params=pltpu.CompilerParams(vmem_limit_bytes=60 * 2**20),
        name="update",
    )(params, adam_m, adam_v, pulls)


def per_device(
    devices,
    params,
    adam_m,
    adam_v,
    target,
    req_rows,
    tile_list,
    tile_len,
    tile_order,
    tile_pos,
    bg_ids,
):
    center_y = 8.0 * (tile_order.shape[0] * devices // TILES_X)
    pulls = step(
        devices,
        center_y,
        params,
        target,
        req_rows,
        tile_list,
        tile_len,
        tile_order,
        tile_pos,
        bg_ids.reshape(1, LANES),
    )
    return update(params, adam_m, adam_v, pulls, center_y)


def solution(mesh):
    return jax.shard_map(
        functools.partial(per_device, mesh.shape["dev"]),
        mesh=mesh,
        in_specs=(
            P(None, "dev"),
            P(None, "dev"),
            P(None, "dev"),
            P(None, "dev"),
            P("dev", None),
            P("dev", None),
            P("dev"),
            P("dev", None),
            P("dev"),
            P(),
        ),
        out_specs=(P(None, "dev"), P(None, "dev"), P(None, "dev")),
        check_vma=False,
    )
```

```python
import functools

import jax
import jax.numpy as jnp
from jax import lax
from jax.experimental import pallas as pl
from jax.experimental.pallas import tpu as pltpu
from jax.sharding import PartitionSpec as P

TILES_X = 32
NEAR = 10
FOCAL = 512.0
BIAS_ONE = 1.0 - 0.9**10
BIAS_TWO = 1.0 - 0.999**10
MESH = pl.DeviceIdType.MESH
F32 = jnp.float32
BF16 = jnp.bfloat16
LANES = 128
INNER = 16
SPLAT = 9


def harmonics(dir_x, dir_y, dir_z):
    sq_x = dir_x * dir_x
    sq_y = dir_y * dir_y
    sq_z = dir_z * dir_z
    return [
        0.28209479177387814 + 0.0 * dir_x,
        -0.4886025119029199 * dir_y,
        0.4886025119029199 * dir_z,
        -0.4886025119029199 * dir_x,
        1.0925484305920792 * dir_x * dir_y,
        -1.0925484305920792 * dir_y * dir_z,
        0.31539156525252005 * (2.0 * sq_z - sq_x - sq_y),
        -1.0925484305920792 * dir_x * dir_z,
        0.5462742152960396 * (sq_x - sq_y),
        -0.5900435899266435 * dir_y * (3.0 * sq_x - sq_y),
        2.890611442640554 * dir_x * dir_y * dir_z,
        -0.4570457994644658 * dir_y * (4.0 * sq_z - sq_x - sq_y),
        0.3731763325901154 * dir_z * (2.0 * sq_z - 3.0 * sq_x - 3.0 * sq_y),
        -0.4570457994644658 * dir_x * (4.0 * sq_z - sq_x - sq_y),
        1.445305721320277 * dir_z * (sq_x - sq_y),
        -0.5900435899266435 * dir_x * (sq_x - 3.0 * sq_y),
    ]


def geometry(rows, center_y):
    pos_x, pos_y, depth = (rows[0], rows[1], rows[2])
    stretches = (jnp.exp(rows[3]), jnp.exp(rows[4]), jnp.exp(rows[5]))
    quat_norm = jnp.sqrt(
        rows[6] * rows[6] + rows[7] * rows[7] + rows[8] * rows[8] + rows[9] * rows[9]
    )
    inv_norm = 1.0 / quat_norm
    quat_w = rows[6] * inv_norm
    quat_x = rows[7] * inv_norm
    quat_y = rows[8] * inv_norm
    quat_z = rows[9] * inv_norm
    rotation = (
        (
            1.0 - 2.0 * (quat_y * quat_y + quat_z * quat_z),
            2.0 * (quat_x * quat_y - quat_w * quat_z),
            2.0 * (quat_x * quat_z + quat_w * quat_y),
        ),
        (
            2.0 * (quat_x * quat_y + quat_w * quat_z),
            1.0 - 2.0 * (quat_x * quat_x + quat_z * quat_z),
            2.0 * (quat_y * quat_z - quat_w * quat_x),
        ),
        (
            2.0 * (quat_x * quat_z - quat_w * quat_y),
            2.0 * (quat_y * quat_z + quat_w * quat_x),
            1.0 - 2.0 * (quat_x * quat_x + quat_y * quat_y),
        ),
    )
    inv_depth = 1.0 / depth
    focal_z = FOCAL * inv_depth
    slope_x = pos_x * inv_depth
    slope_y = pos_y * inv_depth
    cov_a = 0.3
    cov_b = 0.0
    cov_c = 0.3
    for column in range(3):
        axis_x = rotation[0][column] * stretches[column]
        axis_y = rotation[1][column] * stretches[column]
        axis_z = rotation[2][column] * stretches[column]
        image_u = focal_z * (axis_x - slope_x * axis_z)
        image_v = focal_z * (axis_y - slope_y * axis_z)
        cov_a = cov_a + image_u * image_u
        cov_b = cov_b + image_u * image_v
        cov_c = cov_c + image_v * image_v
    inv_determ = 1.0 / (cov_a * cov_c - cov_b * cov_b)
    center_u = FOCAL * slope_x + 8.0 * TILES_X
    center_v = FOCAL * slope_y + center_y
    inv_distance = 1.0 / jnp.sqrt(pos_x * pos_x + pos_y * pos_y + depth * depth)
    basis = harmonics(pos_x * inv_distance, pos_y * inv_distance, depth * inv_distance)
    conic = [cov_c * inv_determ, -cov_b * inv_determ, cov_a * inv_determ]
    return [center_u, center_v] + conic + basis


def lane_gather(source, index):
    numbers = lax.GatherDimensionNumbers(
        offset_dims=(),
        collapsed_slice_dims=(1,),
        start_index_map=(1,),
        operand_batching_dims=(0,),
        start_indices_batching_dims=(0,),
    )
    return lax.gather(
        source,
        index[..., None],
        numbers,
        (1, 1),
        mode=lax.GatherScatterMode.PROMISE_IN_BOUNDS,
    )


def wide(row, rows=8):
    return jnp.broadcast_to(row, (rows, row.shape[-1]))


def pieces_of(value):
    first = value.astype(BF16)
    return first, (value - first.astype(F32)).astype(BF16)


def offsets_of(devices):
    lines = [0, 1, -1, 4, -4]
    return [(lines[w % 5] + w // 5 * (devices // 2)) % devices for w in range(NEAR)]


def window_copy(devices, w, direction, given, taken, send_sem, recv_sem, local_sem):
    offset = offsets_of(devices)[w]
    if offset == 0:
        return pltpu.make_async_copy(given, taken, local_sem)
    ahead = (offset * direction) % devices
    return pltpu.make_async_remote_copy(
        src_ref=given,
        dst_ref=taken,
        send_sem=send_sem.at[w],
        recv_sem=recv_sem.at[w],
        device_id=(lax.rem(lax.axis_index("dev") + ahead, devices),),
        device_id_type=MESH,
    )


def inner_partner(devices, me, k):
    return me // INNER * INNER + lax.rem(lax.rem(me, INNER) + k, INNER)


def outer_partner(devices, me, k):
    return lax.rem(me + INNER * k, devices)


def spread(devices, count, partner, given, taken, send_sem, recv_sem):
    return [
        pltpu.make_async_remote_copy(
            src_ref=given,
            dst_ref=taken.at[k],
            send_sem=send_sem.at[k],
            recv_sem=recv_sem.at[k],
            device_id=(partner(devices, lax.axis_index("dev"), k),),
            device_id_type=MESH,
        )
        for k in range(1, count)
    ]


def greet(devices):
    me = lax.axis_index("dev")
    partners = [lax.rem(me + offset, devices) for offset in offsets_of(devices) if offset]
    partners += [inner_partner(devices, me, k) for k in range(1, INNER)]
    partners += [outer_partner(devices, me, k) for k in range(1, devices // INNER)]
    barrier = pltpu.get_barrier_semaphore()
    for partner in partners:
        pl.semaphore_signal(barrier, inc=1, device_id=(partner,), device_id_type=MESH)
    return lambda: pl.semaphore_wait(barrier, len(partners))


def start(copies):
    for copy in copies:
        copy.start()


def finish(copies):
    for copy in copies:
        copy.wait()


def receive(copies):
    for copy in copies:
        if copy.is_remote:
            copy.wait_recv()
        else:
            copy.wait()


def sent_off(copies):
    for copy in copies:
        if copy.is_remote:
            copy.wait_send()


def sum_of(first, taken):
    total = first
    for k in range(1, taken.shape[0]):
        total = total + taken[k]
    return total


def feature(laid, f, block):
    first = (block // 2 * 16 + block % 2) * 8 + f % 8
    return laid[f // 8, pl.ds(first, 8, stride=16), :]


def lay_out(params, laid, first_chunk, last_chunk):
    count = params.shape[0]

    @pl.loop(first_chunk, last_chunk)
    def _(c):
        columns = pl.ds(pl.multiple_of(c * LANES, LANES), LANES)
        first = pl.multiple_of(c * 8, 8)
        for group in range(count // 8):
            laid[group, pl.ds(first, 8), :] = params[group * 8 : group * 8 + 8, columns]
        over = count % 8
        laid[count // 8, pl.ds(first, over), :] = params[count - over :, columns]


def project(center_y, laid, splats, block):
    rows = [feature(laid, f, block) for f in range(11)]
    made = geometry(rows, center_y)
    opacity = jax.nn.sigmoid(rows[10])
    colors = []
    for c in range(3):
        total = made[5] * feature(laid, 11 + c, block)
        for k in range(1, 16):
            total = total + made[5 + k] * feature(laid, 11 + 3 * k + c, block)
        colors.append(total + 0.5)
    for f, row in enumerate(made[:5] + [opacity] + colors):
        splats[f, block % 2, block // 2 * 8 : block // 2 * 8 + 8, :] = row


def own_back(splats, mine, back):
    local = wide(mine)
    high = jnp.right_shift(local, 7)
    low = jnp.bitwise_and(local, LANES - 1)
    eight = lax.broadcasted_iota(jnp.int32, (8, LANES), 0)
    back[...] = jnp.zeros_like(back)
    for f in range(SPLAT):
        total = jnp.zeros((8, LANES), F32)
        for block in range(2 * splats.shape[2] // 8):
            hb, half = block // 2, block % 2
            found = lane_gather(splats[f, half, hb * 8 : hb * 8 + 8, :], low)
            total = jnp.where(high == hb * 16 + 2 * eight + half, found, total)
        back[f : f + 1, :] = jnp.sum(total, axis=0, keepdims=True)


def owner_gather(splats, wanted, i, sent):
    first = i * 8 * LANES
    rows = jnp.concatenate(
        [wanted[:, first + r * LANES : first + (r + 1) * LANES] for r in range(8)], axis=0
    )
    high = jnp.right_shift(rows, 7)
    low = jnp.bitwise_and(rows, LANES - 1)

    def pick(step, totals):
        totals = list(totals)
        for k in range(4):
            for half in range(2):
                c = step * 4 + k
                here = high == 2 * c + half
                for f in range(SPLAT):
                    source = wide(splats[f, half, pl.ds(c, 1), :])
                    totals[f] = jnp.where(here, lane_gather(source, low), totals[f])
        return tuple(totals)

    totals = tuple(jnp.zeros((8, LANES), F32) for _ in range(SPLAT))
    for step in range(splats.shape[2] // 4):
        totals = pick(step, totals)
    for half in range(2):
        for f in range(SPLAT):
            sent[i * 2 + half, f * 4 : f * 4 + 4, :] = totals[f][half * 4 : half * 4 + 4, :]
        sent[i * 2 + half, 36:40, :] = jnp.zeros((4, LANES), F32)


def scatter_rows(bins):
    return 16 * (bins + -(-bins // 8))


def scatter_lanes(index, right, column):
    low = wide(jnp.bitwise_and(index, 255), 256)
    place = lax.broadcasted_iota(jnp.int32, (256, LANES), 0)
    right[:, pl.ds(column, LANES)] = jnp.where(place == low, 1.0, 0.0).astype(BF16)


def scatter_bins(index, eight, ninth, left, column, bins):
    high = wide(jnp.right_shift(index, 8))

    def put(at, here, value):
        first = value.astype(BF16).astype(F32)
        both = [jnp.where(here, first, 0.0), jnp.where(here, value - first, 0.0)]
        left[at : at + 16, pl.ds(column, LANES)] = jnp.concatenate(both, axis=0).astype(BF16)

    for h in range(bins):
        put(h * 16, high == h, eight)
    ninth = wide(ninth)
    for i in range(-(-bins // 8)):
        own = lax.broadcasted_iota(jnp.int32, (8, LANES), 0) + 8 * i
        put((bins + i) * 16, high == own, ninth)


def bin_values(product, half, h, bins):
    eight = product[half, h * 16 : h * 16 + 8, :] + product[half, h * 16 + 8 : h * 16 + 16, :]
    at = (bins + h // 8) * 16 + h % 8
    return eight, product[half, at : at + 1, :] + product[half, at + 8 : at + 9, :]


def add_product(left, right, first, depth, product):
    columns = pl.ds(first, depth)
    made = lax.dot_general(
        left[:, columns],
        right[:, columns],
        (((1,), (1,)), ((), ())),
        preferred_element_type=F32,
    )
    product[0] += made[:, :LANES]
    product[1] += made[:, LANES:]


def scatter_product(left, right, product):
    product[...] = jnp.zeros_like(product)
    add_product(left, right, 0, left.shape[1], product)


def tiles_setup(
    tile_list, tile_order, tile_len, target, order, live, wished_in, wished, before, after
):
    tiles, list_len = tile_order.shape
    groups = list_len // LANES

    eight = lax.broadcasted_iota(jnp.int32, (8, LANES), 0)
    lengths = jnp.zeros((8, LANES), jnp.int32)
    for t in range(tiles):
        lengths = jnp.where(lax.rem(eight, tiles) == t, tile_len[t], lengths)
    for pair in range(groups // 2):
        ranks = jnp.concatenate(
            [
                tile_order[:, (2 * pair) * LANES : (2 * pair + 1) * LANES],
                tile_order[:, (2 * pair + 1) * LANES : (2 * pair + 2) * LANES],
            ],
            axis=0,
        )
        high = jnp.right_shift(ranks, 7)
        low = jnp.bitwise_and(ranks, LANES - 1)
        named = jnp.zeros((8, LANES), jnp.int32)
        for c in range(groups):
            part = [
                tile_list[:, t * list_len + c * LANES : t * list_len + (c + 1) * LANES]
                for t in range(tiles)
            ]
            source = jnp.concatenate(part + part, axis=0)
            named = jnp.where(high == c, lane_gather(source, low), named)
        order[pair * 8 : pair * 8 + 8, :] = named
        live[pair * 8 : pair * 8 + 8, :] = jnp.where(ranks < lengths, 1.0, 0.0)

    wished_in[...] = jnp.zeros_like(wished_in)
    for t in range(tiles):
        wished_in[3 * t : 3 * t + 3, :] = target[:, t * 256 : (t + 1) * 256]
    columns = jnp.transpose(wished_in[...])
    for t in range(tiles):
        for c in range(3):
            one = columns[:, 3 * t + c : 3 * t + c + 1]
            wished[t * 3 + c] = jnp.broadcast_to(one, (256, LANES))

    row_at = jnp.bitwise_and(lax.broadcasted_iota(jnp.int32, (256, 256), 0), LANES - 1)
    col_at = lax.broadcasted_iota(jnp.int32, (256, 256), 1)
    before[...] = jnp.where((row_at < col_at) | (col_at >= LANES), 1.0, 0.0).astype(BF16)
    after[...] = jnp.where((row_at > col_at) | (col_at >= LANES), 1.0, 0.0).astype(BF16)


def tiles_gather(w, arrived, order, entries):
    for i in range(order.shape[0] // 8):
        spots = pl.ds(i * 8, 8)
        slots = order[spots, :]
        high = jnp.right_shift(slots, 7)
        low = jnp.bitwise_and(slots, LANES - 1)
        totals = [entries[f, spots, :] for f in range(SPLAT)]
        for k in range(4):
            here = high == w * 4 + k
            for f in range(SPLAT):
                source = wide(arrived[w, f * 4 + k : f * 4 + k + 1, :])
                totals[f] = jnp.where(here, lane_gather(source, low), totals[f])
        for f in range(SPLAT):
            entries[f, spots, :] = totals[f]


def tiles_render(
    tiles,
    tile_pos,
    entries,
    wished,
    alphas,
    split,
    sums,
    terms,
    carried,
    slopes,
    color_sums,
    entry_grads,
    before,
    after,
):
    lasts = alphas.shape[0]
    groups = lasts - 1
    back_row = tiles * groups
    entry_grads[...] = jnp.zeros_like(entry_grads)

    def row_of(t, j):
        listed = j // 2 * 8 + lax.rem(j, 2) * 4 + t
        return jnp.where(j == groups, back_row, listed)

    def entry(f, row):
        return wide(entries[f, pl.ds(row, 1), :])

    across = (
        lax.broadcasted_iota(jnp.int32, (2, 8, LANES), 0) * 8
        + lax.broadcasted_iota(jnp.int32, (2, 8, LANES), 1)
    ).astype(F32) + 0.5

    @pl.loop(0, tiles)
    def _(t):
        place = tile_pos[t]
        corner_x = (lax.rem(place, TILES_X) * 16).astype(F32)
        corner_y = (place // TILES_X * 16).astype(F32)

        @pl.loop(0, lasts)
        def _(j):
            row = row_of(t, j)
            delta_x = (across + corner_x) - entry(0, row)[None]
            center_v = entry(1, row)
            flat = -0.5 * entry(2, row)[None] * delta_x * delta_x
            mixed = -entry(3, row)[None] * delta_x
            half_c = -0.5 * entry(4, row)
            opacity = entry(5, row)[None]
            for y in range(16):
                delta_y = (corner_y + (y + 0.5)) - center_v
                slope = half_c * delta_y
                power = (mixed + slope[None]) * delta_y[None] + flat
                alpha = opacity * jnp.exp(power)
                keep = jnp.log(1.0 - alpha)
                spot = slice(y * 16, y * 16 + 16)
                alphas[j, spot, :] = alpha.reshape(16, LANES)
                first, second = pieces_of(keep.reshape(16, LANES))
                split[j, spot, :LANES] = first
                split[j, spot, LANES:] = second

        for j in range(lasts):
            sums[j] = jnp.dot(split[j], before[...], preferred_element_type=F32)

        @pl.loop(0, 4)
        def _(y):
            spot = pl.ds(pl.multiple_of(y * 64, 64), 64)
            gone = jnp.zeros((64, LANES), F32)
            seen = [jnp.zeros((8, 8, LANES), F32) for _ in range(3)]
            for j in range(lasts):
                row = row_of(t, j)
                transmit = jnp.exp(gone + sums[j, spot, :LANES])
                gone = gone + sums[j, spot, LANES:]
                weight = alphas[j, spot, :] * transmit
                terms[j, spot, :] = weight
                for c in range(3):
                    seen[c] = seen[c] + weight.reshape(8, 8, LANES) * entry(6 + c, row)[None]
            for c in range(3):
                slopes[c, spot, :] = seen[c].reshape(64, LANES)

        for c in range(3):
            color = jnp.sum(slopes[c], axis=1, keepdims=True)
            slopes[c] = 16.0 * (color - wished[t * 3 + c])

        @pl.loop(0, lasts)
        def _(j):
            row = row_of(t, j)
            colors = [entry(6 + c, row)[None] for c in range(3)]
            painted = [jnp.zeros((2, 8, LANES), F32) for _ in range(3)]
            for y in range(16):
                spot = slice(y * 16, y * 16 + 16)
                weight = terms[j, spot, :].reshape(2, 8, LANES)
                slope = [slopes[c, spot, :].reshape(2, 8, LANES) for c in range(3)]
                pull = slope[0] * colors[0] + slope[1] * colors[1] + slope[2] * colors[2]
                term = (pull * weight).reshape(16, LANES)
                terms[j, spot, :] = term
                first, second = pieces_of(term)
                split[j, spot, :LANES] = first
                split[j, spot, LANES:] = second
                for c in range(3):
                    painted[c] = painted[c] + slope[c] * weight
            for c in range(3):
                color_sums[c, j] = painted[c][0] + painted[c][1]

        for j in range(lasts):
            sums[j] = jnp.dot(split[j], after[...], preferred_element_type=F32)

        carried[...] = jnp.zeros_like(carried)

        @pl.loop(0, lasts)
        def _(back_j):
            j = groups - back_j
            row = row_of(t, j)
            delta_x = (across + corner_x) - entry(0, row)[None]
            center_v = entry(1, row)
            zero = jnp.zeros((2, 8, LANES), F32)
            sum_none, sum_y, sum_yy = zero, zero, zero
            for y in range(16):
                spot = slice(y * 16, y * 16 + 16)
                behind = carried[spot, :] + sums[j, spot, :LANES]
                carried[spot, :] += sums[j, spot, LANES:]
                alpha = alphas[j, spot, :]
                share = alpha / (1.0 - alpha)
                pull = (terms[j, spot, :] - behind * share).reshape(2, 8, LANES)
                delta_y = ((corner_y + (y + 0.5)) - center_v)[None]
                sum_none = sum_none + pull
                moved = pull * delta_y
                sum_y = sum_y + moved
                sum_yy = sum_yy + moved * delta_y

            def fold(value):
                return jnp.sum(value[0] + value[1], axis=0, keepdims=True)

            first_x = sum_none * delta_x
            in_none = fold(sum_none)
            in_x = fold(first_x)
            in_xx = fold(first_x * delta_x)
            in_xy = fold(sum_y * delta_x)
            in_y = fold(sum_y)
            in_yy = fold(sum_yy)
            con_a, con_b, con_c = (entries[f, pl.ds(row, 1), :] for f in (2, 3, 4))
            made = [
                con_a * in_x + con_b * in_y,
                con_c * in_y + con_b * in_x,
                -0.5 * in_xx,
                -in_xy,
                -0.5 * in_yy,
                in_none,
            ]
            made += [jnp.sum(color_sums[c, j], axis=0, keepdims=True) for c in range(3)]
            for f in range(SPLAT):
                entry_grads[row, f : f + 1, :] += made[f]


def slot_columns(order, entry_grads, left, right):
    @pl.loop(0, order.shape[0])
    def _(r):
        column = pl.multiple_of(r * LANES, LANES)
        values = entry_grads[r]
        index = order[pl.ds(r, 1), :]
        scatter_lanes(index, right, column)
        for half in range(2):
            own = index - half * NEAR * 256
            scatter_bins(own, values[0:8], values[8:9], left.at[half], column, NEAR)


def slot_values(product, part, slot_grads):
    for h in range(NEAR):
        w = part * 5 + h // 2
        for half in range(2):
            eight, ninth = bin_values(product, half, h, NEAR)
            for f in range(SPLAT):
                at = f * 4 + (h % 2) * 2 + half
                slot_grads[w, at : at + 1, :] = eight[f : f + 1] if f < 8 else ninth
        slot_grads[w, 36:40, :] = jnp.zeros((4, LANES), F32)


def owner_columns(w, source, wanted, left, right, bins):
    for k in range(4):
        column = (w * 4 + k) * LANES
        eight = source[w, pl.ds(k, 8, stride=4), :]
        ninth = source[w, 32 + k : 33 + k, :]
        index = wanted[:, column : column + LANES]
        scatter_lanes(index, right, column)
        scatter_bins(index, eight, ninth, left, column, bins)


def owner_values(product, bins, pulls):
    for hb in range(bins // 8):
        for half in range(2):
            spot = slice(hb * 8, hb * 8 + 8)
            for f in range(8):
                first = product[half, pl.ds(hb * 128 + f, 8, stride=16), :]
                second = product[half, pl.ds(hb * 128 + 8 + f, 8, stride=16), :]
                pulls[f, half, spot, :] = first + second
            at = (bins + hb) * 16
            ninth = product[half, at : at + 8, :] + product[half, at + 8 : at + 16, :]
            pulls[8, half, spot, :] = ninth


def step_kernel(
    devices,
    center_y,
    far_params,
    far_target,
    far_req,
    far_list,
    tile_len,
    far_order,
    tile_pos,
    far_ids,
    pulls,
    laid,
    params,
    target,
    req,
    tile_list,
    tile_order,
    bg_ids,
    splats,
    wanted,
    sent,
    arrived,
    slot_grads,
    returned,
    backs,
    inner_held,
    outer_held,
    order,
    live,
    entries,
    wished_in,
    wished,
    alphas,
    split,
    sums,
    terms,
    carried,
    slopes,
    color_sums,
    entry_grads,
    before,
    after,
    left,
    right,
    product,
    owner_left,
    owner_right,
    owner_product,
    load_sem,
    local_sem,
    ask_send,
    ask_recv,
    send_sem,
    recv_sem,
    turn_send,
    turn_recv,
    inner_send,
    inner_recv,
    outer_send,
    outer_recv,
):
    g_local = params.shape[1]
    bins = g_local // 256
    slots = req.shape[1]
    cap = slots // NEAR
    tiles, list_len = tile_order.shape
    back_row = tiles * list_len // LANES
    me = lax.axis_index("dev")
    pairs = [
        (far_params, params),
        (far_req, req),
        (far_ids, bg_ids),
        (far_list, tile_list),
        (far_order, tile_order),
        (far_target, target),
    ]
    loads = [
        pltpu.make_async_copy(given, taken, load_sem.at[i]) for i, (given, taken) in enumerate(pairs)
    ]
    start(loads)
    greeted = greet(devices)

    finish(loads[:3])
    lay_out(params, laid, 0, g_local // LANES)
    for block in range(g_local // 1024):
        project(center_y, laid, splats, block)
    greeted()
    asks = []
    for w in range(NEAR):
        columns = pl.ds(w * cap, cap)
        given, taken = req.at[:, columns], wanted.at[:, columns]
        asks.append(window_copy(devices, w, 1, given, taken, ask_send, ask_recv, local_sem.at[0]))
    start(asks)
    mine = bg_ids[...] - me * g_local
    own_back(splats, mine, backs.at[0])

    def spread_inner(stage):
        return spread(
            devices,
            INNER,
            inner_partner,
            backs.at[2 * stage],
            inner_held.at[stage],
            inner_send.at[stage],
            inner_recv.at[stage],
        )

    def spread_outer(stage):
        return spread(
            devices,
            devices // INNER,
            outer_partner,
            backs.at[2 * stage + 1],
            outer_held.at[stage],
            outer_send.at[stage],
            outer_recv.at[stage],
        )

    inner = spread_inner(0)
    start(inner)
    finish(loads[3:6])
    tiles_setup(
        tile_list, tile_order, tile_len, target, order, live, wished_in, wished, before, after
    )
    entries[...] = jnp.zeros_like(entries)

    supplies = {
        w: window_copy(
            devices, w, -1, sent.at[w], arrived.at[w], send_sem, recv_sem, local_sem.at[1]
        )
        for w in range(NEAR)
    }

    def answer(i):
        receive(asks[2 * i : 2 * i + 2])
        owner_gather(splats, wanted, i, sent)
        start([supplies[2 * i], supplies[2 * i + 1]])

    answer(0)
    answer(1)
    receive(inner)
    backs[1] = sum_of(backs[0], inner_held.at[0])
    outer = spread_outer(0)
    start(outer)
    for i in (4, 3, 2):
        answer(i)
    for w in (0, 1, 2, 3, 5, 4, 7, 6, 9, 8):
        receive([supplies[w]])
        tiles_gather(w, arrived, order, entries)
    entries[5, 0:back_row, :] = entries[5, 0:back_row, :] * live[...]
    receive(outer)
    summed = sum_of(backs[1], outer_held.at[0])
    for f in range(SPLAT):
        entries[f, back_row : back_row + 1, :] = summed[f : f + 1, :]

    tiles_render(
        tiles,
        tile_pos,
        entries,
        wished,
        alphas,
        split,
        sums,
        terms,
        carried,
        slopes,
        color_sums,
        entry_grads,
        before,
        after,
    )

    backs[2] = entry_grads[back_row]
    started = asks + list(supplies.values()) + inner + outer
    inner = spread_inner(1)
    start(inner)
    slot_columns(order, entry_grads, left, right)
    turns = {
        w: window_copy(
            devices, w, 1, slot_grads.at[w], returned.at[w], turn_send, turn_recv, local_sem.at[2]
        )
        for w in range(1, NEAR)
    }
    for half in reversed(range(2)):
        scatter_product(left.at[half], right, product)
        slot_values(product, half, slot_grads)
        start([turns[w] for w in reversed(range(max(1, half * 5), half * 5 + 5))])
        if half == 1:
            receive(inner)
            backs[3] = sum_of(backs[2], inner_held.at[1])
            outer = spread_outer(1)
            start(outer)
    owner_product[...] = jnp.zeros_like(owner_product)
    owner_columns(0, slot_grads, wanted, owner_left, owner_right, bins)
    add_product(owner_left, owner_right, 0, cap, owner_product)
    for w in (5, 1, 2, 3, 4, 7, 6, 9, 8):
        receive([turns[w]])
        owner_columns(w, returned, wanted, owner_left, owner_right, bins)
        add_product(owner_left, owner_right, w * cap, cap, owner_product)
        if w == 4:
            receive(outer)
            summed = sum_of(backs[3], outer_held.at[1])
            scatter_lanes(mine, owner_right, slots)
            scatter_bins(mine, summed[0:8], summed[8:9], owner_left, slots, bins)
            add_product(owner_left, owner_right, slots, LANES, owner_product)
    owner_values(owner_product, bins, pulls)
    sent_off(started + inner + outer + list(turns.values()))


def step(devices, center_y, *args):
    params, target, req_rows, tile_list, tile_len, tile_order, tile_pos, ids = args
    count, g_local = params.shape
    slots = req_rows.shape[1]
    tiles, list_len = tile_order.shape
    rows = tiles * list_len // LANES
    lasts = list_len // LANES + 1
    bins = g_local // 256
    depth = slots + LANES
    outers = devices // INNER
    far = pl.BlockSpec(memory_space=pltpu.HBM)
    near = pl.BlockSpec(memory_space=pltpu.VMEM)
    smem = pl.BlockSpec(memory_space=pltpu.SMEM)
    dma = pltpu.SemaphoreType.DMA
    shape = jax.ShapeDtypeStruct
    vmem = pltpu.VMEM
    return pl.pallas_call(
        functools.partial(step_kernel, devices, center_y),
        out_shape=shape((SPLAT, 2, bins, LANES), F32),
        in_specs=[far] * 4 + [smem, far, smem, far],
        out_specs=near,
        scratch_shapes=[
            vmem((8, g_local // 16, LANES), F32),
            vmem(params.shape, F32),
            vmem(target.shape, F32),
            vmem(req_rows.shape, jnp.int32),
            vmem(tile_list.shape, jnp.int32),
            vmem(tile_order.shape, jnp.int32),
            vmem(ids.shape, jnp.int32),
            vmem((SPLAT, 2, g_local // 256, LANES), F32),
            vmem(req_rows.shape, jnp.int32),
            vmem((NEAR, 40, LANES), F32),
            vmem((NEAR, 40, LANES), F32),
            vmem((NEAR, 40, LANES), F32),
            vmem((NEAR, 40, LANES), F32),
            vmem((4, 16, LANES), F32),
            vmem((2, INNER, 16, LANES), F32),
            vmem((2, outers, 16, LANES), F32),
            vmem((rows, LANES), jnp.int32),
            vmem((rows, LANES), F32),
            vmem((SPLAT, rows + 8, LANES), F32),
            vmem((LANES, 256), F32),
            vmem((tiles * 3, 256, LANES), F32),
            vmem((lasts, 256, LANES), F32),
            vmem((lasts, 256, 256), BF16),
            vmem((lasts, 256, 256), F32),
            vmem((lasts, 256, LANES), F32),
            vmem((256, LANES), F32),
            vmem((3, 256, LANES), F32),
            vmem((3, lasts, 8, LANES), F32),
            vmem((rows + 1, 16, LANES), F32),
            vmem((256, 256), BF16),
            vmem((256, 256), BF16),
            vmem((2, scatter_rows(NEAR), rows * LANES), BF16),
            vmem((256, rows * LANES), BF16),
            vmem((2, scatter_rows(NEAR), LANES), F32),
            vmem((scatter_rows(bins), depth), BF16),
            vmem((256, depth), BF16),
            vmem((2, scatter_rows(bins), LANES), F32),
            dma((6,)),
            dma((3,)),
            dma((NEAR,)),
            dma((NEAR,)),
            dma((NEAR,)),
            dma((NEAR,)),
            dma((NEAR,)),
            dma((NEAR,)),
            dma((2, INNER)),
            dma((2, INNER)),
            dma((2, outers)),
            dma((2, outers)),
        ],
        compiler_params=pltpu.CompilerParams(
            collective_id=0, has_side_effects=True, vmem_limit_bytes=60 * 2**20
        ),
        name="step",
    )(*args)


def update_kernel(
    center_y,
    far_params,
    far_m,
    far_v,
    far_pulls,
    new_params,
    new_m,
    new_v,
    params,
    adam_m,
    adam_v,
    pulls,
    laid,
    grads,
    held_params,
    held_m,
    held_v,
    load_sem,
    sems,
):
    count, g_local = params.shape
    loads = [pltpu.make_async_copy(far_pulls, pulls, load_sem.at[0])]
    for hb in range(g_local // 2048):
        columns = pl.ds(hb * 2048, 2048)
        for given, taken in ((far_params, params), (far_m, adam_m), (far_v, adam_v)):
            given, taken = given.at[:, columns], taken.at[:, columns]
            loads.append(pltpu.make_async_copy(given, taken, load_sem.at[len(loads)]))
    start(loads)
    copies = []
    finish(loads[:1])
    for hb in range(g_local // 2048):
        finish(loads[1 + 3 * hb : 2 + 3 * hb])
        lay_out(params, laid, hb * 16, hb * 16 + 16)
        for half in range(2):
            block = hb * 2 + half
            rows = [feature(laid, f, block) for f in range(10)]
            made, pull_back = jax.vjp(lambda given: geometry(given, center_y), rows)
            got = [pulls[f, half, hb * 8 : hb * 8 + 8, :] for f in range(SPLAT)]

            def put(f, value):
                first = (hb * 16 + half) * 8 + f % 8
                grads[f // 8, pl.ds(first, 8, stride=16), :] = value

            given = got[:5]
            for k in range(16):
                at = 11 + 3 * k
                total = got[6] * feature(laid, at, block)
                total = total + got[7] * feature(laid, at + 1, block)
                total = total + got[8] * feature(laid, at + 2, block)
                given.append(total)
                for c in range(3):
                    put(at + c, made[5 + k] * got[6 + c])
            for f, row in enumerate(pull_back(given)[0]):
                put(f, row)
            put(10, got[5] * (1.0 - jax.nn.sigmoid(feature(laid, 10, block))))

        finish(loads[2 + 3 * hb : 4 + 3 * hb])

        @pl.loop(0, 16)
        def _(chunk):
            c = hb * 16 + chunk
            columns = pl.ds(pl.multiple_of(c * LANES, LANES), LANES)
            first = pl.multiple_of(c * 8, 8)
            for group in range(-(-count // 8)):
                size = min(8, count - group * 8)
                spot = slice(group * 8, group * 8 + size)
                slope = grads[group, pl.ds(first, size), :]
                moment = 0.9 * adam_m[spot, columns] + 0.1 * slope
                power = 0.999 * adam_v[spot, columns] + 0.001 * slope * slope
                change = moment / BIAS_ONE / (jnp.sqrt(power / BIAS_TWO) + 1e-08)
                held_params[spot, columns] = params[spot, columns] - 0.05 * change
                held_m[spot, columns] = moment
                held_v[spot, columns] = power

        columns = pl.ds(hb * 2048, 2048)
        for i, (held, out) in enumerate(
            ((held_params, new_params), (held_m, new_m), (held_v, new_v))
        ):
            copies.append(
                pltpu.make_async_copy(held.at[:, columns], out.at[:, columns], sems.at[hb * 3 + i])
            )
        start(copies[-3:])
    finish(copies)


def update(params, adam_m, adam_v, pulls, center_y):
    count, g_local = params.shape
    far = pl.BlockSpec(memory_space=pltpu.HBM)
    shape = jax.ShapeDtypeStruct(params.shape, F32)
    return pl.pallas_call(
        functools.partial(update_kernel, center_y),
        out_shape=(shape, shape, shape),
        in_specs=[far] * 4,
        out_specs=(far, far, far),
        scratch_shapes=[
            pltpu.VMEM((count, g_local), F32),
            pltpu.VMEM((count, g_local), F32),
            pltpu.VMEM((count, g_local), F32),
            pltpu.VMEM(pulls.shape, F32),
            pltpu.VMEM((8, g_local // 16, LANES), F32),
            pltpu.VMEM((8, g_local // 16, LANES), F32),
            pltpu.VMEM((count, g_local), F32),
            pltpu.VMEM((count, g_local), F32),
            pltpu.VMEM((count, g_local), F32),
            pltpu.SemaphoreType.DMA((1 + 3 * (g_local // 2048),)),
            pltpu.SemaphoreType.DMA((3 * (g_local // 2048),)),
        ],
        compiler_params=pltpu.CompilerParams(vmem_limit_bytes=60 * 2**20),
        name="update",
    )(params, adam_m, adam_v, pulls)


def per_device(
    devices,
    params,
    adam_m,
    adam_v,
    target,
    req_rows,
    tile_list,
    tile_len,
    tile_order,
    tile_pos,
    bg_ids,
):
    center_y = 8.0 * (tile_order.shape[0] * devices // TILES_X)
    pulls = step(
        devices,
        center_y,
        params,
        target,
        req_rows,
        tile_list,
        tile_len,
        tile_order,
        tile_pos,
        bg_ids.reshape(1, LANES),
    )
    return update(params, adam_m, adam_v, pulls, center_y)


def solution(mesh):
    return jax.shard_map(
        functools.partial(per_device, mesh.shape["dev"]),
        mesh=mesh,
        in_specs=(
            P(None, "dev"),
            P(None, "dev"),
            P(None, "dev"),
            P(None, "dev"),
            P("dev", None),
            P("dev", None),
            P("dev"),
            P("dev", None),
            P("dev"),
            P(),
        ),
        out_specs=(P(None, "dev"), P(None, "dev"), P(None, "dev")),
        check_vma=False,
    )
```
